32 devices in a mesh: ctx: 4 (over y, core), section: 2 (over x), tp: 4 (over z).
Axes of the slice: x: 2, y: 2, z: 4, core: 2. Of those that a mesh axis runs over, the one named last changes fastest.
Arguments:
- text_embed: bfloat16 [512, 4096], P('ctx', ('section', 'tp')), may hold values from -6 to 6
- frame_feats: bfloat16 [512, 1024], P('ctx', ('section', 'tp')), may hold values from -6 to 6
- frame_count: int32 [4], P('ctx'), may hold values from 0 to 128
- proj_weight: bfloat16 [1024, 4096], P(None, ('section', 'tp')), may hold values from -0.1875 to 0.1875
- norm_gain: bfloat16 [4096], replicated, may hold values from 0.099609375 to 1.8984375
- q_weight: bfloat16 [4096, 2048], P('ctx', ('section', 'tp')), may hold values from -0.046875 to 0.046875
- k_weight: bfloat16 [4096, 2048], P('ctx', ('section', 'tp')), may hold values from -0.046875 to 0.046875
- v_weight: bfloat16 [4096, 2048], P('ctx', ('section', 'tp')), may hold values from -0.09375 to 0.09375
Outputs:
- attended: bfloat16 [512, 2048], P('ctx', ('section', 'tp'))
The draws below stay inside these ranges and needn't reach their ends.
All inputs are finite; a program needn't handle non-finite values.
Results may differ from the reference program's by a relative error of at most 0.012.
Values may be sent and summed in bfloat16 or wider, within the bound.
A program may use at most 64 MiB of HBM per device.

```python
import math
import jax
import jax.numpy as jnp
from jax import lax

D = 4096
ROOT_D = 64
DV = 1024
HEADS = 16
HD = 128
TOK_DEV = 128
TOKENS = 512
N_CTX = 4


def draw_text_embed(key, part):
    drawn = jnp.clip(jax.random.normal(jax.random.fold_in(key, 11), (TOKENS, D), jnp.float32), -6.0, 6.0)
    return drawn.astype(jnp.bfloat16)


def draw_q_weight(key, part):
    edge_value = 3.0 / ROOT_D
    drawn = jax.random.uniform(jax.random.fold_in(key, 21), (D, HEADS * HD), jnp.float32, -edge_value, edge_value)
    return drawn.astype(jnp.bfloat16)


def draw_k_weight(key, part):
    edge_value = 3.0 / ROOT_D
    drawn = jax.random.normal(jax.random.fold_in(key, 31), (D, HEADS * HD), jnp.float32) / ROOT_D
    drawn = jnp.clip(drawn, -edge_value, edge_value)
    return drawn.astype(jnp.bfloat16)


def plant(result, stream_key, low, high):
    shape = result.shape
    spot = [jax.random.randint(jax.random.fold_in(stream_key, axis), (), 0, shape[axis]) for axis in range(len(shape))]
    result = result.at[tuple(spot)].set(low)
    longest = shape.index(max(shape))
    spot[longest] = (spot[longest] + 1) % shape[longest]
    return result.at[tuple(spot)].set(high)


def block_scale(rng, extent, pieces, smallest, high):
    def one(position, parts):
        steps = jax.random.uniform(jax.random.fold_in(jax.random.fold_in(rng, 6), position), (parts,), jnp.float32, smallest / len(pieces), high / len(pieces))
        return jnp.repeat(jnp.exp(steps), extent[position] // parts).reshape((-1,) + (1,) * (len(extent) - position - 1))

    factor_of = one(*pieces[0])
    for cut in pieces[1:]:
        factor_of = factor_of * one(*cut)
    return factor_of


def scatter_about(stream_key, dims, width, limit, cuts=(), held_as=jnp.bfloat16):
    result = width * jax.random.normal(stream_key, dims, jnp.float32)
    if cuts:
        result = result * block_scale(stream_key, dims, cuts, -0.22, 0.18)
    return jnp.clip(result, -limit, limit).astype(held_as)


def setup_inputs(seed: int = 0) -> dict:
    key_of = jax.random.split(jax.random.key(seed), 9)
    return {
        "text_embed": draw_text_embed(jax.random.fold_in(key_of[8], 71), 0),
        "frame_feats": scatter_about(key_of[1], (TOKENS, DV), 1.0, 6.0, ((0, 4), (1, 8))),
        "frame_count": plant(jax.random.randint(key_of[2], (N_CTX,), 0, TOK_DEV + 1), jax.random.fold_in(key_of[2], 1), 0, TOK_DEV).astype(jnp.int32),
        "proj_weight": scatter_about(key_of[3], (DV, D), DV ** -0.5, 0.1875, ((1, 8),)),
        "norm_gain": jnp.clip(1.0 + 0.18 * jax.random.normal(key_of[4], (D,), jnp.float32), 0.099609375, 1.8984375).astype(jnp.bfloat16),
        "q_weight": draw_q_weight(jax.random.fold_in(key_of[8], 71), 0),
        "k_weight": draw_k_weight(jax.random.fold_in(key_of[8], 71), 0),
        "v_weight": scatter_about(key_of[7], (D, HEADS * HD), D ** -0.5, 0.09375, ((0, 4), (1, 8))),
    }


ROPE_BASE = 1000000.0
NORM_EPS = 1e-05
MASKED = -1e+30

def rotate(values, positions):
    half = values.shape[-1] // 2
    ladder = jnp.arange(half, dtype=jnp.float32) * 2.0 / values.shape[-1]
    freq = ROPE_BASE ** (-ladder)
    angle = positions.astype(jnp.float32)[:, None] * freq[None, :]
    cosine = jnp.cos(angle)[:, None, :]
    sine = jnp.sin(angle)[:, None, :]
    first = values[..., :half]
    second = values[..., half:]
    return jnp.concatenate([first * cosine - second * sine, second * cosine + first * sine], axis=-1)

def reference(text_embed, frame_feats, frame_count, proj_weight, norm_gain, q_weight, k_weight, v_weight):
    vision = jnp.dot(frame_feats, proj_weight, preferred_element_type=jnp.float32)
    places = jnp.arange(TOKENS, dtype=jnp.int32)
    blocks = places // TOK_DEV
    is_frame = places % TOK_DEV < frame_count[blocks]
    joined = jnp.where(is_frame[:, None], vision, text_embed.astype(jnp.float32)).astype(jnp.bfloat16)
    wide = joined.astype(jnp.float32)
    mean_square = lax.optimization_barrier(jnp.mean(wide * wide, axis=-1, keepdims=True))
    normed = (wide * lax.rsqrt(mean_square + NORM_EPS) * norm_gain.astype(jnp.float32)).astype(jnp.bfloat16)
    qlin = jnp.dot(normed, q_weight, preferred_element_type=jnp.float32)
    klin = jnp.dot(normed, k_weight, preferred_element_type=jnp.float32)
    vlin = jnp.dot(normed, v_weight, preferred_element_type=jnp.float32)
    queries = rotate(qlin.reshape(TOKENS, HEADS, HD), places).astype(jnp.bfloat16)
    keys = rotate(klin.reshape(TOKENS, HEADS, HD), places).astype(jnp.bfloat16)
    values = vlin.reshape(TOKENS, HEADS, HD).astype(jnp.bfloat16)
    scale = 1.0 / math.sqrt(HD)
    allowed = places[None, :] <= places[:, None]

    def one_head(items):
        query_head, key_head, value_head = items
        scores = jnp.dot(query_head, key_head.T, preferred_element_type=jnp.float32) * scale
        best = lax.optimization_barrier(jnp.max(jnp.where(allowed, scores, MASKED), axis=-1))
        weights = jnp.where(allowed, jnp.exp(scores - best[:, None]), 0.0)
        total = lax.optimization_barrier(jnp.sum(weights, axis=-1))
        product = jnp.dot(weights.astype(jnp.bfloat16), value_head, preferred_element_type=jnp.float32)
        return product / total[:, None]
    outputs = lax.map(one_head, (queries.transpose(1, 0, 2), keys.transpose(1, 0, 2), values.transpose(1, 0, 2)))
    return outputs.transpose(1, 0, 2).reshape(TOKENS, HEADS * HD).astype(jnp.bfloat16)
```

```python
import math

import jax
import jax.numpy as jnp
import numpy as np
from jax import lax
from jax.experimental import pallas as pl
from jax.experimental.pallas import tpu as pltpu
from jax.sharding import PartitionSpec as P

HD = 128


ROPE_BASE = 1000000.0
NORM_EPS = 1e-05
MASKED = -1e30


def rotate(values, positions):
    half = values.shape[-1] // 2
    ladder = jnp.arange(half, dtype=jnp.float32) * 2.0 / values.shape[-1]
    freq = ROPE_BASE ** (-ladder)
    angle = positions.astype(jnp.float32)[:, None] * freq[None, :]
    cosine = jnp.cos(angle)[:, None, :]
    sine = jnp.sin(angle)[:, None, :]
    first = values[..., :half]
    second = values[..., half:]
    return jnp.concatenate(
        [first * cosine - second * sine, second * cosine + first * sine], axis=-1
    )


def attend_block(state, key_rows, value_rows, queries, query_pos, scale):
    best, total, accum = state
    rows = key_rows.shape[0]
    heads = queries.shape[1]
    width = queries.shape[2]
    keys_three = key_rows.reshape(rows, heads, width)
    values_three = value_rows.reshape(rows, heads, width)
    scores = (
        jnp.einsum("qhd,khd->hqk", queries, keys_three, preferred_element_type=jnp.float32) * scale
    )
    key_pos = jnp.arange(rows, dtype=jnp.int32)
    allowed = key_pos[None, None, :] <= query_pos[None, :, None]
    block_best = jnp.max(jnp.where(allowed, scores, MASKED), axis=-1)
    new_best = jnp.maximum(best, block_best)
    weights = jnp.where(allowed, jnp.exp(scores - new_best[..., None]), 0.0)
    total = jnp.sum(weights, axis=-1)
    product = jnp.einsum(
        "hqk,khd->hqd",
        weights.astype(jnp.bfloat16),
        values_three,
        preferred_element_type=jnp.float32,
    )
    accum = product
    return (new_best, total, accum)


def local(
    text_embed, frame_feats, frame_count, proj_weight, norm_gain, q_weight, k_weight, v_weight
):
    tok_rows = text_embed.shape[0]
    vision = jnp.dot(
        lax.all_gather(frame_feats, ("section", "tp"), axis=1, tiled=True),
        proj_weight,
        preferred_element_type=jnp.float32,
    )
    offsets = jnp.arange(tok_rows, dtype=jnp.int32)
    is_frame = offsets < frame_count[0]
    joined = jnp.where(is_frame[:, None], vision, text_embed.astype(jnp.float32)).astype(
        jnp.bfloat16
    )
    whole = lax.all_gather(joined, ("section", "tp"), axis=1, tiled=True)
    wide = whole.astype(jnp.float32)
    mean_square = jnp.mean(wide * wide, axis=-1, keepdims=True)
    normed = (wide * lax.rsqrt(mean_square + NORM_EPS) * norm_gain.astype(jnp.float32)).astype(
        jnp.bfloat16
    )
    head_cols = q_weight.shape[1]

    def add_rows(piece):
        return jnp.dot(normed, piece, preferred_element_type=jnp.float32)

    q_full = add_rows(lax.all_gather(q_weight, "ctx", axis=0, tiled=True))
    k_full = add_rows(lax.all_gather(k_weight, "ctx", axis=0, tiled=True))
    v_full = add_rows(lax.all_gather(v_weight, "ctx", axis=0, tiled=True))
    first_pos = lax.axis_index("ctx") * tok_rows
    query_pos = first_pos + offsets
    heads = head_cols // HD
    queries = rotate(q_full.reshape(tok_rows, heads, HD), query_pos).astype(jnp.bfloat16)
    keys = (
        rotate(k_full.reshape(tok_rows, heads, HD), query_pos)
        .astype(jnp.bfloat16)
        .reshape(tok_rows, head_cols)
    )
    values = v_full.astype(jnp.bfloat16)
    scale = 1.0 / math.sqrt(HD)
    initial = (
        jnp.full((heads, tok_rows), MASKED, jnp.float32),
        jnp.zeros((heads, tok_rows), jnp.float32),
        jnp.zeros((heads, tok_rows, HD), jnp.float32),
    )
    state = attend_block(
        initial,
        lax.all_gather(keys, "ctx", axis=0, tiled=True),
        lax.all_gather(values, "ctx", axis=0, tiled=True),
        queries,
        query_pos,
        scale,
    )
    best, total, accum = state
    result = accum / total[..., None]
    return result.transpose(1, 0, 2).reshape(tok_rows, head_cols).astype(jnp.bfloat16)


MESH = pl.DeviceIdType.MESH
F32 = jnp.float32
BF16 = jnp.bfloat16


def rope_tables(tokens):
    half = HD // 2
    freq = ROPE_BASE ** (-(np.arange(half, dtype=np.float64) * 2.0 / HD))
    angle = np.arange(tokens, dtype=np.float64)[:, None] * freq[None, :]
    cosine, sine = np.cos(angle), np.sin(angle)
    return (
        np.concatenate([cosine, cosine], axis=1).astype(np.float32),
        np.concatenate([-sine, sine], axis=1).astype(np.float32),
    )


def fused_kernel(
    text_ref,
    feats_ref,
    count_ref,
    gain_ref,
    proj_hbm,
    q_hbm,
    k_hbm,
    v_hbm,
    cos_hbm,
    sin_hbm,
    out_ref,
    proj,
    weight,
    cos_tab,
    sin_tab,
    feats,
    vision,
    joined,
    blocks,
    partial,
    squares,
    own,
    own_row,
    core_out,
    core_in,
    y_out,
    y_in,
    queries,
    keys,
    values,
    head_out,
    head_in,
    load_sem,
    feats_send,
    feats_recv,
    entry_send,
    next_send,
    back_send,
    block_recv,
    core_send,
    core_recv,
    y_send,
    y_recv,
    head_send,
    head_recv,
):
    ctx = lax.axis_index("ctx")
    x = lax.axis_index("section")
    z = lax.axis_index("tp")
    y = ctx // 2
    core = ctx % 2
    g = x * 4 + z

    def at(c, s, t):
        return {"ctx": c, "section": s, "tp": t}

    loads = [
        pltpu.make_async_copy(proj_hbm, proj, load_sem.at[0]),
        pltpu.make_async_copy(cos_hbm, cos_tab, load_sem.at[1]),
        pltpu.make_async_copy(sin_hbm, sin_tab, load_sem.at[2]),
    ]
    for place, head in enumerate((core, 1 - core)):
        for kind, source in enumerate((q_hbm, k_hbm, v_hbm)):
            loads.append(
                pltpu.make_async_copy(
                    source.at[:, pl.ds(pl.multiple_of(head * HD, HD), HD)],
                    weight.at[:, pl.ds((place * 3 + kind) * HD, HD)],
                    load_sem.at[3 + place * 3 + kind],
                )
            )
    for load in loads:
        load.start()

    barrier = pltpu.get_barrier_semaphore()

    def greet_plane(k, carry):
        other = (ctx * 2 + x + k) % 8
        pl.semaphore_signal(
            barrier, inc=1, device_id=at(other // 2, other % 2, z), device_id_type=MESH
        )
        return carry

    lax.fori_loop(1, 8, greet_plane, 0)

    def greet_line(k, carry):
        for side in (0, 1):
            pl.semaphore_signal(
                barrier, inc=1, device_id=at(ctx, side, (z + k) % 4), device_id_type=MESH
            )
        return carry

    lax.fori_loop(1, 4, greet_line, 0)
    pl.semaphore_wait(barrier, 13)

    def feats_copy(k):
        other = (g + k) % 8
        return pltpu.make_async_remote_copy(
            src_ref=feats_ref,
            dst_ref=feats.at[k],
            send_sem=feats_send.at[k],
            recv_sem=feats_recv.at[k],
            device_id=at(ctx, other // 4, other % 4),
            device_id_type=MESH,
        )

    def send_feats(k, carry):
        feats_copy(k).start()
        return carry

    lax.fori_loop(1, 8, send_feats, 0)
    loads[0].wait()

    def proj_rows(owner):
        return proj[pl.ds(pl.multiple_of(owner * 128, 128), 128), :]

    vision[...] = jnp.dot(feats_ref[...], proj_rows(g), preferred_element_type=F32)

    def add_feats(k, carry):
        feats_copy(k).wait_recv()
        vision[...] += jnp.dot(feats[k], proj_rows((g + 8 - k) % 8), preferred_element_type=F32)
        return carry

    lax.fori_loop(1, 8, add_feats, 0)
    rows = lax.broadcasted_iota(jnp.int32, (128, 512), 0)
    mixed = jnp.where(rows < count_ref[0], vision[...], text_ref[...].astype(F32)).astype(BF16)
    joined[...] = mixed

    to_core = z // 2
    to_ctx = x * 2 + to_core
    to_part = z * (1 - to_core) + (3 - z) * to_core

    def entry_copy(side):
        return pltpu.make_async_remote_copy(
            src_ref=joined,
            dst_ref=blocks.at[ctx * 2 + to_part],
            send_sem=entry_send.at[side],
            recv_sem=block_recv.at[ctx * 2 + to_part],
            device_id=at(to_ctx, side, z),
            device_id_type=MESH,
        )

    stays = to_ctx == ctx
    for side in (0, 1):
        here = jnp.logical_and(stays, x == side)

        @pl.when(here)
        def _():
            blocks[ctx * 2 + to_part] = mixed

        @pl.when(jnp.logical_not(here))
        def _():
            entry_copy(side).start()

    level = z * (1 - core) + (3 - z) * core
    step = 1 - 2 * core

    def block_arrival(slot):
        pltpu.make_async_copy(blocks.at[slot], blocks.at[slot], block_recv.at[slot]).wait()

    def next_copy(slot):
        return pltpu.make_async_remote_copy(
            src_ref=blocks.at[slot],
            dst_ref=blocks.at[slot],
            send_sem=next_send.at[slot],
            recv_sem=block_recv.at[slot],
            device_id=at(ctx, x, (z + step + 4) % 4),
            device_id_type=MESH,
        )

    def back_copy(c):
        slot = c * 2 + 1
        return pltpu.make_async_remote_copy(
            src_ref=blocks.at[slot],
            dst_ref=blocks.at[slot],
            send_sem=back_send.at[c],
            recv_sem=block_recv.at[slot],
            device_id=at(ctx, x, (z - step + 4) % 4),
            device_id_type=MESH,
        )

    @pl.when(level <= 1)
    def _():
        def pass_on(c, carry):
            slot = c * 2 + level
            local_block = jnp.logical_and(c == ctx, x == y)

            @pl.when(jnp.logical_not(local_block))
            def _():
                block_arrival(slot)

            next_copy(slot).start()

            @pl.when(level == 1)
            def _():
                back_copy(c).start()

            return carry

        lax.fori_loop(0, 4, pass_on, 0)

    for load in loads[1:]:
        load.wait()

    def product(slot, part):
        offset = (part + core) % 2 * 512
        block = blocks[slot].astype(F32)
        gain = gain_ref[:, pl.ds(pl.multiple_of(ctx * 1024 + offset, 512), 512)]
        scaled = (block * gain).astype(BF16)
        square = block * block
        lanes = (square[:, :128] + square[:, 128:256]) + (square[:, 256:384] + square[:, 384:])
        rows_of = pl.ds(pl.multiple_of(offset, 512), 512)
        return jnp.dot(scaled, weight[rows_of, :], preferred_element_type=F32), lanes

    def first_part(c, carry):
        slot = c * 2 + 1

        @pl.when(level != 1)
        def _():
            block_arrival(slot)

        @pl.when(level == 2)
        def _():
            next_copy(slot).start()

        result, lanes = product(slot, 1)
        partial[c] = result
        squares[c] = lanes
        return carry

    lax.fori_loop(0, 4, first_part, 0)

    @pl.when(level == 1)
    def _():
        def pass_on(c, carry):
            block_arrival(c * 2)
            next_copy(c * 2).start()
            return carry

        lax.fori_loop(0, 4, pass_on, 0)

    def core_copy(r):
        return pltpu.make_async_remote_copy(
            src_ref=core_out.at[r],
            dst_ref=core_in.at[r],
            send_sem=core_send.at[r],
            recv_sem=core_recv.at[r],
            device_id=at(y * 2 + 1 - core, x, z),
            device_id_type=MESH,
        )

    def y_copy(r, kinds):
        columns = pl.ds((3 - kinds) * HD, kinds * HD)
        return pltpu.make_async_remote_copy(
            src_ref=y_out.at[r, :, columns],
            dst_ref=y_in.at[r, :, columns],
            send_sem=y_send.at[r],
            recv_sem=y_recv.at[r],
            device_id=at((1 - y) * 2 + core, x, z),
            device_id_type=MESH,
        )

    def write_row(ref, r, row):
        high = row.astype(BF16)
        low = (row - high.astype(F32)).astype(BF16)
        ref[r, 128:144, 0:128] = jnp.zeros((16, 128), BF16)
        ref[r, 128:144, 128:256] = jnp.broadcast_to(high, (16, 128))
        ref[r, 128:144, 256:384] = jnp.broadcast_to(low, (16, 128))

    def read_row(ref, r):
        tail = ref[r, 128:144, 128:384].astype(F32)
        return tail[0:1, 0:128] + tail[0:1, 128:256]

    def core_sum(r):
        core_copy(r).wait_recv()
        total = own[r] + core_in[r, 0:128, :].astype(F32)
        row = own_row[r, 0:1, :] + read_row(core_in, r)
        own[r] = total
        own_row[r] = jnp.broadcast_to(row, (8, 128))
        y_out[r, 0:128, :] = total.astype(BF16)
        write_row(y_out, r, row)

        @pl.when(jnp.logical_and(y == 0, r < 2))
        def _():
            y_copy(r, 2).start()

        @pl.when(jnp.logical_or(jnp.logical_and(y == 0, r >= 2), jnp.logical_and(y == 1, r < 2)))
        def _():
            y_copy(r, 3).start()

    def second_part(c, carry):
        slot = c * 2

        @pl.when(level >= 2)
        def _():
            block_arrival(slot)

        @pl.when(level == 2)
        def _():
            next_copy(slot).start()

        result, lanes = product(slot, 0)
        result = partial[c] + result
        own[c] = result[:, :384]
        core_out[c, 0:128, :] = result[:, 384:].astype(BF16)
        row = jnp.sum((squares[c] + lanes).T, axis=0, keepdims=True)
        own_row[c] = jnp.broadcast_to(row, (8, 128))
        write_row(core_out, c, row)
        core_copy(c).start()

        @pl.when(c >= 1)
        def _():
            core_sum(c - 1)

        return carry

    lax.fori_loop(0, 4, second_part, 0)
    core_sum(3)

    def turn(vector, r):
        rows_of = pl.ds(r * 128, 128)
        return vector * cos_tab[rows_of, :] + pltpu.roll(vector, HD // 2, 1) * sin_tab[rows_of, :]

    def finish(r, with_query):
        row = own_row[r, 0:1, :] + read_row(y_in, r)
        factor = lax.rsqrt(row * (1.0 / 4096.0) + NORM_EPS)
        factor = jnp.broadcast_to(factor, (128, 128)).T

        def whole(kind):
            columns = pl.ds(kind * HD, HD)
            return (own[r, :, columns] + y_in[r, 0:128, columns].astype(F32)) * factor

        if with_query:
            queries[pl.ds(r % 2 * 128, 128), :] = turn(whole(0), r).astype(BF16)
        keys[pl.ds(r * 128, 128), :] = turn(whole(1), r).astype(BF16)
        values[pl.ds(r * 128, 128), :] = whole(2).astype(BF16)

    def attend(r, count):
        query = queries[pl.ds(pl.multiple_of(r % 2 * 128, 128), 128), :]
        scores = lax.dot_general(
            query, keys[0:count, :], (((1,), (1,)), ((), ())), preferred_element_type=F32
        ) * (1.0 / math.sqrt(HD))
        place = r * 128 + lax.broadcasted_iota(jnp.int32, (128, count), 0)
        allowed = lax.broadcasted_iota(jnp.int32, (128, count), 1) <= place
        best = jnp.max(jnp.where(allowed, scores, MASKED), axis=1, keepdims=True)
        weights = jnp.where(allowed, jnp.exp(scores - best), 0.0)
        total = jnp.sum(weights, axis=1, keepdims=True)
        out = jnp.dot(weights.astype(BF16), values[0:count, :], preferred_element_type=F32)
        return (out / total).astype(BF16)

    head_copy = pltpu.make_async_remote_copy(
        src_ref=head_out,
        dst_ref=head_in,
        send_sem=head_send,
        recv_sem=head_recv,
        device_id=at(y * 2 + 1 - core, x, z),
        device_id_type=MESH,
    )

    def both_heads(count):
        head_out[...] = attend(y * 2 + 1 - core, count)
        head_copy.start()
        out_ref[:, pl.ds(pl.multiple_of(core * HD, HD), HD)] = attend(ctx, count)

    @pl.when(y == 0)
    def _():
        for r in (0, 1):
            y_copy(r, 3).wait_recv()
            finish(r, True)
        both_heads(256)

    @pl.when(y == 1)
    def _():
        for r in (0, 1):
            y_copy(r, 2).wait_recv()
            finish(r, False)
        for r in (2, 3):
            y_copy(r, 3).wait_recv()
            finish(r, True)
        both_heads(512)

    head_copy.wait_recv()
    out_ref[:, pl.ds(pl.multiple_of((1 - core) * HD, HD), HD)] = head_in[...]

    head_copy.wait_send()

    def drain_feats(k, carry):
        feats_copy(k).wait_send()
        return carry

    lax.fori_loop(1, 8, drain_feats, 0)
    for side in (0, 1):

        @pl.when(jnp.logical_not(jnp.logical_and(stays, x == side)))
        def _():
            entry_copy(side).wait_send()

    def drain(c, carry):
        core_copy(c).wait_send()

        @pl.when(level <= 2)
        def _():
            next_copy(c * 2 + lax.min(level, 1)).wait_send()

        @pl.when(jnp.logical_or(level == 1, level == 2))
        def _():
            next_copy(c * 2).wait_send()

        @pl.when(level == 1)
        def _():
            back_copy(c).wait_send()

        return carry

    lax.fori_loop(0, 4, drain, 0)

    @pl.when(y == 0)
    def _():
        for r in range(4):
            y_copy(r, 2 if r < 2 else 3).wait_send()

    @pl.when(y == 1)
    def _():
        for r in range(2):
            y_copy(r, 3).wait_send()


def fused(
    text_embed, frame_feats, frame_count, proj_weight, norm_gain, q_weight, k_weight, v_weight
):
    cosine, sine = rope_tables(512)
    vmem = pl.BlockSpec(memory_space=pltpu.VMEM)
    hbm = pl.BlockSpec(memory_space=pl.ANY)
    dma = pltpu.SemaphoreType.DMA
    return pl.pallas_call(
        fused_kernel,
        out_shape=jax.ShapeDtypeStruct((128, 256), BF16),
        in_specs=[vmem, vmem, pl.BlockSpec(memory_space=pltpu.SMEM), vmem] + [hbm] * 6,
        out_specs=vmem,
        scratch_shapes=[
            pltpu.VMEM((1024, 512), BF16),
            pltpu.VMEM((1024, 768), BF16),
            pltpu.VMEM((512, HD), F32),
            pltpu.VMEM((512, HD), F32),
            pltpu.VMEM((8, 128, 128), BF16),
            pltpu.VMEM((128, 512), F32),
            pltpu.VMEM((128, 512), BF16),
            pltpu.VMEM((8, 128, 512), BF16),
            pltpu.VMEM((4, 128, 768), F32),
            pltpu.VMEM((4, 128, 128), F32),
            pltpu.VMEM((4, 128, 384), F32),
            pltpu.VMEM((4, 8, 128), F32),
            pltpu.VMEM((4, 144, 384), BF16),
            pltpu.VMEM((4, 144, 384), BF16),
            pltpu.VMEM((4, 144, 384), BF16),
            pltpu.VMEM((4, 144, 384), BF16),
            pltpu.VMEM((256, HD), BF16),
            pltpu.VMEM((512, HD), BF16),
            pltpu.VMEM((512, HD), BF16),
            pltpu.VMEM((128, HD), BF16),
            pltpu.VMEM((128, HD), BF16),
            dma((9,)),
            dma((8,)),
            dma((8,)),
            dma((2,)),
            dma((8,)),
            dma((4,)),
            dma((8,)),
            dma((4,)),
            dma((4,)),
            dma((4,)),
            dma((4,)),
            dma,
            dma,
        ],
        compiler_params=pltpu.CompilerParams(
            collective_id=0, has_side_effects=True, vmem_limit_bytes=40 * 1024 * 1024
        ),
    )(
        text_embed,
        frame_feats,
        frame_count,
        norm_gain.astype(F32).reshape(1, -1),
        proj_weight,
        q_weight,
        k_weight,
        v_weight,
        jnp.asarray(cosine),
        jnp.asarray(sine),
    )


def solution(mesh):
    small = (mesh.shape["ctx"], mesh.shape["section"], mesh.shape["tp"]) == (4, 2, 4)
    body = fused if small else local
    in_specs = (
        P("ctx", ("section", "tp")),
        P("ctx", ("section", "tp")),
        P("ctx"),
        P(None, ("section", "tp")),
        P(),
        P("ctx", ("section", "tp")),
        P("ctx", ("section", "tp")),
        P("ctx", ("section", "tp")),
    )
    out_specs = P("ctx", ("section", "tp"))
    return jax.shard_map(body, mesh=mesh, in_specs=in_specs, out_specs=out_specs, check_vma=False)
```

```python
import math

import jax
import jax.numpy as jnp
import numpy as np
from jax import lax
from jax.experimental import pallas as pl
from jax.experimental.pallas import tpu as pltpu
from jax.sharding import PartitionSpec as P

HD = 128


ROPE_BASE = 1000000.0
NORM_EPS = 1e-05
MASKED = -1e30


def rotate(values, positions):
    half = values.shape[-1] // 2
    ladder = jnp.arange(half, dtype=jnp.float32) * 2.0 / values.shape[-1]
    freq = ROPE_BASE ** (-ladder)
    angle = positions.astype(jnp.float32)[:, None] * freq[None, :]
    cosine = jnp.cos(angle)[:, None, :]
    sine = jnp.sin(angle)[:, None, :]
    first = values[..., :half]
    second = values[..., half:]
    return jnp.concatenate(
        [first * cosine - second * sine, second * cosine + first * sine], axis=-1
    )


def attend_block(state, key_rows, value_rows, queries, query_pos, scale):
    best, total, accum = state
    rows = key_rows.shape[0]
    heads = queries.shape[1]
    width = queries.shape[2]
    keys_three = key_rows.reshape(rows, heads, width)
    values_three = value_rows.reshape(rows, heads, width)
    scores = (
        jnp.einsum("qhd,khd->hqk", queries, keys_three, preferred_element_type=jnp.float32) * scale
    )
    key_pos = jnp.arange(rows, dtype=jnp.int32)
    allowed = key_pos[None, None, :] <= query_pos[None, :, None]
    block_best = jnp.max(jnp.where(allowed, scores, MASKED), axis=-1)
    new_best = jnp.maximum(best, block_best)
    weights = jnp.where(allowed, jnp.exp(scores - new_best[..., None]), 0.0)
    total = jnp.sum(weights, axis=-1)
    product = jnp.einsum(
        "hqk,khd->hqd",
        weights.astype(jnp.bfloat16),
        values_three,
        preferred_element_type=jnp.float32,
    )
    accum = product
    return (new_best, total, accum)


def local(
    text_embed, frame_feats, frame_count, proj_weight, norm_gain, q_weight, k_weight, v_weight
):
    tok_rows = text_embed.shape[0]
    vision = jnp.dot(
        lax.all_gather(frame_feats, ("section", "tp"), axis=1, tiled=True),
        proj_weight,
        preferred_element_type=jnp.float32,
    )
    offsets = jnp.arange(tok_rows, dtype=jnp.int32)
    is_frame = offsets < frame_count[0]
    joined = jnp.where(is_frame[:, None], vision, text_embed.astype(jnp.float32)).astype(
        jnp.bfloat16
    )
    whole = lax.all_gather(joined, ("section", "tp"), axis=1, tiled=True)
    wide = whole.astype(jnp.float32)
    mean_square = jnp.mean(wide * wide, axis=-1, keepdims=True)
    normed = (wide * lax.rsqrt(mean_square + NORM_EPS) * norm_gain.astype(jnp.float32)).astype(
        jnp.bfloat16
    )
    head_cols = q_weight.shape[1]

    def add_rows(piece):
        return jnp.dot(normed, piece, preferred_element_type=jnp.float32)

    q_full = add_rows(lax.all_gather(q_weight, "ctx", axis=0, tiled=True))
    k_full = add_rows(lax.all_gather(k_weight, "ctx", axis=0, tiled=True))
    v_full = add_rows(lax.all_gather(v_weight, "ctx", axis=0, tiled=True))
    first_pos = lax.axis_index("ctx") * tok_rows
    query_pos = first_pos + offsets
    heads = head_cols // HD
    queries = rotate(q_full.reshape(tok_rows, heads, HD), query_pos).astype(jnp.bfloat16)
    keys = (
        rotate(k_full.reshape(tok_rows, heads, HD), query_pos)
        .astype(jnp.bfloat16)
        .reshape(tok_rows, head_cols)
    )
    values = v_full.astype(jnp.bfloat16)
    scale = 1.0 / math.sqrt(HD)
    initial = (
        jnp.full((heads, tok_rows), MASKED, jnp.float32),
        jnp.zeros((heads, tok_rows), jnp.float32),
        jnp.zeros((heads, tok_rows, HD), jnp.float32),
    )
    state = attend_block(
        initial,
        lax.all_gather(keys, "ctx", axis=0, tiled=True),
        lax.all_gather(values, "ctx", axis=0, tiled=True),
        queries,
        query_pos,
        scale,
    )
    best, total, accum = state
    result = accum / total[..., None]
    return result.transpose(1, 0, 2).reshape(tok_rows, head_cols).astype(jnp.bfloat16)


MESH = pl.DeviceIdType.MESH
F32 = jnp.float32
BF16 = jnp.bfloat16


def rope_tables(tokens):
    half = HD // 2
    freq = ROPE_BASE ** (-(np.arange(half, dtype=np.float64) * 2.0 / HD))
    angle = np.arange(tokens, dtype=np.float64)[:, None] * freq[None, :]
    cosine, sine = np.cos(angle), np.sin(angle)
    return (
        np.concatenate([cosine, cosine], axis=1).astype(np.float32),
        np.concatenate([-sine, sine], axis=1).astype(np.float32),
    )


def fused_kernel(
    text_hbm,
    feats_hbm,
    count_ref,
    gain_hbm,
    proj_hbm,
    q_hbm,
    k_hbm,
    v_hbm,
    cos_hbm,
    sin_hbm,
    out_ref,
    proj,
    weight,
    cos_tab,
    sin_tab,
    gain_raw,
    gain_ref,
    text_ref,
    feats,
    vision,
    joined,
    blocks,
    partial,
    squares,
    own,
    own_row,
    core_out,
    core_in,
    y_out,
    y_in,
    queries,
    keys,
    values,
    head_out,
    head_in,
    load_sem,
    feats_send,
    feats_recv,
    entry_send,
    next_send,
    back_send,
    block_recv,
    core_send,
    core_recv,
    y_send,
    y_recv,
    head_send,
    head_recv,
):
    ctx = lax.axis_index("ctx")
    x = lax.axis_index("section")
    z = lax.axis_index("tp")
    y = ctx // 2
    core = ctx % 2
    g = x * 4 + z

    def at(c, s, t):
        return {"ctx": c, "section": s, "tp": t}

    feats_load = pltpu.make_async_copy(feats_hbm, feats.at[0], load_sem.at[10])
    feats_load.start()
    loads = [
        pltpu.make_async_copy(proj_hbm, proj, load_sem.at[0]),
        pltpu.make_async_copy(text_hbm, text_ref, load_sem.at[11]),
        pltpu.make_async_copy(cos_hbm, cos_tab, load_sem.at[1]),
        pltpu.make_async_copy(sin_hbm, sin_tab, load_sem.at[2]),
        pltpu.make_async_copy(
            gain_hbm.at[pl.ds(pl.multiple_of(ctx * 1024, 1024), 1024)], gain_raw, load_sem.at[9]
        ),
    ]
    for place, head in enumerate((core, 1 - core)):
        for kind, source in enumerate((q_hbm, k_hbm, v_hbm)):
            loads.append(
                pltpu.make_async_copy(
                    source.at[:, pl.ds(pl.multiple_of(head * HD, HD), HD)],
                    weight.at[:, pl.ds((place * 3 + kind) * HD, HD)],
                    load_sem.at[3 + place * 3 + kind],
                )
            )
    for load in loads:
        load.start()

    barrier = pltpu.get_barrier_semaphore()

    def greet_plane(k, carry):
        other = (ctx * 2 + x + k) % 8
        pl.semaphore_signal(
            barrier, inc=1, device_id=at(other // 2, other % 2, z), device_id_type=MESH
        )
        return carry

    lax.fori_loop(1, 8, greet_plane, 0)

    def greet_line(k, carry):
        for side in (0, 1):
            pl.semaphore_signal(
                barrier, inc=1, device_id=at(ctx, side, (z + k) % 4), device_id_type=MESH
            )
        return carry

    lax.fori_loop(1, 4, greet_line, 0)
    feats_load.wait()
    pl.semaphore_wait(barrier, 13)

    def feats_copy(k):
        other = (g + k) % 8
        return pltpu.make_async_remote_copy(
            src_ref=feats.at[0],
            dst_ref=feats.at[k],
            send_sem=feats_send.at[k],
            recv_sem=feats_recv.at[k],
            device_id=at(ctx, other // 4, other % 4),
            device_id_type=MESH,
        )

    def send_feats(k, carry):
        feats_copy(k).start()
        return carry

    lax.fori_loop(1, 8, send_feats, 0)
    loads[0].wait()
    loads[1].wait()

    def proj_rows(owner):
        return proj[pl.ds(pl.multiple_of(owner * 128, 128), 128), :]

    vision[...] = jnp.dot(feats[0], proj_rows(g), preferred_element_type=F32)

    def add_feats(k, carry):
        feats_copy(k).wait_recv()
        vision[...] += jnp.dot(feats[k], proj_rows((g + 8 - k) % 8), preferred_element_type=F32)
        return carry

    lax.fori_loop(1, 8, add_feats, 0)
    rows = lax.broadcasted_iota(jnp.int32, (128, 512), 0)
    mixed = jnp.where(rows < count_ref[0], vision[...], text_ref[...].astype(F32)).astype(BF16)
    joined[...] = mixed

    to_core = z // 2
    to_ctx = x * 2 + to_core
    to_part = z * (1 - to_core) + (3 - z) * to_core

    def entry_copy(side):
        return pltpu.make_async_remote_copy(
            src_ref=joined,
            dst_ref=blocks.at[ctx * 2 + to_part],
            send_sem=entry_send.at[side],
            recv_sem=block_recv.at[ctx * 2 + to_part],
            device_id=at(to_ctx, side, z),
            device_id_type=MESH,
        )

    stays = to_ctx == ctx
    for side in (0, 1):
        here = jnp.logical_and(stays, x == side)

        @pl.when(here)
        def _():
            blocks[ctx * 2 + to_part] = mixed

        @pl.when(jnp.logical_not(here))
        def _():
            entry_copy(side).start()

    level = z * (1 - core) + (3 - z) * core
    step = 1 - 2 * core

    def block_arrival(slot):
        pltpu.make_async_copy(blocks.at[slot], blocks.at[slot], block_recv.at[slot]).wait()

    def next_copy(slot):
        return pltpu.make_async_remote_copy(
            src_ref=blocks.at[slot],
            dst_ref=blocks.at[slot],
            send_sem=next_send.at[slot],
            recv_sem=block_recv.at[slot],
            device_id=at(ctx, x, (z + step + 4) % 4),
            device_id_type=MESH,
        )

    def back_copy(c):
        slot = c * 2 + 1
        return pltpu.make_async_remote_copy(
            src_ref=blocks.at[slot],
            dst_ref=blocks.at[slot],
            send_sem=back_send.at[c],
            recv_sem=block_recv.at[slot],
            device_id=at(ctx, x, (z - step + 4) % 4),
            device_id_type=MESH,
        )

    @pl.when(level <= 1)
    def _():
        def pass_on(c, carry):
            slot = c * 2 + level
            local_block = jnp.logical_and(c == ctx, x == y)

            @pl.when(jnp.logical_not(local_block))
            def _():
                block_arrival(slot)

            next_copy(slot).start()

            @pl.when(level == 1)
            def _():
                back_copy(c).start()

            return carry

        lax.fori_loop(0, 4, pass_on, 0)

    for load in loads[2:]:
        load.wait()
    gain_ref[...] = gain_raw[...].astype(F32).reshape(1, 1024)

    def product(slot, part):
        offset = (part + core) % 2 * 512
        block = blocks[slot].astype(F32)
        gain = gain_ref[:, pl.ds(pl.multiple_of(offset, 512), 512)]
        scaled = (block * gain).astype(BF16)
        square = block * block
        lanes = (square[:, :128] + square[:, 128:256]) + (square[:, 256:384] + square[:, 384:])
        rows_of = pl.ds(pl.multiple_of(offset, 512), 512)
        return jnp.dot(scaled, weight[rows_of, :], preferred_element_type=F32), lanes

    def first_part(c, carry):
        slot = c * 2 + 1

        @pl.when(level != 1)
        def _():
            block_arrival(slot)

        @pl.when(level == 2)
        def _():
            next_copy(slot).start()

        result, lanes = product(slot, 1)
        partial[c] = result
        squares[c] = lanes
        return carry

    lax.fori_loop(0, 4, first_part, 0)

    @pl.when(level == 1)
    def _():
        def pass_on(c, carry):
            block_arrival(c * 2)
            next_copy(c * 2).start()
            return carry

        lax.fori_loop(0, 4, pass_on, 0)

    def core_copy(r):
        return pltpu.make_async_remote_copy(
            src_ref=core_out.at[r],
            dst_ref=core_in.at[r],
            send_sem=core_send.at[r],
            recv_sem=core_recv.at[r],
            device_id=at(y * 2 + 1 - core, x, z),
            device_id_type=MESH,
        )

    def y_copy(r, kinds):
        columns = pl.ds((3 - kinds) * HD, kinds * HD)
        return pltpu.make_async_remote_copy(
            src_ref=y_out.at[r, :, columns],
            dst_ref=y_in.at[r, :, columns],
            send_sem=y_send.at[r],
            recv_sem=y_recv.at[r],
            device_id=at((1 - y) * 2 + core, x, z),
            device_id_type=MESH,
        )

    def write_row(ref, r, row):
        high = row.astype(BF16)
        low = (row - high.astype(F32)).astype(BF16)
        ref[r, 128:144, 0:128] = jnp.zeros((16, 128), BF16)
        ref[r, 128:144, 128:256] = jnp.broadcast_to(high, (16, 128))
        ref[r, 128:144, 256:384] = jnp.broadcast_to(low, (16, 128))

    def read_row(ref, r):
        tail = ref[r, 128:144, 128:384].astype(F32)
        return tail[0:1, 0:128] + tail[0:1, 128:256]

    def core_sum(r):
        core_copy(r).wait_recv()
        total = own[r] + core_in[r, 0:128, :].astype(F32)
        row = own_row[r, 0:1, :] + read_row(core_in, r)
        own[r] = total
        own_row[r] = jnp.broadcast_to(row, (8, 128))
        y_out[r, 0:128, :] = total.astype(BF16)
        write_row(y_out, r, row)

        @pl.when(jnp.logical_and(y == 0, r < 2))
        def _():
            y_copy(r, 2).start()

        @pl.when(jnp.logical_or(jnp.logical_and(y == 0, r >= 2), jnp.logical_and(y == 1, r < 2)))
        def _():
            y_copy(r, 3).start()

    def second_part(c, carry):
        slot = c * 2

        @pl.when(level >= 2)
        def _():
            block_arrival(slot)

        @pl.when(level == 2)
        def _():
            next_copy(slot).start()

        result, lanes = product(slot, 0)
        result = partial[c] + result
        own[c] = result[:, :384]
        core_out[c, 0:128, :] = result[:, 384:].astype(BF16)
        row = jnp.sum((squares[c] + lanes).T, axis=0, keepdims=True)
        own_row[c] = jnp.broadcast_to(row, (8, 128))
        write_row(core_out, c, row)
        core_copy(c).start()

        @pl.when(c >= 1)
        def _():
            core_sum(c - 1)

        return carry

    lax.fori_loop(0, 4, second_part, 0)
    core_sum(3)

    def turn(vector, r):
        rows_of = pl.ds(r * 128, 128)
        return vector * cos_tab[rows_of, :] + pltpu.roll(vector, HD // 2, 1) * sin_tab[rows_of, :]

    def finish(r, with_query):
        row = own_row[r, 0:1, :] + read_row(y_in, r)
        factor = lax.rsqrt(row * (1.0 / 4096.0) + NORM_EPS)
        factor = jnp.broadcast_to(factor, (128, 128)).T

        def whole(kind):
            columns = pl.ds(kind * HD, HD)
            return (own[r, :, columns] + y_in[r, 0:128, columns].astype(F32)) * factor

        if with_query:
            queries[pl.ds(r % 2 * 128, 128), :] = turn(whole(0), r).astype(BF16)
        keys[pl.ds(r * 128, 128), :] = turn(whole(1), r).astype(BF16)
        values[pl.ds(r * 128, 128), :] = whole(2).astype(BF16)

    def attend(r, count):
        query = queries[pl.ds(pl.multiple_of(r % 2 * 128, 128), 128), :]
        scores = lax.dot_general(
            query, keys[0:count, :], (((1,), (1,)), ((), ())), preferred_element_type=F32
        ) * (1.0 / math.sqrt(HD))
        place = r * 128 + lax.broadcasted_iota(jnp.int32, (128, count), 0)
        allowed = lax.broadcasted_iota(jnp.int32, (128, count), 1) <= place
        best = jnp.max(jnp.where(allowed, scores, MASKED), axis=1, keepdims=True)
        weights = jnp.where(allowed, jnp.exp(scores - best), 0.0)
        total = jnp.sum(weights, axis=1, keepdims=True)
        out = jnp.dot(weights.astype(BF16), values[0:count, :], preferred_element_type=F32)
        return (out / total).astype(BF16)

    head_copy = pltpu.make_async_remote_copy(
        src_ref=head_out,
        dst_ref=head_in,
        send_sem=head_send,
        recv_sem=head_recv,
        device_id=at(y * 2 + 1 - core, x, z),
        device_id_type=MESH,
    )

    def both_heads(count):
        head_out[...] = attend(y * 2 + 1 - core, count)
        head_copy.start()
        out_ref[:, pl.ds(pl.multiple_of(core * HD, HD), HD)] = attend(ctx, count)

    @pl.when(y == 0)
    def _():
        for r in (0, 1):
            y_copy(r, 3).wait_recv()
            finish(r, True)
        both_heads(256)

    @pl.when(y == 1)
    def _():
        for r in (0, 1):
            y_copy(r, 2).wait_recv()
            finish(r, False)
        for r in (2, 3):
            y_copy(r, 3).wait_recv()
            finish(r, True)
        both_heads(512)

    head_copy.wait_recv()
    out_ref[:, pl.ds(pl.multiple_of((1 - core) * HD, HD), HD)] = head_in[...]

    head_copy.wait_send()

    def drain_feats(k, carry):
        feats_copy(k).wait_send()
        return carry

    lax.fori_loop(1, 8, drain_feats, 0)
    for side in (0, 1):

        @pl.when(jnp.logical_not(jnp.logical_and(stays, x == side)))
        def _():
            entry_copy(side).wait_send()

    def drain(c, carry):
        core_copy(c).wait_send()

        @pl.when(level <= 2)
        def _():
            next_copy(c * 2 + lax.min(level, 1)).wait_send()

        @pl.when(jnp.logical_or(level == 1, level == 2))
        def _():
            next_copy(c * 2).wait_send()

        @pl.when(level == 1)
        def _():
            back_copy(c).wait_send()

        return carry

    lax.fori_loop(0, 4, drain, 0)

    @pl.when(y == 0)
    def _():
        for r in range(4):
            y_copy(r, 2 if r < 2 else 3).wait_send()

    @pl.when(y == 1)
    def _():
        for r in range(2):
            y_copy(r, 3).wait_send()


def fused(
    text_embed, frame_feats, frame_count, proj_weight, norm_gain, q_weight, k_weight, v_weight
):
    cosine, sine = rope_tables(512)
    vmem = pl.BlockSpec(memory_space=pltpu.VMEM)
    hbm = pl.BlockSpec(memory_space=pltpu.MemorySpace.HBM)
    dma = pltpu.SemaphoreType.DMA
    return pl.pallas_call(
        fused_kernel,
        out_shape=jax.ShapeDtypeStruct((128, 256), BF16),
        in_specs=[hbm, hbm, pl.BlockSpec(memory_space=pltpu.SMEM)] + [hbm] * 7,
        out_specs=vmem,
        scratch_shapes=[
            pltpu.VMEM((1024, 512), BF16),
            pltpu.VMEM((1024, 768), BF16),
            pltpu.VMEM((512, HD), F32),
            pltpu.VMEM((512, HD), F32),
            pltpu.VMEM((1024,), BF16),
            pltpu.VMEM((1, 1024), F32),
            pltpu.VMEM((128, 512), BF16),
            pltpu.VMEM((8, 128, 128), BF16),
            pltpu.VMEM((128, 512), F32),
            pltpu.VMEM((128, 512), BF16),
            pltpu.VMEM((8, 128, 512), BF16),
            pltpu.VMEM((4, 128, 768), F32),
            pltpu.VMEM((4, 128, 128), F32),
            pltpu.VMEM((4, 128, 384), F32),
            pltpu.VMEM((4, 8, 128), F32),
            pltpu.VMEM((4, 144, 384), BF16),
            pltpu.VMEM((4, 144, 384), BF16),
            pltpu.VMEM((4, 144, 384), BF16),
            pltpu.VMEM((4, 144, 384), BF16),
            pltpu.VMEM((256, HD), BF16),
            pltpu.VMEM((512, HD), BF16),
            pltpu.VMEM((512, HD), BF16),
            pltpu.VMEM((128, HD), BF16),
            pltpu.VMEM((128, HD), BF16),
            dma((12,)),
            dma((8,)),
            dma((8,)),
            dma((2,)),
            dma((8,)),
            dma((4,)),
            dma((8,)),
            dma((4,)),
            dma((4,)),
            dma((4,)),
            dma((4,)),
            dma,
            dma,
        ],
        compiler_params=pltpu.CompilerParams(
            collective_id=0, has_side_effects=True, vmem_limit_bytes=63 * 1024 * 1024
        ),
    )(
        text_embed,
        frame_feats,
        frame_count,
        norm_gain,
        proj_weight,
        q_weight,
        k_weight,
        v_weight,
        jnp.asarray(cosine),
        jnp.asarray(sine),
    )


def solution(mesh):
    small = (mesh.shape["ctx"], mesh.shape["section"], mesh.shape["tp"]) == (4, 2, 4)
    body = fused if small else local
    in_specs = (
        P("ctx", ("section", "tp")),
        P("ctx", ("section", "tp")),
        P("ctx"),
        P(None, ("section", "tp")),
        P(),
        P("ctx", ("section", "tp")),
        P("ctx", ("section", "tp")),
        P("ctx", ("section", "tp")),
    )
    out_specs = P("ctx", ("section", "tp"))
    return jax.shard_map(body, mesh=mesh, in_specs=in_specs, out_specs=out_specs, check_vma=False)
```

```python
import math

import jax
import jax.numpy as jnp
import numpy as np
from jax import lax
from jax.experimental import pallas as pl
from jax.experimental.pallas import tpu as pltpu
from jax.sharding import PartitionSpec as P

HD = 128


ROPE_BASE = 1000000.0
NORM_EPS = 1e-05
MASKED = -1e30


def rotate(values, positions):
    half = values.shape[-1] // 2
    ladder = jnp.arange(half, dtype=jnp.float32) * 2.0 / values.shape[-1]
    freq = ROPE_BASE ** (-ladder)
    angle = positions.astype(jnp.float32)[:, None] * freq[None, :]
    cosine = jnp.cos(angle)[:, None, :]
    sine = jnp.sin(angle)[:, None, :]
    first = values[..., :half]
    second = values[..., half:]
    return jnp.concatenate(
        [first * cosine - second * sine, second * cosine + first * sine], axis=-1
    )


def attend_block(state, key_rows, value_rows, queries, query_pos, scale):
    best, total, accum = state
    rows = key_rows.shape[0]
    heads = queries.shape[1]
    width = queries.shape[2]
    keys_three = key_rows.reshape(rows, heads, width)
    values_three = value_rows.reshape(rows, heads, width)
    scores = (
        jnp.einsum("qhd,khd->hqk", queries, keys_three, preferred_element_type=jnp.float32) * scale
    )
    key_pos = jnp.arange(rows, dtype=jnp.int32)
    allowed = key_pos[None, None, :] <= query_pos[None, :, None]
    block_best = jnp.max(jnp.where(allowed, scores, MASKED), axis=-1)
    new_best = jnp.maximum(best, block_best)
    weights = jnp.where(allowed, jnp.exp(scores - new_best[..., None]), 0.0)
    total = jnp.sum(weights, axis=-1)
    product = jnp.einsum(
        "hqk,khd->hqd",
        weights.astype(jnp.bfloat16),
        values_three,
        preferred_element_type=jnp.float32,
    )
    accum = product
    return (new_best, total, accum)


def local(
    text_embed, frame_feats, frame_count, proj_weight, norm_gain, q_weight, k_weight, v_weight
):
    tok_rows = text_embed.shape[0]
    vision = jnp.dot(
        lax.all_gather(frame_feats, ("section", "tp"), axis=1, tiled=True),
        proj_weight,
        preferred_element_type=jnp.float32,
    )
    offsets = jnp.arange(tok_rows, dtype=jnp.int32)
    is_frame = offsets < frame_count[0]
    joined = jnp.where(is_frame[:, None], vision, text_embed.astype(jnp.float32)).astype(
        jnp.bfloat16
    )
    whole = lax.all_gather(joined, ("section", "tp"), axis=1, tiled=True)
    wide = whole.astype(jnp.float32)
    mean_square = jnp.mean(wide * wide, axis=-1, keepdims=True)
    normed = (wide * lax.rsqrt(mean_square + NORM_EPS) * norm_gain.astype(jnp.float32)).astype(
        jnp.bfloat16
    )
    head_cols = q_weight.shape[1]

    def add_rows(piece):
        return jnp.dot(normed, piece, preferred_element_type=jnp.float32)

    q_full = add_rows(lax.all_gather(q_weight, "ctx", axis=0, tiled=True))
    k_full = add_rows(lax.all_gather(k_weight, "ctx", axis=0, tiled=True))
    v_full = add_rows(lax.all_gather(v_weight, "ctx", axis=0, tiled=True))
    first_pos = lax.axis_index("ctx") * tok_rows
    query_pos = first_pos + offsets
    heads = head_cols // HD
    queries = rotate(q_full.reshape(tok_rows, heads, HD), query_pos).astype(jnp.bfloat16)
    keys = (
        rotate(k_full.reshape(tok_rows, heads, HD), query_pos)
        .astype(jnp.bfloat16)
        .reshape(tok_rows, head_cols)
    )
    values = v_full.astype(jnp.bfloat16)
    scale = 1.0 / math.sqrt(HD)
    initial = (
        jnp.full((heads, tok_rows), MASKED, jnp.float32),
        jnp.zeros((heads, tok_rows), jnp.float32),
        jnp.zeros((heads, tok_rows, HD), jnp.float32),
    )
    state = attend_block(
        initial,
        lax.all_gather(keys, "ctx", axis=0, tiled=True),
        lax.all_gather(values, "ctx", axis=0, tiled=True),
        queries,
        query_pos,
        scale,
    )
    best, total, accum = state
    result = accum / total[..., None]
    return result.transpose(1, 0, 2).reshape(tok_rows, head_cols).astype(jnp.bfloat16)


MESH = pl.DeviceIdType.MESH
F32 = jnp.float32
BF16 = jnp.bfloat16


def rope_tables(tokens):
    half = HD // 2
    freq = ROPE_BASE ** (-(np.arange(half, dtype=np.float64) * 2.0 / HD))
    angle = np.arange(tokens, dtype=np.float64)[:, None] * freq[None, :]
    cosine, sine = np.cos(angle), np.sin(angle)
    return (
        np.concatenate([cosine, cosine], axis=1).astype(np.float32),
        np.concatenate([-sine, sine], axis=1).astype(np.float32),
    )


def fused_kernel(
    text_hbm,
    feats_hbm,
    count_ref,
    gain_hbm,
    proj_hbm,
    q_hbm,
    k_hbm,
    v_hbm,
    cos_hbm,
    sin_hbm,
    out_ref,
    proj,
    weight,
    cos_tab,
    sin_tab,
    gain_raw,
    gain_ref,
    text_ref,
    feats,
    vision,
    joined,
    blocks,
    partial,
    squares,
    own,
    own_row,
    core_out,
    core_in,
    y_out,
    y_in,
    queries,
    keys,
    values,
    head_out,
    head_in,
    load_sem,
    feats_send,
    feats_recv,
    entry_send,
    next_send,
    back_send,
    cross_send,
    block_recv,
    core_send,
    core_recv,
    y_send,
    y_recv,
    head_send,
    head_recv,
):
    ctx = lax.axis_index("ctx")
    x = lax.axis_index("section")
    z = lax.axis_index("tp")
    y = ctx // 2
    core = ctx % 2
    g = x * 4 + z

    def at(c, s, t):
        return {"ctx": c, "section": s, "tp": t}

    feats_load = pltpu.make_async_copy(feats_hbm, feats.at[0], load_sem.at[10])
    feats_load.start()
    loads = [
        pltpu.make_async_copy(proj_hbm, proj, load_sem.at[0]),
        pltpu.make_async_copy(text_hbm, text_ref, load_sem.at[11]),
        pltpu.make_async_copy(cos_hbm, cos_tab, load_sem.at[1]),
        pltpu.make_async_copy(sin_hbm, sin_tab, load_sem.at[2]),
        pltpu.make_async_copy(
            gain_hbm.at[pl.ds(pl.multiple_of(ctx * 1024, 1024), 1024)], gain_raw, load_sem.at[9]
        ),
    ]
    for place, head in enumerate((core, 1 - core)):
        for kind, source in enumerate((q_hbm, k_hbm, v_hbm)):
            loads.append(
                pltpu.make_async_copy(
                    source.at[:, pl.ds(pl.multiple_of(head * HD, HD), HD)],
                    weight.at[:, pl.ds((place * 3 + kind) * HD, HD)],
                    load_sem.at[3 + place * 3 + kind],
                )
            )
    for load in loads:
        load.start()

    barrier = pltpu.get_barrier_semaphore()

    def greet_plane(k, carry):
        other = (ctx * 2 + x + k) % 8
        pl.semaphore_signal(
            barrier, inc=1, device_id=at(other // 2, other % 2, z), device_id_type=MESH
        )
        return carry

    lax.fori_loop(1, 8, greet_plane, 0)

    def greet_line(k, carry):
        for side in (0, 1):
            pl.semaphore_signal(
                barrier, inc=1, device_id=at(ctx, side, (z + k) % 4), device_id_type=MESH
            )
        return carry

    lax.fori_loop(1, 4, greet_line, 0)
    feats_load.wait()
    pl.semaphore_wait(barrier, 13)

    def feats_copy(k):
        return pltpu.make_async_remote_copy(
            src_ref=feats.at[0],
            dst_ref=feats.at[k * 2],
            send_sem=feats_send.at[k * 2],
            recv_sem=feats_recv.at[k * 2],
            device_id=at(ctx, x, (z + k) % 4),
            device_id_type=MESH,
        )

    def feats_cross(k):
        return pltpu.make_async_remote_copy(
            src_ref=feats.at[k * 2],
            dst_ref=feats.at[k * 2 + 1],
            send_sem=feats_send.at[k * 2 + 1],
            recv_sem=feats_recv.at[k * 2 + 1],
            device_id=at(ctx, 1 - x, z),
            device_id_type=MESH,
        )

    for k in (1, 3, 2):
        feats_copy(k).start()
    feats_cross(0).start()
    loads[0].wait()
    loads[1].wait()

    def feats_dot(k, side):
        owner = (x * (1 - side) + (1 - x) * side) * 4 + (z + 4 - k) % 4
        rows_of = pl.ds(pl.multiple_of(owner * 128, 128), 128)
        return jnp.dot(feats[k * 2 + side], proj[rows_of, :], preferred_element_type=F32)

    vision[...] = feats_dot(0, 0)
    for k in (1, 3, 2):
        feats_copy(k).wait_recv()
        feats_cross(k).start()
    vision[...] += (feats_dot(1, 0) + feats_dot(3, 0)) + feats_dot(2, 0)
    for k in (0, 1, 3, 2):
        feats_cross(k).wait_recv()
        vision[...] += feats_dot(k, 1)
    rows = lax.broadcasted_iota(jnp.int32, (128, 512), 0)
    mixed = jnp.where(rows < count_ref[0], vision[...], text_ref[...].astype(F32)).astype(BF16)
    joined[...] = mixed

    to_core = z // 2
    to_ctx = x * 2 + to_core
    to_part = z * (1 - to_core) + (3 - z) * to_core

    def entry_copy(side):
        return pltpu.make_async_remote_copy(
            src_ref=joined,
            dst_ref=blocks.at[ctx * 2 + to_part],
            send_sem=entry_send.at[side],
            recv_sem=block_recv.at[ctx * 2 + to_part],
            device_id=at(to_ctx, side, z),
            device_id_type=MESH,
        )

    stays = to_ctx == ctx
    for side in (0, 1):
        here = jnp.logical_and(stays, x == side)

        @pl.when(here)
        def _():
            blocks[ctx * 2 + to_part] = mixed

        @pl.when(jnp.logical_not(here))
        def _():
            entry_copy(side).start()

    level = z * (1 - core) + (3 - z) * core
    step = 1 - 2 * core

    mine = (1 - (x + y) % 2) * 2

    def nth(i):
        return (i + mine) % 4

    def carried(i):
        return i < 2

    def block_arrival(slot):
        pltpu.make_async_copy(blocks.at[slot], blocks.at[slot], block_recv.at[slot]).wait()

    def next_copy(slot):
        return pltpu.make_async_remote_copy(
            src_ref=blocks.at[slot],
            dst_ref=blocks.at[slot],
            send_sem=next_send.at[slot],
            recv_sem=block_recv.at[slot],
            device_id=at(ctx, x, (z + step + 4) % 4),
            device_id_type=MESH,
        )

    def cross_copy(slot):
        return pltpu.make_async_remote_copy(
            src_ref=blocks.at[slot],
            dst_ref=blocks.at[slot],
            send_sem=cross_send.at[slot],
            recv_sem=block_recv.at[slot],
            device_id=at(ctx, 1 - x, z),
            device_id_type=MESH,
        )

    def back_copy(c):
        slot = c * 2 + 1
        return pltpu.make_async_remote_copy(
            src_ref=blocks.at[slot],
            dst_ref=blocks.at[slot],
            send_sem=back_send.at[c],
            recv_sem=block_recv.at[slot],
            device_id=at(ctx, x, (z - step + 4) % 4),
            device_id_type=MESH,
        )

    @pl.when(level <= 1)
    def _():
        def pass_on(i, carry):
            c = nth(i)
            slot = c * 2 + level
            local_block = jnp.logical_and(c == ctx, x == y)

            @pl.when(jnp.logical_not(local_block))
            def _():
                block_arrival(slot)

            @pl.when(jnp.logical_or(level == 0, carried(i)))
            def _():
                next_copy(slot).start()

            @pl.when(level == 1)
            def _():
                back_copy(c).start()

            return carry

        lax.fori_loop(0, 4, pass_on, 0)

    for load in loads[2:]:
        load.wait()
    gain_ref[...] = gain_raw[...].astype(F32).reshape(1, 1024)

    def product(slot, part):
        offset = (part + core) % 2 * 512
        block = blocks[slot].astype(F32)
        gain = gain_ref[:, pl.ds(pl.multiple_of(offset, 512), 512)]
        scaled = (block * gain).astype(BF16)
        square = block * block
        lanes = (square[:, :128] + square[:, 128:256]) + (square[:, 256:384] + square[:, 384:])
        rows_of = pl.ds(pl.multiple_of(offset, 512), 512)
        return jnp.dot(scaled, weight[rows_of, :], preferred_element_type=F32), lanes

    def forward(i, slot):
        @pl.when(jnp.logical_and(level == 2, carried(i)))
        def _():
            next_copy(slot).start()

        @pl.when(jnp.logical_and(level >= 2, carried(i)))
        def _():
            cross_copy(slot).start()

    def first_part(i, carry):
        c = nth(i)
        slot = c * 2 + 1

        @pl.when(level != 1)
        def _():
            block_arrival(slot)

        forward(i, slot)
        result, lanes = product(slot, 1)
        partial[c] = result
        squares[c] = lanes
        return carry

    lax.fori_loop(0, 4, first_part, 0)

    @pl.when(level == 1)
    def _():
        def pass_on(i, carry):
            slot = nth(i) * 2
            block_arrival(slot)

            @pl.when(carried(i))
            def _():
                next_copy(slot).start()

            return carry

        lax.fori_loop(0, 4, pass_on, 0)

    def core_copy(r):
        return pltpu.make_async_remote_copy(
            src_ref=core_out.at[r],
            dst_ref=core_in.at[r],
            send_sem=core_send.at[r],
            recv_sem=core_recv.at[r],
            device_id=at(y * 2 + 1 - core, x, z),
            device_id_type=MESH,
        )

    def y_copy(r, kinds):
        columns = pl.ds((3 - kinds) * HD, kinds * HD)
        return pltpu.make_async_remote_copy(
            src_ref=y_out.at[r, :, columns],
            dst_ref=y_in.at[r, :, columns],
            send_sem=y_send.at[r],
            recv_sem=y_recv.at[r],
            device_id=at((1 - y) * 2 + core, x, z),
            device_id_type=MESH,
        )

    def write_row(ref, r, row):
        high = row.astype(BF16)
        low = (row - high.astype(F32)).astype(BF16)
        ref[r, 128:144, 0:128] = jnp.zeros((16, 128), BF16)
        ref[r, 128:144, 128:256] = jnp.broadcast_to(high, (16, 128))
        ref[r, 128:144, 256:384] = jnp.broadcast_to(low, (16, 128))

    def read_row(ref, r):
        tail = ref[r, 128:144, 128:384].astype(F32)
        return tail[0:1, 0:128] + tail[0:1, 128:256]

    def core_sum(r):
        core_copy(r).wait_recv()
        total = own[r] + core_in[r, 0:128, :].astype(F32)
        row = own_row[r, 0:1, :] + read_row(core_in, r)
        own[r] = total
        own_row[r] = jnp.broadcast_to(row, (8, 128))
        y_out[r, 0:128, :] = total.astype(BF16)
        write_row(y_out, r, row)

        @pl.when(jnp.logical_and(y == 0, r < 2))
        def _():
            y_copy(r, 2).start()

        @pl.when(jnp.logical_or(jnp.logical_and(y == 0, r >= 2), jnp.logical_and(y == 1, r < 2)))
        def _():
            y_copy(r, 3).start()

    def second_part(i, carry):
        c = nth(i)
        slot = c * 2

        @pl.when(level >= 2)
        def _():
            block_arrival(slot)

        forward(i, slot)
        result, lanes = product(slot, 0)
        result = partial[c] + result
        own[c] = result[:, :384]
        core_out[c, 0:128, :] = result[:, 384:].astype(BF16)
        row = jnp.sum((squares[c] + lanes).T, axis=0, keepdims=True)
        own_row[c] = jnp.broadcast_to(row, (8, 128))
        write_row(core_out, c, row)
        core_copy(c).start()

        @pl.when(i >= 1)
        def _():
            core_sum(nth(i + 3))

        return carry

    lax.fori_loop(0, 4, second_part, 0)
    core_sum(nth(3))

    def turn(vector, r):
        rows_of = pl.ds(r * 128, 128)
        return vector * cos_tab[rows_of, :] + pltpu.roll(vector, HD // 2, 1) * sin_tab[rows_of, :]

    def finish(r, with_query):
        row = own_row[r, 0:1, :] + read_row(y_in, r)
        factor = lax.rsqrt(row * (1.0 / 4096.0) + NORM_EPS)
        factor = jnp.broadcast_to(factor, (128, 128)).T

        def whole(kind):
            columns = pl.ds(kind * HD, HD)
            return (own[r, :, columns] + y_in[r, 0:128, columns].astype(F32)) * factor

        if with_query:
            queries[pl.ds(r % 2 * 128, 128), :] = turn(whole(0), r).astype(BF16)
        keys[pl.ds(r * 128, 128), :] = turn(whole(1), r).astype(BF16)
        values[pl.ds(r * 128, 128), :] = whole(2).astype(BF16)

    def attend(r, count):
        query = queries[pl.ds(pl.multiple_of(r % 2 * 128, 128), 128), :]
        scores = lax.dot_general(
            query, keys[0:count, :], (((1,), (1,)), ((), ())), preferred_element_type=F32
        ) * (1.0 / math.sqrt(HD))
        place = r * 128 + lax.broadcasted_iota(jnp.int32, (128, count), 0)
        allowed = lax.broadcasted_iota(jnp.int32, (128, count), 1) <= place
        best = jnp.max(jnp.where(allowed, scores, MASKED), axis=1, keepdims=True)
        weights = jnp.where(allowed, jnp.exp(scores - best), 0.0)
        total = jnp.sum(weights, axis=1, keepdims=True)
        out = jnp.dot(weights.astype(BF16), values[0:count, :], preferred_element_type=F32)
        return (out / total).astype(BF16)

    head_copy = pltpu.make_async_remote_copy(
        src_ref=head_out,
        dst_ref=head_in,
        send_sem=head_send,
        recv_sem=head_recv,
        device_id=at(y * 2 + 1 - core, x, z),
        device_id_type=MESH,
    )

    def both_heads(count):
        head_out[...] = attend(y * 2 + 1 - core, count)
        head_copy.start()
        out_ref[:, pl.ds(pl.multiple_of(core * HD, HD), HD)] = attend(ctx, count)

    @pl.when(y == 0)
    def _():
        for r in (0, 1):
            y_copy(r, 3).wait_recv()
            finish(r, True)
        both_heads(256)

    @pl.when(y == 1)
    def _():
        for r in (0, 1):
            y_copy(r, 2).wait_recv()
            finish(r, False)
        for r in (2, 3):
            y_copy(r, 3).wait_recv()
            finish(r, True)
        both_heads(512)

    head_copy.wait_recv()
    out_ref[:, pl.ds(pl.multiple_of((1 - core) * HD, HD), HD)] = head_in[...]

    head_copy.wait_send()

    for k in range(4):
        feats_cross(k).wait_send()
        if k > 0:
            feats_copy(k).wait_send()
    for side in (0, 1):

        @pl.when(jnp.logical_not(jnp.logical_and(stays, x == side)))
        def _():
            entry_copy(side).wait_send()

    def drain(i, carry):
        c = nth(i)
        core_copy(c).wait_send()

        @pl.when(level == 0)
        def _():
            next_copy(c * 2).wait_send()

        @pl.when(level == 1)
        def _():
            back_copy(c).wait_send()

        for part in (0, 1):

            @pl.when(jnp.logical_and(carried(i), jnp.logical_or(level == 1, level == 2)))
            def _():
                next_copy(c * 2 + part).wait_send()

            @pl.when(jnp.logical_and(carried(i), level >= 2))
            def _():
                cross_copy(c * 2 + part).wait_send()

        return carry

    lax.fori_loop(0, 4, drain, 0)

    @pl.when(y == 0)
    def _():
        for r in range(4):
            y_copy(r, 2 if r < 2 else 3).wait_send()

    @pl.when(y == 1)
    def _():
        for r in range(2):
            y_copy(r, 3).wait_send()


def fused(
    text_embed, frame_feats, frame_count, proj_weight, norm_gain, q_weight, k_weight, v_weight
):
    cosine, sine = rope_tables(512)
    vmem = pl.BlockSpec(memory_space=pltpu.VMEM)
    hbm = pl.BlockSpec(memory_space=pltpu.MemorySpace.HBM)
    dma = pltpu.SemaphoreType.DMA
    return pl.pallas_call(
        fused_kernel,
        out_shape=jax.ShapeDtypeStruct((128, 256), BF16),
        in_specs=[hbm, hbm, pl.BlockSpec(memory_space=pltpu.SMEM)] + [hbm] * 7,
        out_specs=vmem,
        scratch_shapes=[
            pltpu.VMEM((1024, 512), BF16),
            pltpu.VMEM((1024, 768), BF16),
            pltpu.VMEM((512, HD), F32),
            pltpu.VMEM((512, HD), F32),
            pltpu.VMEM((1024,), BF16),
            pltpu.VMEM((1, 1024), F32),
            pltpu.VMEM((128, 512), BF16),
            pltpu.VMEM((8, 128, 128), BF16),
            pltpu.VMEM((128, 512), F32),
            pltpu.VMEM((128, 512), BF16),
            pltpu.VMEM((8, 128, 512), BF16),
            pltpu.VMEM((4, 128, 768), F32),
            pltpu.VMEM((4, 128, 128), F32),
            pltpu.VMEM((4, 128, 384), F32),
            pltpu.VMEM((4, 8, 128), F32),
            pltpu.VMEM((4, 144, 384), BF16),
            pltpu.VMEM((4, 144, 384), BF16),
            pltpu.VMEM((4, 144, 384), BF16),
            pltpu.VMEM((4, 144, 384), BF16),
            pltpu.VMEM((256, HD), BF16),
            pltpu.VMEM((512, HD), BF16),
            pltpu.VMEM((512, HD), BF16),
            pltpu.VMEM((128, HD), BF16),
            pltpu.VMEM((128, HD), BF16),
            dma((12,)),
            dma((8,)),
            dma((8,)),
            dma((2,)),
            dma((8,)),
            dma((4,)),
            dma((8,)),
            dma((8,)),
            dma((4,)),
            dma((4,)),
            dma((4,)),
            dma((4,)),
            dma,
            dma,
        ],
        compiler_params=pltpu.CompilerParams(
            collective_id=0, has_side_effects=True, vmem_limit_bytes=63 * 1024 * 1024
        ),
    )(
        text_embed,
        frame_feats,
        frame_count,
        norm_gain,
        proj_weight,
        q_weight,
        k_weight,
        v_weight,
        jnp.asarray(cosine),
        jnp.asarray(sine),
    )


def solution(mesh):
    small = (mesh.shape["ctx"], mesh.shape["section"], mesh.shape["tp"]) == (4, 2, 4)
    body = fused if small else local
    in_specs = (
        P("ctx", ("section", "tp")),
        P("ctx", ("section", "tp")),
        P("ctx"),
        P(None, ("section", "tp")),
        P(),
        P("ctx", ("section", "tp")),
        P("ctx", ("section", "tp")),
        P("ctx", ("section", "tp")),
    )
    out_specs = P("ctx", ("section", "tp"))
    return jax.shard_map(body, mesh=mesh, in_specs=in_specs, out_specs=out_specs, check_vma=False)
```

```python
import math

import jax
import jax.numpy as jnp
import numpy as np
from jax import lax
from jax.experimental import pallas as pl
from jax.experimental.pallas import tpu as pltpu
from jax.sharding import PartitionSpec as P

HD = 128


ROPE_BASE = 1000000.0
NORM_EPS = 1e-05
MASKED = -1e30


def rotate(values, positions):
    half = values.shape[-1] // 2
    ladder = jnp.arange(half, dtype=jnp.float32) * 2.0 / values.shape[-1]
    freq = ROPE_BASE ** (-ladder)
    angle = positions.astype(jnp.float32)[:, None] * freq[None, :]
    cosine = jnp.cos(angle)[:, None, :]
    sine = jnp.sin(angle)[:, None, :]
    first = values[..., :half]
    second = values[..., half:]
    return jnp.concatenate(
        [first * cosine - second * sine, second * cosine + first * sine], axis=-1
    )


def attend_block(state, key_rows, value_rows, queries, query_pos, scale):
    best, total, accum = state
    rows = key_rows.shape[0]
    heads = queries.shape[1]
    width = queries.shape[2]
    keys_three = key_rows.reshape(rows, heads, width)
    values_three = value_rows.reshape(rows, heads, width)
    scores = (
        jnp.einsum("qhd,khd->hqk", queries, keys_three, preferred_element_type=jnp.float32) * scale
    )
    key_pos = jnp.arange(rows, dtype=jnp.int32)
    allowed = key_pos[None, None, :] <= query_pos[None, :, None]
    block_best = jnp.max(jnp.where(allowed, scores, MASKED), axis=-1)
    new_best = jnp.maximum(best, block_best)
    weights = jnp.where(allowed, jnp.exp(scores - new_best[..., None]), 0.0)
    total = jnp.sum(weights, axis=-1)
    product = jnp.einsum(
        "hqk,khd->hqd",
        weights.astype(jnp.bfloat16),
        values_three,
        preferred_element_type=jnp.float32,
    )
    accum = product
    return (new_best, total, accum)


def local(
    text_embed, frame_feats, frame_count, proj_weight, norm_gain, q_weight, k_weight, v_weight
):
    tok_rows = text_embed.shape[0]
    vision = jnp.dot(
        lax.all_gather(frame_feats, ("section", "tp"), axis=1, tiled=True),
        proj_weight,
        preferred_element_type=jnp.float32,
    )
    offsets = jnp.arange(tok_rows, dtype=jnp.int32)
    is_frame = offsets < frame_count[0]
    joined = jnp.where(is_frame[:, None], vision, text_embed.astype(jnp.float32)).astype(
        jnp.bfloat16
    )
    whole = lax.all_gather(joined, ("section", "tp"), axis=1, tiled=True)
    wide = whole.astype(jnp.float32)
    mean_square = jnp.mean(wide * wide, axis=-1, keepdims=True)
    normed = (wide * lax.rsqrt(mean_square + NORM_EPS) * norm_gain.astype(jnp.float32)).astype(
        jnp.bfloat16
    )
    head_cols = q_weight.shape[1]

    def add_rows(piece):
        return jnp.dot(normed, piece, preferred_element_type=jnp.float32)

    q_full = add_rows(lax.all_gather(q_weight, "ctx", axis=0, tiled=True))
    k_full = add_rows(lax.all_gather(k_weight, "ctx", axis=0, tiled=True))
    v_full = add_rows(lax.all_gather(v_weight, "ctx", axis=0, tiled=True))
    first_pos = lax.axis_index("ctx") * tok_rows
    query_pos = first_pos + offsets
    heads = head_cols // HD
    queries = rotate(q_full.reshape(tok_rows, heads, HD), query_pos).astype(jnp.bfloat16)
    keys = (
        rotate(k_full.reshape(tok_rows, heads, HD), query_pos)
        .astype(jnp.bfloat16)
        .reshape(tok_rows, head_cols)
    )
    values = v_full.astype(jnp.bfloat16)
    scale = 1.0 / math.sqrt(HD)
    initial = (
        jnp.full((heads, tok_rows), MASKED, jnp.float32),
        jnp.zeros((heads, tok_rows), jnp.float32),
        jnp.zeros((heads, tok_rows, HD), jnp.float32),
    )
    state = attend_block(
        initial,
        lax.all_gather(keys, "ctx", axis=0, tiled=True),
        lax.all_gather(values, "ctx", axis=0, tiled=True),
        queries,
        query_pos,
        scale,
    )
    best, total, accum = state
    result = accum / total[..., None]
    return result.transpose(1, 0, 2).reshape(tok_rows, head_cols).astype(jnp.bfloat16)


MESH = pl.DeviceIdType.MESH
F32 = jnp.float32
BF16 = jnp.bfloat16


def rope_tables(tokens):
    half = HD // 2
    freq = ROPE_BASE ** (-(np.arange(half, dtype=np.float64) * 2.0 / HD))
    angle = np.arange(tokens, dtype=np.float64)[:, None] * freq[None, :]
    cosine, sine = np.cos(angle), np.sin(angle)
    return (
        np.concatenate([cosine, cosine], axis=1).astype(np.float32),
        np.concatenate([-sine, sine], axis=1).astype(np.float32),
    )


def fused_kernel(
    text_hbm,
    feats_hbm,
    count_ref,
    gain_hbm,
    proj_hbm,
    q_hbm,
    k_hbm,
    v_hbm,
    cos_hbm,
    sin_hbm,
    out_ref,
    proj,
    weight,
    cos_tab,
    sin_tab,
    gain_raw,
    gain_ref,
    text_ref,
    feats,
    vision,
    joined,
    blocks,
    own,
    own_row,
    core_out,
    core_in,
    y_out,
    y_in,
    queries,
    keys,
    values,
    head_out,
    head_in,
    load_sem,
    feats_send,
    feats_recv,
    entry_send,
    line_send,
    cross_send,
    block_recv,
    core_send,
    core_recv,
    y_send,
    y_recv,
    head_send,
    head_recv,
):
    ctx = lax.axis_index("ctx")
    x = lax.axis_index("section")
    z = lax.axis_index("tp")
    y = ctx // 2
    core = ctx % 2
    g = x * 4 + z

    def at(c, s, t):
        return {"ctx": c, "section": s, "tp": t}

    feats_load = pltpu.make_async_copy(feats_hbm, feats.at[0], load_sem.at[10])
    feats_load.start()
    loads = [
        pltpu.make_async_copy(proj_hbm, proj, load_sem.at[0]),
        pltpu.make_async_copy(text_hbm, text_ref, load_sem.at[11]),
        pltpu.make_async_copy(cos_hbm, cos_tab, load_sem.at[1]),
        pltpu.make_async_copy(sin_hbm, sin_tab, load_sem.at[2]),
        pltpu.make_async_copy(
            gain_hbm.at[pl.ds(pl.multiple_of(ctx * 1024, 1024), 1024)], gain_raw, load_sem.at[9]
        ),
    ]
    for place, head in enumerate((core, 1 - core)):
        for kind, source in enumerate((q_hbm, k_hbm, v_hbm)):
            loads.append(
                pltpu.make_async_copy(
                    source.at[:, pl.ds(pl.multiple_of(head * HD, HD), HD)],
                    weight.at[:, pl.ds((place * 3 + kind) * HD, HD)],
                    load_sem.at[3 + place * 3 + kind],
                )
            )
    for load in loads:
        load.start()

    barrier = pltpu.get_barrier_semaphore()

    def greet_plane(k, carry):
        other = (ctx * 2 + x + k) % 8
        pl.semaphore_signal(
            barrier, inc=1, device_id=at(other // 2, other % 2, z), device_id_type=MESH
        )
        return carry

    lax.fori_loop(1, 8, greet_plane, 0)

    def greet_line(k, carry):
        for side in (0, 1):
            pl.semaphore_signal(
                barrier, inc=1, device_id=at(ctx, side, (z + k) % 4), device_id_type=MESH
            )
        return carry

    lax.fori_loop(1, 4, greet_line, 0)
    feats_load.wait()
    pl.semaphore_wait(barrier, 13)

    def feats_copy(k):
        return pltpu.make_async_remote_copy(
            src_ref=feats.at[0],
            dst_ref=feats.at[k * 2],
            send_sem=feats_send.at[k * 2],
            recv_sem=feats_recv.at[k * 2],
            device_id=at(ctx, x, (z + k) % 4),
            device_id_type=MESH,
        )

    def feats_cross(k):
        return pltpu.make_async_remote_copy(
            src_ref=feats.at[k * 2],
            dst_ref=feats.at[k * 2 + 1],
            send_sem=feats_send.at[k * 2 + 1],
            recv_sem=feats_recv.at[k * 2 + 1],
            device_id=at(ctx, 1 - x, z),
            device_id_type=MESH,
        )

    for k in (1, 3, 2):
        feats_copy(k).start()
    feats_cross(0).start()
    loads[0].wait()
    loads[1].wait()

    def feats_dot(k, side):
        owner = (x * (1 - side) + (1 - x) * side) * 4 + (z + 4 - k) % 4
        rows_of = pl.ds(pl.multiple_of(owner * 128, 128), 128)
        return jnp.dot(feats[k * 2 + side], proj[rows_of, :], preferred_element_type=F32)

    vision[...] = feats_dot(0, 0)
    for k in (1, 3, 2):
        feats_copy(k).wait_recv()
        feats_cross(k).start()
    vision[...] += (feats_dot(1, 0) + feats_dot(3, 0)) + feats_dot(2, 0)
    for k in (0, 1, 3, 2):
        feats_cross(k).wait_recv()
        vision[...] += feats_dot(k, 1)
    rows = lax.broadcasted_iota(jnp.int32, (128, 512), 0)
    mixed = jnp.where(rows < count_ref[0], vision[...], text_ref[...].astype(F32)).astype(BF16)
    joined[...] = mixed

    to_core = z // 2
    to_ctx = x * 2 + to_core
    to_part = z * (1 - to_core) + (3 - z) * to_core

    def entry_copy(side):
        return pltpu.make_async_remote_copy(
            src_ref=joined,
            dst_ref=blocks.at[ctx * 2 + to_part],
            send_sem=entry_send.at[side],
            recv_sem=block_recv.at[ctx * 2 + to_part],
            device_id=at(to_ctx, side, z),
            device_id_type=MESH,
        )

    stays = to_ctx == ctx
    for side in (0, 1):
        here = jnp.logical_and(stays, x == side)

        @pl.when(here)
        def _():
            blocks[ctx * 2 + to_part] = mixed

        @pl.when(jnp.logical_not(here))
        def _():
            entry_copy(side).start()

    level = z * (1 - core) + (3 - z) * core

    mine = (1 - (x + y) % 2) * 2

    def nth(i):
        return (i + mine) % 4

    def carried(i):
        return i < 2

    def block_arrival(slot):
        pltpu.make_async_copy(blocks.at[slot], blocks.at[slot], block_recv.at[slot]).wait()

    def line_copy(c, to_level):
        slot = c * 2 + level
        return pltpu.make_async_remote_copy(
            src_ref=blocks.at[slot],
            dst_ref=blocks.at[slot],
            send_sem=line_send.at[c * 4 + to_level],
            recv_sem=block_recv.at[slot],
            device_id=at(ctx, x, to_level * (1 - core) + (3 - to_level) * core),
            device_id_type=MESH,
        )

    def cross_copy(slot):
        return pltpu.make_async_remote_copy(
            src_ref=blocks.at[slot],
            dst_ref=blocks.at[slot],
            send_sem=cross_send.at[slot],
            recv_sem=block_recv.at[slot],
            device_id=at(ctx, 1 - x, z),
            device_id_type=MESH,
        )

    @pl.when(level <= 1)
    def _():
        def pass_on(i, carry):
            c = nth(i)
            slot = c * 2 + level
            local_block = jnp.logical_and(c == ctx, x == y)

            @pl.when(jnp.logical_not(local_block))
            def _():
                block_arrival(slot)

            @pl.when(carried(i))
            def _():
                line_copy(c, 3).start()
                line_copy(c, 2).start()

            line_copy(c, 1 - level).start()
            return carry

        lax.fori_loop(0, 4, pass_on, 0)

    for load in loads[2:]:
        load.wait()
    gain_ref[...] = gain_raw[...].astype(F32).reshape(1, 1024)

    def product(slot, part):
        offset = (part + core) % 2 * 512
        block = blocks[slot].astype(F32)
        gain = gain_ref[:, pl.ds(pl.multiple_of(offset, 512), 512)]
        scaled = (block * gain).astype(BF16)
        square = block * block
        lanes = (square[:, :128] + square[:, 128:256]) + (square[:, 256:384] + square[:, 384:])
        rows_of = pl.ds(pl.multiple_of(offset, 512), 512)
        return jnp.dot(scaled, weight[rows_of, :], preferred_element_type=F32), lanes

    def core_copy(r):
        return pltpu.make_async_remote_copy(
            src_ref=core_out.at[r],
            dst_ref=core_in.at[r],
            send_sem=core_send.at[r],
            recv_sem=core_recv.at[r],
            device_id=at(y * 2 + 1 - core, x, z),
            device_id_type=MESH,
        )

    def y_copy(r, kinds):
        columns = pl.ds((3 - kinds) * HD, kinds * HD)
        return pltpu.make_async_remote_copy(
            src_ref=y_out.at[r, :, columns],
            dst_ref=y_in.at[r, :, columns],
            send_sem=y_send.at[r],
            recv_sem=y_recv.at[r],
            device_id=at((1 - y) * 2 + core, x, z),
            device_id_type=MESH,
        )

    def write_row(ref, r, row):
        high = row.astype(BF16)
        low = (row - high.astype(F32)).astype(BF16)
        ref[r, 128:144, 0:128] = jnp.zeros((16, 128), BF16)
        ref[r, 128:144, 128:256] = jnp.broadcast_to(high, (16, 128))
        ref[r, 128:144, 256:384] = jnp.broadcast_to(low, (16, 128))

    def read_row(ref, r):
        tail = ref[r, 128:144, 128:384].astype(F32)
        return tail[0:1, 0:128] + tail[0:1, 128:256]

    def core_sum(r):
        core_copy(r).wait_recv()
        total = own[r] + core_in[r, 0:128, :].astype(F32)
        row = own_row[r, 0:1, :] + read_row(core_in, r)
        own[r] = total
        own_row[r] = jnp.broadcast_to(row, (8, 128))
        y_out[r, 0:128, :] = total.astype(BF16)
        write_row(y_out, r, row)

        @pl.when(jnp.logical_and(y == 0, r < 2))
        def _():
            y_copy(r, 2).start()

        @pl.when(jnp.logical_or(jnp.logical_and(y == 0, r >= 2), jnp.logical_and(y == 1, r < 2)))
        def _():
            y_copy(r, 3).start()

    def row_block(i, carry):
        c = nth(i)
        for part in (1, 0):
            slot = c * 2 + part

            @pl.when(level != part)
            def _():
                block_arrival(slot)

            @pl.when(jnp.logical_and(level >= 2, carried(i)))
            def _():
                cross_copy(slot).start()

        first, first_lanes = product(c * 2 + 1, 1)
        second, second_lanes = product(c * 2, 0)
        result = first + second
        own[c] = result[:, :384]
        core_out[c, 0:128, :] = result[:, 384:].astype(BF16)
        row = jnp.sum((first_lanes + second_lanes).T, axis=0, keepdims=True)
        own_row[c] = jnp.broadcast_to(row, (8, 128))
        write_row(core_out, c, row)
        core_copy(c).start()

        @pl.when(i >= 1)
        def _():
            core_sum(nth(i + 3))

        return carry

    lax.fori_loop(0, 4, row_block, 0)
    core_sum(nth(3))

    def turn(vector, r):
        rows_of = pl.ds(pl.multiple_of(r * 128, 128), 128)
        return vector * cos_tab[rows_of, :] + pltpu.roll(vector, HD // 2, 1) * sin_tab[rows_of, :]

    def finish(r):
        row = own_row[r, 0:1, :] + read_row(y_in, r)
        factor = lax.rsqrt(row * (1.0 / 4096.0) + NORM_EPS)
        factor = jnp.broadcast_to(factor, (128, 128)).T

        def whole(kind):
            columns = pl.ds(kind * HD, HD)
            return (own[r, :, columns] + y_in[r, 0:128, columns].astype(F32)) * factor

        rows_of = pl.ds(pl.multiple_of(r * 128, 128), 128)

        @pl.when(r // 2 == y)
        def _():
            query_rows = pl.ds(pl.multiple_of(r % 2 * 128, 128), 128)
            queries[query_rows, :] = turn(whole(0), r).astype(BF16)

        keys[rows_of, :] = turn(whole(1), r).astype(BF16)
        values[rows_of, :] = whole(2).astype(BF16)

    def attend(r, count):
        query = queries[pl.ds(pl.multiple_of(r % 2 * 128, 128), 128), :]
        scores = lax.dot_general(
            query, keys[0:count, :], (((1,), (1,)), ((), ())), preferred_element_type=F32
        ) * (1.0 / math.sqrt(HD))
        place = r * 128 + lax.broadcasted_iota(jnp.int32, (128, count), 0)
        allowed = lax.broadcasted_iota(jnp.int32, (128, count), 1) <= place
        best = jnp.max(jnp.where(allowed, scores, MASKED), axis=1, keepdims=True)
        weights = jnp.where(allowed, jnp.exp(scores - best), 0.0)
        total = jnp.sum(weights, axis=1, keepdims=True)
        out = jnp.dot(weights.astype(BF16), values[0:count, :], preferred_element_type=F32)
        return (out / total).astype(BF16)

    head_copy = pltpu.make_async_remote_copy(
        src_ref=head_out,
        dst_ref=head_in,
        send_sem=head_send,
        recv_sem=head_recv,
        device_id=at(y * 2 + 1 - core, x, z),
        device_id_type=MESH,
    )

    def both_heads(count):
        head_out[...] = attend(y * 2 + 1 - core, count)
        head_copy.start()
        out_ref[:, pl.ds(pl.multiple_of(core * HD, HD), HD)] = attend(ctx, count)

    @pl.when(y == 0)
    def _():
        for r in (0, 1):
            y_copy(r, 3).wait_recv()
            finish(r)
        both_heads(256)

    @pl.when(y == 1)
    def _():
        def arrived(i, carry):
            r = (i + 2 - mine) % 4

            @pl.when(r < 2)
            def _():
                y_copy(r, 2).wait_recv()

            @pl.when(r >= 2)
            def _():
                y_copy(r, 3).wait_recv()

            finish(r)
            return carry

        lax.fori_loop(0, 4, arrived, 0)
        both_heads(512)

    head_copy.wait_recv()
    out_ref[:, pl.ds(pl.multiple_of((1 - core) * HD, HD), HD)] = head_in[...]

    head_copy.wait_send()

    for k in range(4):
        feats_cross(k).wait_send()
        if k > 0:
            feats_copy(k).wait_send()
    for side in (0, 1):

        @pl.when(jnp.logical_not(jnp.logical_and(stays, x == side)))
        def _():
            entry_copy(side).wait_send()

    def drain(i, carry):
        c = nth(i)
        core_copy(c).wait_send()

        @pl.when(level <= 1)
        def _():
            line_copy(c, 1 - level).wait_send()

        @pl.when(jnp.logical_and(level <= 1, carried(i)))
        def _():
            line_copy(c, 3).wait_send()
            line_copy(c, 2).wait_send()

        @pl.when(jnp.logical_and(level >= 2, carried(i)))
        def _():
            cross_copy(c * 2 + 1).wait_send()
            cross_copy(c * 2).wait_send()

        return carry

    lax.fori_loop(0, 4, drain, 0)

    @pl.when(y == 0)
    def _():
        for r in range(4):
            y_copy(r, 2 if r < 2 else 3).wait_send()

    @pl.when(y == 1)
    def _():
        for r in range(2):
            y_copy(r, 3).wait_send()


def fused(
    text_embed, frame_feats, frame_count, proj_weight, norm_gain, q_weight, k_weight, v_weight
):
    cosine, sine = rope_tables(512)
    vmem = pl.BlockSpec(memory_space=pltpu.VMEM)
    hbm = pl.BlockSpec(memory_space=pltpu.MemorySpace.HBM)
    dma = pltpu.SemaphoreType.DMA
    return pl.pallas_call(
        fused_kernel,
        out_shape=jax.ShapeDtypeStruct((128, 256), BF16),
        in_specs=[hbm, hbm, pl.BlockSpec(memory_space=pltpu.SMEM)] + [hbm] * 7,
        out_specs=vmem,
        scratch_shapes=[
            pltpu.VMEM((1024, 512), BF16),
            pltpu.VMEM((1024, 768), BF16),
            pltpu.VMEM((512, HD), F32),
            pltpu.VMEM((512, HD), F32),
            pltpu.VMEM((1024,), BF16),
            pltpu.VMEM((1, 1024), F32),
            pltpu.VMEM((128, 512), BF16),
            pltpu.VMEM((8, 128, 128), BF16),
            pltpu.VMEM((128, 512), F32),
            pltpu.VMEM((128, 512), BF16),
            pltpu.VMEM((8, 128, 512), BF16),
            pltpu.VMEM((4, 128, 384), F32),
            pltpu.VMEM((4, 8, 128), F32),
            pltpu.VMEM((4, 144, 384), BF16),
            pltpu.VMEM((4, 144, 384), BF16),
            pltpu.VMEM((4, 144, 384), BF16),
            pltpu.VMEM((4, 144, 384), BF16),
            pltpu.VMEM((256, HD), BF16),
            pltpu.VMEM((512, HD), BF16),
            pltpu.VMEM((512, HD), BF16),
            pltpu.VMEM((128, HD), BF16),
            pltpu.VMEM((128, HD), BF16),
            dma((12,)),
            dma((8,)),
            dma((8,)),
            dma((2,)),
            dma((16,)),
            dma((8,)),
            dma((8,)),
            dma((4,)),
            dma((4,)),
            dma((4,)),
            dma((4,)),
            dma,
            dma,
        ],
        compiler_params=pltpu.CompilerParams(
            collective_id=0, has_side_effects=True, vmem_limit_bytes=63 * 1024 * 1024
        ),
    )(
        text_embed,
        frame_feats,
        frame_count,
        norm_gain,
        proj_weight,
        q_weight,
        k_weight,
        v_weight,
        jnp.asarray(cosine),
        jnp.asarray(sine),
    )


def solution(mesh):
    small = (mesh.shape["ctx"], mesh.shape["section"], mesh.shape["tp"]) == (4, 2, 4)
    body = fused if small else local
    in_specs = (
        P("ctx", ("section", "tp")),
        P("ctx", ("section", "tp")),
        P("ctx"),
        P(None, ("section", "tp")),
        P(),
        P("ctx", ("section", "tp")),
        P("ctx", ("section", "tp")),
        P("ctx", ("section", "tp")),
    )
    out_specs = P("ctx", ("section", "tp"))
    return jax.shard_map(body, mesh=mesh, in_specs=in_specs, out_specs=out_specs, check_vma=False)
```

```python
import math

import jax
import jax.numpy as jnp
import numpy as np
from jax import lax
from jax.experimental import pallas as pl
from jax.experimental.pallas import tpu as pltpu
from jax.sharding import PartitionSpec as P

HD = 128


ROPE_BASE = 1000000.0
NORM_EPS = 1e-05
MASKED = -1e30


def rotate(values, positions):
    half = values.shape[-1] // 2
    ladder = jnp.arange(half, dtype=jnp.float32) * 2.0 / values.shape[-1]
    freq = ROPE_BASE ** (-ladder)
    angle = positions.astype(jnp.float32)[:, None] * freq[None, :]
    cosine = jnp.cos(angle)[:, None, :]
    sine = jnp.sin(angle)[:, None, :]
    first = values[..., :half]
    second = values[..., half:]
    return jnp.concatenate(
        [first * cosine - second * sine, second * cosine + first * sine], axis=-1
    )


def attend_block(state, key_rows, value_rows, queries, query_pos, scale):
    best, total, accum = state
    rows = key_rows.shape[0]
    heads = queries.shape[1]
    width = queries.shape[2]
    keys_three = key_rows.reshape(rows, heads, width)
    values_three = value_rows.reshape(rows, heads, width)
    scores = (
        jnp.einsum("qhd,khd->hqk", queries, keys_three, preferred_element_type=jnp.float32) * scale
    )
    key_pos = jnp.arange(rows, dtype=jnp.int32)
    allowed = key_pos[None, None, :] <= query_pos[None, :, None]
    block_best = jnp.max(jnp.where(allowed, scores, MASKED), axis=-1)
    new_best = jnp.maximum(best, block_best)
    weights = jnp.where(allowed, jnp.exp(scores - new_best[..., None]), 0.0)
    total = jnp.sum(weights, axis=-1)
    product = jnp.einsum(
        "hqk,khd->hqd",
        weights.astype(jnp.bfloat16),
        values_three,
        preferred_element_type=jnp.float32,
    )
    accum = product
    return (new_best, total, accum)


def local(
    text_embed, frame_feats, frame_count, proj_weight, norm_gain, q_weight, k_weight, v_weight
):
    tok_rows = text_embed.shape[0]
    vision = jnp.dot(
        lax.all_gather(frame_feats, ("section", "tp"), axis=1, tiled=True),
        proj_weight,
        preferred_element_type=jnp.float32,
    )
    offsets = jnp.arange(tok_rows, dtype=jnp.int32)
    is_frame = offsets < frame_count[0]
    joined = jnp.where(is_frame[:, None], vision, text_embed.astype(jnp.float32)).astype(
        jnp.bfloat16
    )
    whole = lax.all_gather(joined, ("section", "tp"), axis=1, tiled=True)
    wide = whole.astype(jnp.float32)
    mean_square = jnp.mean(wide * wide, axis=-1, keepdims=True)
    normed = (wide * lax.rsqrt(mean_square + NORM_EPS) * norm_gain.astype(jnp.float32)).astype(
        jnp.bfloat16
    )
    head_cols = q_weight.shape[1]

    def add_rows(piece):
        return jnp.dot(normed, piece, preferred_element_type=jnp.float32)

    q_full = add_rows(lax.all_gather(q_weight, "ctx", axis=0, tiled=True))
    k_full = add_rows(lax.all_gather(k_weight, "ctx", axis=0, tiled=True))
    v_full = add_rows(lax.all_gather(v_weight, "ctx", axis=0, tiled=True))
    first_pos = lax.axis_index("ctx") * tok_rows
    query_pos = first_pos + offsets
    heads = head_cols // HD
    queries = rotate(q_full.reshape(tok_rows, heads, HD), query_pos).astype(jnp.bfloat16)
    keys = (
        rotate(k_full.reshape(tok_rows, heads, HD), query_pos)
        .astype(jnp.bfloat16)
        .reshape(tok_rows, head_cols)
    )
    values = v_full.astype(jnp.bfloat16)
    scale = 1.0 / math.sqrt(HD)
    initial = (
        jnp.full((heads, tok_rows), MASKED, jnp.float32),
        jnp.zeros((heads, tok_rows), jnp.float32),
        jnp.zeros((heads, tok_rows, HD), jnp.float32),
    )
    state = attend_block(
        initial,
        lax.all_gather(keys, "ctx", axis=0, tiled=True),
        lax.all_gather(values, "ctx", axis=0, tiled=True),
        queries,
        query_pos,
        scale,
    )
    best, total, accum = state
    result = accum / total[..., None]
    return result.transpose(1, 0, 2).reshape(tok_rows, head_cols).astype(jnp.bfloat16)


MESH = pl.DeviceIdType.MESH
F32 = jnp.float32
BF16 = jnp.bfloat16


def rope_tables(tokens):
    half = HD // 2
    freq = ROPE_BASE ** (-(np.arange(half, dtype=np.float64) * 2.0 / HD))
    angle = np.arange(tokens, dtype=np.float64)[:, None] * freq[None, :]
    cosine, sine = np.cos(angle), np.sin(angle)
    return (
        np.concatenate([cosine, cosine], axis=1).astype(np.float32),
        np.concatenate([-sine, sine], axis=1).astype(np.float32),
    )


def fused_kernel(
    text_hbm,
    feats_hbm,
    count_ref,
    gain_hbm,
    proj_hbm,
    q_hbm,
    k_hbm,
    v_hbm,
    cos_hbm,
    sin_hbm,
    out_ref,
    proj,
    weight,
    cos_tab,
    sin_tab,
    gain_raw,
    gain_ref,
    text_ref,
    feats,
    vision,
    joined,
    blocks,
    own,
    own_row,
    core_out,
    core_in,
    y_out,
    y_in,
    queries,
    keys,
    values,
    head_out,
    head_in,
    load_sem,
    feats_send,
    feats_recv,
    entry_send,
    line_send,
    cross_send,
    block_recv,
    core_send,
    core_recv,
    y_send,
    y_recv,
    head_send,
    head_recv,
):
    ctx = lax.axis_index("ctx")
    x = lax.axis_index("section")
    z = lax.axis_index("tp")
    y = ctx // 2
    core = ctx % 2
    g = x * 4 + z

    def at(c, s, t):
        return {"ctx": c, "section": s, "tp": t}

    feats_load = pltpu.make_async_copy(feats_hbm, feats.at[0], load_sem.at[10])
    feats_load.start()
    loads = [
        pltpu.make_async_copy(proj_hbm, proj, load_sem.at[0]),
        pltpu.make_async_copy(text_hbm, text_ref, load_sem.at[11]),
        pltpu.make_async_copy(cos_hbm, cos_tab, load_sem.at[1]),
        pltpu.make_async_copy(sin_hbm, sin_tab, load_sem.at[2]),
        pltpu.make_async_copy(
            gain_hbm.at[pl.ds(pl.multiple_of(ctx * 1024, 1024), 1024)], gain_raw, load_sem.at[9]
        ),
    ]
    for place, head in enumerate((core, 1 - core)):
        for kind, source in enumerate((q_hbm, k_hbm, v_hbm)):
            loads.append(
                pltpu.make_async_copy(
                    source.at[:, pl.ds(pl.multiple_of(head * HD, HD), HD)],
                    weight.at[:, pl.ds((place * 3 + kind) * HD, HD)],
                    load_sem.at[3 + place * 3 + kind],
                )
            )
    for load in loads:
        load.start()

    barrier = pltpu.get_barrier_semaphore()

    def greet_plane(k, carry):
        other = (ctx * 2 + x + k) % 8
        pl.semaphore_signal(
            barrier, inc=1, device_id=at(other // 2, other % 2, z), device_id_type=MESH
        )
        return carry

    lax.fori_loop(1, 8, greet_plane, 0)

    def greet_line(k, carry):
        for side in (0, 1):
            pl.semaphore_signal(
                barrier, inc=1, device_id=at(ctx, side, (z + k) % 4), device_id_type=MESH
            )
        return carry

    lax.fori_loop(1, 4, greet_line, 0)
    feats_load.wait()
    pl.semaphore_wait(barrier, 13)

    def feats_copy(k):
        return pltpu.make_async_remote_copy(
            src_ref=feats.at[0],
            dst_ref=feats.at[k * 2],
            send_sem=feats_send.at[k * 2],
            recv_sem=feats_recv.at[k * 2],
            device_id=at(ctx, x, (z + k) % 4),
            device_id_type=MESH,
        )

    def feats_cross(k):
        return pltpu.make_async_remote_copy(
            src_ref=feats.at[k * 2],
            dst_ref=feats.at[k * 2 + 1],
            send_sem=feats_send.at[k * 2 + 1],
            recv_sem=feats_recv.at[k * 2 + 1],
            device_id=at(ctx, 1 - x, z),
            device_id_type=MESH,
        )

    for k in (1, 3, 2):
        feats_copy(k).start()
    feats_cross(0).start()
    loads[0].wait()
    loads[1].wait()

    def feats_dot(k, side):
        owner = (x * (1 - side) + (1 - x) * side) * 4 + (z + 4 - k) % 4
        rows_of = pl.ds(pl.multiple_of(owner * 128, 128), 128)
        return jnp.dot(feats[k * 2 + side], proj[rows_of, :], preferred_element_type=F32)

    vision[...] = feats_dot(0, 0)
    for k in (1, 3, 2):
        feats_copy(k).wait_recv()
        feats_cross(k).start()
    vision[...] += (feats_dot(1, 0) + feats_dot(3, 0)) + feats_dot(2, 0)
    for k in (0, 1, 3, 2):
        feats_cross(k).wait_recv()
        vision[...] += feats_dot(k, 1)
    rows = lax.broadcasted_iota(jnp.int32, (128, 512), 0)
    mixed = jnp.where(rows < count_ref[0], vision[...], text_ref[...].astype(F32)).astype(BF16)
    joined[...] = mixed

    to_core = z // 2
    to_ctx = x * 2 + to_core
    to_part = z * (1 - to_core) + (3 - z) * to_core

    def entry_copy(side):
        return pltpu.make_async_remote_copy(
            src_ref=joined,
            dst_ref=blocks.at[ctx * 2 + to_part],
            send_sem=entry_send.at[side],
            recv_sem=block_recv.at[ctx * 2 + to_part],
            device_id=at(to_ctx, side, z),
            device_id_type=MESH,
        )

    stays = to_ctx == ctx
    for side in (0, 1):
        here = jnp.logical_and(stays, x == side)

        @pl.when(here)
        def _():
            blocks[ctx * 2 + to_part] = mixed

        @pl.when(jnp.logical_not(here))
        def _():
            entry_copy(side).start()

    level = z * (1 - core) + (3 - z) * core

    parity = (x + y) % 2

    def nth(i):
        return (i + 2 * (1 - y)) % 4

    def carried(i):
        return i % 2 == parity

    def block_arrival(slot):
        pltpu.make_async_copy(blocks.at[slot], blocks.at[slot], block_recv.at[slot]).wait()

    def line_copy(c, to_level):
        slot = c * 2 + level
        return pltpu.make_async_remote_copy(
            src_ref=blocks.at[slot],
            dst_ref=blocks.at[slot],
            send_sem=line_send.at[c * 4 + to_level],
            recv_sem=block_recv.at[slot],
            device_id=at(ctx, x, to_level * (1 - core) + (3 - to_level) * core),
            device_id_type=MESH,
        )

    def cross_copy(slot):
        return pltpu.make_async_remote_copy(
            src_ref=blocks.at[slot],
            dst_ref=blocks.at[slot],
            send_sem=cross_send.at[slot],
            recv_sem=block_recv.at[slot],
            device_id=at(ctx, 1 - x, z),
            device_id_type=MESH,
        )

    @pl.when(level <= 1)
    def _():
        def pass_on(i, carry):
            c = nth(i)
            slot = c * 2 + level
            local_block = jnp.logical_and(c == ctx, x == y)

            @pl.when(jnp.logical_not(local_block))
            def _():
                block_arrival(slot)

            @pl.when(carried(i))
            def _():
                line_copy(c, 3).start()
                line_copy(c, 2).start()

            line_copy(c, 1 - level).start()
            return carry

        lax.fori_loop(0, 4, pass_on, 0)

    for load in loads[2:]:
        load.wait()
    gain_ref[...] = gain_raw[...].astype(F32).reshape(1, 1024)

    def product(slot, part):
        offset = (part + core) % 2 * 512
        block = blocks[slot].astype(F32)
        gain = gain_ref[:, pl.ds(pl.multiple_of(offset, 512), 512)]
        scaled = (block * gain).astype(BF16)
        square = block * block
        lanes = (square[:, :128] + square[:, 128:256]) + (square[:, 256:384] + square[:, 384:])
        rows_of = pl.ds(pl.multiple_of(offset, 512), 512)
        return jnp.dot(scaled, weight[rows_of, :], preferred_element_type=F32), lanes

    def core_copy(r):
        return pltpu.make_async_remote_copy(
            src_ref=core_out.at[r],
            dst_ref=core_in.at[r],
            send_sem=core_send.at[r],
            recv_sem=core_recv.at[r],
            device_id=at(y * 2 + 1 - core, x, z),
            device_id_type=MESH,
        )

    def y_copy(r, kinds):
        columns = pl.ds((3 - kinds) * HD, kinds * HD)
        return pltpu.make_async_remote_copy(
            src_ref=y_out.at[r, :, columns],
            dst_ref=y_in.at[r, :, columns],
            send_sem=y_send.at[r],
            recv_sem=y_recv.at[r],
            device_id=at((1 - y) * 2 + core, x, z),
            device_id_type=MESH,
        )

    def write_row(ref, r, row):
        high = row.astype(BF16)
        low = (row - high.astype(F32)).astype(BF16)
        ref[r, 128:144, 0:128] = jnp.zeros((16, 128), BF16)
        ref[r, 128:144, 128:256] = jnp.broadcast_to(high, (16, 128))
        ref[r, 128:144, 256:384] = jnp.broadcast_to(low, (16, 128))

    def read_row(ref, r):
        tail = ref[r, 128:144, 128:384].astype(F32)
        return tail[0:1, 0:128] + tail[0:1, 128:256]

    def core_sum(r):
        core_copy(r).wait_recv()
        total = own[r] + core_in[r, 0:128, :].astype(F32)
        row = own_row[r, 0:1, :] + read_row(core_in, r)
        own[r] = total
        own_row[r] = jnp.broadcast_to(row, (8, 128))
        y_out[r, 0:128, :] = total.astype(BF16)
        write_row(y_out, r, row)

        @pl.when(jnp.logical_and(y == 0, r < 2))
        def _():
            y_copy(r, 2).start()

        @pl.when(jnp.logical_or(jnp.logical_and(y == 0, r >= 2), jnp.logical_and(y == 1, r < 2)))
        def _():
            y_copy(r, 3).start()

    def row_block(i, carry):
        c = nth(i)
        for part in (1, 0):
            slot = c * 2 + part

            @pl.when(level != part)
            def _():
                block_arrival(slot)

            @pl.when(jnp.logical_and(level >= 2, carried(i)))
            def _():
                cross_copy(slot).start()

        first, first_lanes = product(c * 2 + 1, 1)
        second, second_lanes = product(c * 2, 0)
        result = first + second
        own[c] = result[:, :384]
        core_out[c, 0:128, :] = result[:, 384:].astype(BF16)
        row = jnp.sum((first_lanes + second_lanes).T, axis=0, keepdims=True)
        own_row[c] = jnp.broadcast_to(row, (8, 128))
        write_row(core_out, c, row)
        core_copy(c).start()

        @pl.when(i >= 1)
        def _():
            core_sum(nth(i + 3))

        return carry

    lax.fori_loop(0, 4, row_block, 0)
    core_sum(nth(3))

    def turn(vector, r):
        rows_of = pl.ds(pl.multiple_of(r * 128, 128), 128)
        return vector * cos_tab[rows_of, :] + pltpu.roll(vector, HD // 2, 1) * sin_tab[rows_of, :]

    def finish(r):
        row = own_row[r, 0:1, :] + read_row(y_in, r)
        factor = lax.rsqrt(row * (1.0 / 4096.0) + NORM_EPS)
        factor = jnp.broadcast_to(factor, (128, 128)).T

        def whole(kind):
            columns = pl.ds(kind * HD, HD)
            return (own[r, :, columns] + y_in[r, 0:128, columns].astype(F32)) * factor

        rows_of = pl.ds(pl.multiple_of(r * 128, 128), 128)

        @pl.when(r // 2 == y)
        def _():
            query_rows = pl.ds(pl.multiple_of(r % 2 * 128, 128), 128)
            queries[query_rows, :] = turn(whole(0), r).astype(BF16)

        keys[rows_of, :] = turn(whole(1), r).astype(BF16)
        values[rows_of, :] = whole(2).astype(BF16)

    def attend(r, count):
        query = queries[pl.ds(pl.multiple_of(r % 2 * 128, 128), 128), :]
        scores = lax.dot_general(
            query, keys[0:count, :], (((1,), (1,)), ((), ())), preferred_element_type=F32
        ) * (1.0 / math.sqrt(HD))
        place = r * 128 + lax.broadcasted_iota(jnp.int32, (128, count), 0)
        allowed = lax.broadcasted_iota(jnp.int32, (128, count), 1) <= place
        best = jnp.max(jnp.where(allowed, scores, MASKED), axis=1, keepdims=True)
        weights = jnp.where(allowed, jnp.exp(scores - best), 0.0)
        total = jnp.sum(weights, axis=1, keepdims=True)
        out = jnp.dot(weights.astype(BF16), values[0:count, :], preferred_element_type=F32)
        return (out / total).astype(BF16)

    head_copy = pltpu.make_async_remote_copy(
        src_ref=head_out,
        dst_ref=head_in,
        send_sem=head_send,
        recv_sem=head_recv,
        device_id=at(y * 2 + 1 - core, x, z),
        device_id_type=MESH,
    )

    def both_heads(count):
        head_out[...] = attend(y * 2 + 1 - core, count)
        head_copy.start()
        out_ref[:, pl.ds(pl.multiple_of(core * HD, HD), HD)] = attend(ctx, count)

    @pl.when(y == 0)
    def _():
        for r in (0, 1):
            y_copy(r, 3).wait_recv()
            finish(r)
        both_heads(256)

    @pl.when(y == 1)
    def _():
        def arrived(i, carry):
            r = (i + 2) % 4

            @pl.when(r < 2)
            def _():
                y_copy(r, 2).wait_recv()

            @pl.when(r >= 2)
            def _():
                y_copy(r, 3).wait_recv()

            finish(r)
            return carry

        lax.fori_loop(0, 4, arrived, 0)
        both_heads(512)

    head_copy.wait_recv()
    out_ref[:, pl.ds(pl.multiple_of((1 - core) * HD, HD), HD)] = head_in[...]

    head_copy.wait_send()

    for k in range(4):
        feats_cross(k).wait_send()
        if k > 0:
            feats_copy(k).wait_send()
    for side in (0, 1):

        @pl.when(jnp.logical_not(jnp.logical_and(stays, x == side)))
        def _():
            entry_copy(side).wait_send()

    def drain(i, carry):
        c = nth(i)
        core_copy(c).wait_send()

        @pl.when(level <= 1)
        def _():
            line_copy(c, 1 - level).wait_send()

        @pl.when(jnp.logical_and(level <= 1, carried(i)))
        def _():
            line_copy(c, 3).wait_send()
            line_copy(c, 2).wait_send()

        @pl.when(jnp.logical_and(level >= 2, carried(i)))
        def _():
            cross_copy(c * 2 + 1).wait_send()
            cross_copy(c * 2).wait_send()

        return carry

    lax.fori_loop(0, 4, drain, 0)

    @pl.when(y == 0)
    def _():
        for r in range(4):
            y_copy(r, 2 if r < 2 else 3).wait_send()

    @pl.when(y == 1)
    def _():
        for r in range(2):
            y_copy(r, 3).wait_send()


def fused(
    text_embed, frame_feats, frame_count, proj_weight, norm_gain, q_weight, k_weight, v_weight
):
    cosine, sine = rope_tables(512)
    vmem = pl.BlockSpec(memory_space=pltpu.VMEM)
    hbm = pl.BlockSpec(memory_space=pltpu.MemorySpace.HBM)
    dma = pltpu.SemaphoreType.DMA
    return pl.pallas_call(
        fused_kernel,
        out_shape=jax.ShapeDtypeStruct((128, 256), BF16),
        in_specs=[hbm, hbm, pl.BlockSpec(memory_space=pltpu.SMEM)] + [hbm] * 7,
        out_specs=vmem,
        scratch_shapes=[
            pltpu.VMEM((1024, 512), BF16),
            pltpu.VMEM((1024, 768), BF16),
            pltpu.VMEM((512, HD), F32),
            pltpu.VMEM((512, HD), F32),
            pltpu.VMEM((1024,), BF16),
            pltpu.VMEM((1, 1024), F32),
            pltpu.VMEM((128, 512), BF16),
            pltpu.VMEM((8, 128, 128), BF16),
            pltpu.VMEM((128, 512), F32),
            pltpu.VMEM((128, 512), BF16),
            pltpu.VMEM((8, 128, 512), BF16),
            pltpu.VMEM((4, 128, 384), F32),
            pltpu.VMEM((4, 8, 128), F32),
            pltpu.VMEM((4, 144, 384), BF16),
            pltpu.VMEM((4, 144, 384), BF16),
            pltpu.VMEM((4, 144, 384), BF16),
            pltpu.VMEM((4, 144, 384), BF16),
            pltpu.VMEM((256, HD), BF16),
            pltpu.VMEM((512, HD), BF16),
            pltpu.VMEM((512, HD), BF16),
            pltpu.VMEM((128, HD), BF16),
            pltpu.VMEM((128, HD), BF16),
            dma((12,)),
            dma((8,)),
            dma((8,)),
            dma((2,)),
            dma((16,)),
            dma((8,)),
            dma((8,)),
            dma((4,)),
            dma((4,)),
            dma((4,)),
            dma((4,)),
            dma,
            dma,
        ],
        compiler_params=pltpu.CompilerParams(
            collective_id=0, has_side_effects=True, vmem_limit_bytes=63 * 1024 * 1024
        ),
    )(
        text_embed,
        frame_feats,
        frame_count,
        norm_gain,
        proj_weight,
        q_weight,
        k_weight,
        v_weight,
        jnp.asarray(cosine),
        jnp.asarray(sine),
    )


def solution(mesh):
    small = (mesh.shape["ctx"], mesh.shape["section"], mesh.shape["tp"]) == (4, 2, 4)
    body = fused if small else local
    in_specs = (
        P("ctx", ("section", "tp")),
        P("ctx", ("section", "tp")),
        P("ctx"),
        P(None, ("section", "tp")),
        P(),
        P("ctx", ("section", "tp")),
        P("ctx", ("section", "tp")),
        P("ctx", ("section", "tp")),
    )
    out_specs = P("ctx", ("section", "tp"))
    return jax.shard_map(body, mesh=mesh, in_specs=in_specs, out_specs=out_specs, check_vma=False)
```

```python
import math

import jax
import jax.numpy as jnp
import numpy as np
from jax import lax
from jax.experimental import pallas as pl
from jax.experimental.pallas import tpu as pltpu
from jax.sharding import PartitionSpec as P

HD = 128


ROPE_BASE = 1000000.0
NORM_EPS = 1e-05
MASKED = -1e30


def rotate(values, positions):
    half = values.shape[-1] // 2
    ladder = jnp.arange(half, dtype=jnp.float32) * 2.0 / values.shape[-1]
    freq = ROPE_BASE ** (-ladder)
    angle = positions.astype(jnp.float32)[:, None] * freq[None, :]
    cosine = jnp.cos(angle)[:, None, :]
    sine = jnp.sin(angle)[:, None, :]
    first = values[..., :half]
    second = values[..., half:]
    return jnp.concatenate(
        [first * cosine - second * sine, second * cosine + first * sine], axis=-1
    )


def attend_block(state, key_rows, value_rows, queries, query_pos, scale):
    best, total, accum = state
    rows = key_rows.shape[0]
    heads = queries.shape[1]
    width = queries.shape[2]
    keys_three = key_rows.reshape(rows, heads, width)
    values_three = value_rows.reshape(rows, heads, width)
    scores = (
        jnp.einsum("qhd,khd->hqk", queries, keys_three, preferred_element_type=jnp.float32) * scale
    )
    key_pos = jnp.arange(rows, dtype=jnp.int32)
    allowed = key_pos[None, None, :] <= query_pos[None, :, None]
    block_best = jnp.max(jnp.where(allowed, scores, MASKED), axis=-1)
    new_best = jnp.maximum(best, block_best)
    weights = jnp.where(allowed, jnp.exp(scores - new_best[..., None]), 0.0)
    total = jnp.sum(weights, axis=-1)
    product = jnp.einsum(
        "hqk,khd->hqd",
        weights.astype(jnp.bfloat16),
        values_three,
        preferred_element_type=jnp.float32,
    )
    accum = product
    return (new_best, total, accum)


def local(
    text_embed, frame_feats, frame_count, proj_weight, norm_gain, q_weight, k_weight, v_weight
):
    tok_rows = text_embed.shape[0]
    vision = jnp.dot(
        lax.all_gather(frame_feats, ("section", "tp"), axis=1, tiled=True),
        proj_weight,
        preferred_element_type=jnp.float32,
    )
    offsets = jnp.arange(tok_rows, dtype=jnp.int32)
    is_frame = offsets < frame_count[0]
    joined = jnp.where(is_frame[:, None], vision, text_embed.astype(jnp.float32)).astype(
        jnp.bfloat16
    )
    whole = lax.all_gather(joined, ("section", "tp"), axis=1, tiled=True)
    wide = whole.astype(jnp.float32)
    mean_square = jnp.mean(wide * wide, axis=-1, keepdims=True)
    normed = (wide * lax.rsqrt(mean_square + NORM_EPS) * norm_gain.astype(jnp.float32)).astype(
        jnp.bfloat16
    )
    head_cols = q_weight.shape[1]

    def add_rows(piece):
        return jnp.dot(normed, piece, preferred_element_type=jnp.float32)

    q_full = add_rows(lax.all_gather(q_weight, "ctx", axis=0, tiled=True))
    k_full = add_rows(lax.all_gather(k_weight, "ctx", axis=0, tiled=True))
    v_full = add_rows(lax.all_gather(v_weight, "ctx", axis=0, tiled=True))
    first_pos = lax.axis_index("ctx") * tok_rows
    query_pos = first_pos + offsets
    heads = head_cols // HD
    queries = rotate(q_full.reshape(tok_rows, heads, HD), query_pos).astype(jnp.bfloat16)
    keys = (
        rotate(k_full.reshape(tok_rows, heads, HD), query_pos)
        .astype(jnp.bfloat16)
        .reshape(tok_rows, head_cols)
    )
    values = v_full.astype(jnp.bfloat16)
    scale = 1.0 / math.sqrt(HD)
    initial = (
        jnp.full((heads, tok_rows), MASKED, jnp.float32),
        jnp.zeros((heads, tok_rows), jnp.float32),
        jnp.zeros((heads, tok_rows, HD), jnp.float32),
    )
    state = attend_block(
        initial,
        lax.all_gather(keys, "ctx", axis=0, tiled=True),
        lax.all_gather(values, "ctx", axis=0, tiled=True),
        queries,
        query_pos,
        scale,
    )
    best, total, accum = state
    result = accum / total[..., None]
    return result.transpose(1, 0, 2).reshape(tok_rows, head_cols).astype(jnp.bfloat16)


MESH = pl.DeviceIdType.MESH
F32 = jnp.float32
BF16 = jnp.bfloat16


def rope_tables(tokens):
    half = HD // 2
    freq = ROPE_BASE ** (-(np.arange(half, dtype=np.float64) * 2.0 / HD))
    angle = np.arange(tokens, dtype=np.float64)[:, None] * freq[None, :]
    cosine, sine = np.cos(angle), np.sin(angle)
    return (
        np.concatenate([cosine, cosine], axis=1).astype(np.float32),
        np.concatenate([-sine, sine], axis=1).astype(np.float32),
    )


def fused_kernel(
    text_hbm,
    feats_hbm,
    count_ref,
    gain_hbm,
    proj_hbm,
    q_hbm,
    k_hbm,
    v_hbm,
    cos_hbm,
    sin_hbm,
    out_ref,
    proj,
    weight,
    cos_tab,
    sin_tab,
    gain_raw,
    gain_ref,
    text_ref,
    feats,
    vision,
    joined,
    blocks,
    own,
    own_row,
    core_out,
    core_in,
    y_out,
    y_in,
    queries,
    keys,
    values,
    head_out,
    head_in,
    load_sem,
    feats_send,
    feats_recv,
    entry_send,
    line_send,
    cross_send,
    block_recv,
    core_send,
    core_recv,
    y_send,
    y_recv,
    head_send,
    head_recv,
):
    ctx = lax.axis_index("ctx")
    x = lax.axis_index("section")
    z = lax.axis_index("tp")
    y = ctx // 2
    core = ctx % 2
    g = x * 4 + z

    def at(c, s, t):
        return {"ctx": c, "section": s, "tp": t}

    feats_load = pltpu.make_async_copy(feats_hbm, feats.at[0], load_sem.at[10])
    feats_load.start()
    loads = [
        pltpu.make_async_copy(proj_hbm, proj, load_sem.at[0]),
        pltpu.make_async_copy(text_hbm, text_ref, load_sem.at[11]),
        pltpu.make_async_copy(cos_hbm, cos_tab, load_sem.at[1]),
        pltpu.make_async_copy(sin_hbm, sin_tab, load_sem.at[2]),
        pltpu.make_async_copy(
            gain_hbm.at[pl.ds(pl.multiple_of(ctx * 1024, 1024), 1024)], gain_raw, load_sem.at[9]
        ),
    ]
    for place, head in enumerate((core, 1 - core)):
        for kind, source in enumerate((q_hbm, k_hbm, v_hbm)):
            loads.append(
                pltpu.make_async_copy(
                    source.at[:, pl.ds(pl.multiple_of(head * HD, HD), HD)],
                    weight.at[:, pl.ds((place * 3 + kind) * HD, HD)],
                    load_sem.at[3 + place * 3 + kind],
                )
            )
    for load in loads:
        load.start()

    barrier = pltpu.get_barrier_semaphore()

    def greet_plane(k, carry):
        other = (ctx * 2 + x + k) % 8
        pl.semaphore_signal(
            barrier, inc=1, device_id=at(other // 2, other % 2, z), device_id_type=MESH
        )
        return carry

    lax.fori_loop(1, 8, greet_plane, 0)

    def greet_line(k, carry):
        for side in (0, 1):
            pl.semaphore_signal(
                barrier, inc=1, device_id=at(ctx, side, (z + k) % 4), device_id_type=MESH
            )
        return carry

    lax.fori_loop(1, 4, greet_line, 0)
    feats_load.wait()
    pl.semaphore_wait(barrier, 13)

    def feats_copy(k):
        return pltpu.make_async_remote_copy(
            src_ref=feats.at[0],
            dst_ref=feats.at[k * 2],
            send_sem=feats_send.at[k * 2],
            recv_sem=feats_recv.at[k * 2],
            device_id=at(ctx, x, (z + k) % 4),
            device_id_type=MESH,
        )

    def feats_cross(k):
        return pltpu.make_async_remote_copy(
            src_ref=feats.at[k * 2],
            dst_ref=feats.at[k * 2 + 1],
            send_sem=feats_send.at[k * 2 + 1],
            recv_sem=feats_recv.at[k * 2 + 1],
            device_id=at(ctx, 1 - x, z),
            device_id_type=MESH,
        )

    for k in (1, 3, 2):
        feats_copy(k).start()
    feats_cross(0).start()
    loads[0].wait()
    loads[1].wait()

    def feats_dot(k, side):
        owner = (x * (1 - side) + (1 - x) * side) * 4 + (z + 4 - k) % 4
        rows_of = pl.ds(pl.multiple_of(owner * 128, 128), 128)
        return jnp.dot(feats[k * 2 + side], proj[rows_of, :], preferred_element_type=F32)

    vision[...] = feats_dot(0, 0)
    for k in (1, 3, 2):
        feats_copy(k).wait_recv()
        feats_cross(k).start()
    vision[...] += (feats_dot(1, 0) + feats_dot(3, 0)) + feats_dot(2, 0)
    for k in (0, 1, 3, 2):
        feats_cross(k).wait_recv()
        vision[...] += feats_dot(k, 1)
    rows = lax.broadcasted_iota(jnp.int32, (128, 512), 0)
    mixed = jnp.where(rows < count_ref[0], vision[...], text_ref[...].astype(F32)).astype(BF16)
    joined[...] = mixed

    to_core = z // 2
    to_ctx = x * 2 + to_core
    to_part = z * (1 - to_core) + (3 - z) * to_core

    def entry_copy(side):
        return pltpu.make_async_remote_copy(
            src_ref=joined,
            dst_ref=blocks.at[ctx * 2 + to_part],
            send_sem=entry_send.at[side],
            recv_sem=block_recv.at[ctx * 2 + to_part],
            device_id=at(to_ctx, side, z),
            device_id_type=MESH,
        )

    stays = to_ctx == ctx
    for side in (0, 1):
        here = jnp.logical_and(stays, x == side)

        @pl.when(here)
        def _():
            blocks[ctx * 2 + to_part] = mixed

        @pl.when(jnp.logical_not(here))
        def _():
            entry_copy(side).start()

    level = z * (1 - core) + (3 - z) * core

    parity = (x + y) % 2

    def nth(i):
        return (i + 2 * (1 - y)) % 4

    def carried(i):
        return i % 2 == parity

    def block_arrival(slot):
        pltpu.make_async_copy(blocks.at[slot], blocks.at[slot], block_recv.at[slot]).wait()

    def line_copy(c, to_level):
        slot = c * 2 + level
        return pltpu.make_async_remote_copy(
            src_ref=blocks.at[slot],
            dst_ref=blocks.at[slot],
            send_sem=line_send.at[c * 4 + to_level],
            recv_sem=block_recv.at[slot],
            device_id=at(ctx, x, to_level * (1 - core) + (3 - to_level) * core),
            device_id_type=MESH,
        )

    def cross_copy(slot):
        return pltpu.make_async_remote_copy(
            src_ref=blocks.at[slot],
            dst_ref=blocks.at[slot],
            send_sem=cross_send.at[slot],
            recv_sem=block_recv.at[slot],
            device_id=at(ctx, 1 - x, z),
            device_id_type=MESH,
        )

    @pl.when(level <= 1)
    def _():
        def pass_on(i, carry):
            c = nth(i)
            slot = c * 2 + level
            local_block = jnp.logical_and(c == ctx, x == y)

            @pl.when(jnp.logical_not(local_block))
            def _():
                block_arrival(slot)

            @pl.when(carried(i))
            def _():
                line_copy(c, 3).start()
                line_copy(c, 2).start()

            line_copy(c, 1 - level).start()
            return carry

        lax.fori_loop(0, 4, pass_on, 0)

    for load in loads[2:]:
        load.wait()
    gain_ref[...] = gain_raw[...].astype(F32).reshape(1, 1024)

    def product(slot, part):
        offset = (part + core) % 2 * 512
        block = blocks[slot].astype(F32)
        gain = gain_ref[:, pl.ds(pl.multiple_of(offset, 512), 512)]
        scaled = (block * gain).astype(BF16)
        square = block * block
        lanes = (square[:, :128] + square[:, 128:256]) + (square[:, 256:384] + square[:, 384:])
        rows_of = pl.ds(pl.multiple_of(offset, 512), 512)
        return jnp.dot(scaled, weight[rows_of, :], preferred_element_type=F32), lanes

    def core_copy(r):
        return pltpu.make_async_remote_copy(
            src_ref=core_out.at[r],
            dst_ref=core_in.at[r],
            send_sem=core_send.at[r],
            recv_sem=core_recv.at[r],
            device_id=at(y * 2 + 1 - core, x, z),
            device_id_type=MESH,
        )

    def y_copy(r, kinds):
        columns = pl.ds((3 - kinds) * HD, kinds * HD)
        return pltpu.make_async_remote_copy(
            src_ref=y_out.at[r, :, columns],
            dst_ref=y_in.at[r, :, columns],
            send_sem=y_send.at[r],
            recv_sem=y_recv.at[r],
            device_id=at((1 - y) * 2 + core, x, z),
            device_id_type=MESH,
        )

    def write_row(ref, r, row):
        high = row.astype(BF16)
        low = (row - high.astype(F32)).astype(BF16)
        ref[r, 128:144, 0:128] = jnp.zeros((16, 128), BF16)
        ref[r, 128:144, 128:256] = jnp.broadcast_to(high, (16, 128))
        ref[r, 128:144, 256:384] = jnp.broadcast_to(low, (16, 128))

    def read_row(ref, r):
        tail = ref[r, 128:144, 128:384].astype(F32)
        return tail[0:1, 0:128] + tail[0:1, 128:256]

    def core_sum(r):
        core_copy(r).wait_recv()
        total = own[r] + core_in[r, 0:128, :].astype(F32)
        row = own_row[r, 0:1, :] + read_row(core_in, r)
        own[r] = total
        own_row[r] = jnp.broadcast_to(row, (8, 128))
        y_out[r, 0:128, :] = total.astype(BF16)
        write_row(y_out, r, row)

        @pl.when(jnp.logical_and(y == 0, r < 2))
        def _():
            y_copy(r, 2).start()

        @pl.when(jnp.logical_or(jnp.logical_and(y == 0, r >= 2), jnp.logical_and(y == 1, r < 2)))
        def _():
            y_copy(r, 3).start()

    def row_block(i, carry):
        c = nth(i)

        @pl.when(i >= 1)
        def _():
            core_sum(nth(i + 3))

        @pl.when(jnp.logical_and(level >= 2, i % 2 == 0))
        def _():
            for part in (1, 0):
                slot = nth(i + parity) * 2 + part
                block_arrival(slot)
                cross_copy(slot).start()

        for part in (1, 0):
            by_line = jnp.logical_and(level >= 2, carried(i))

            @pl.when(jnp.logical_not(jnp.logical_or(level == part, by_line)))
            def _():
                block_arrival(c * 2 + part)

        first, first_lanes = product(c * 2 + 1, 1)
        second, second_lanes = product(c * 2, 0)
        result = first + second
        own[c] = result[:, :384]
        core_out[c, 0:128, :] = result[:, 384:].astype(BF16)
        row = jnp.sum((first_lanes + second_lanes).T, axis=0, keepdims=True)
        own_row[c] = jnp.broadcast_to(row, (8, 128))
        write_row(core_out, c, row)
        core_copy(c).start()
        return carry

    lax.fori_loop(0, 4, row_block, 0)
    core_sum(nth(3))

    def turn(vector, r):
        rows_of = pl.ds(pl.multiple_of(r * 128, 128), 128)
        return vector * cos_tab[rows_of, :] + pltpu.roll(vector, HD // 2, 1) * sin_tab[rows_of, :]

    def finish(r):
        row = own_row[r, 0:1, :] + read_row(y_in, r)
        factor = lax.rsqrt(row * (1.0 / 4096.0) + NORM_EPS)
        factor = jnp.broadcast_to(factor, (128, 128)).T

        def whole(kind):
            columns = pl.ds(kind * HD, HD)
            return (own[r, :, columns] + y_in[r, 0:128, columns].astype(F32)) * factor

        rows_of = pl.ds(pl.multiple_of(r * 128, 128), 128)

        @pl.when(r // 2 == y)
        def _():
            query_rows = pl.ds(pl.multiple_of(r % 2 * 128, 128), 128)
            queries[query_rows, :] = turn(whole(0), r).astype(BF16)

        keys[rows_of, :] = turn(whole(1), r).astype(BF16)
        values[rows_of, :] = whole(2).astype(BF16)

    def attend(r, count):
        query = queries[pl.ds(pl.multiple_of(r % 2 * 128, 128), 128), :]
        scores = lax.dot_general(
            query, keys[0:count, :], (((1,), (1,)), ((), ())), preferred_element_type=F32
        ) * (1.0 / math.sqrt(HD))
        place = r * 128 + lax.broadcasted_iota(jnp.int32, (128, count), 0)
        allowed = lax.broadcasted_iota(jnp.int32, (128, count), 1) <= place
        best = jnp.max(jnp.where(allowed, scores, MASKED), axis=1, keepdims=True)
        weights = jnp.where(allowed, jnp.exp(scores - best), 0.0)
        total = jnp.sum(weights, axis=1, keepdims=True)
        out = jnp.dot(weights.astype(BF16), values[0:count, :], preferred_element_type=F32)
        return (out / total).astype(BF16)

    head_copy = pltpu.make_async_remote_copy(
        src_ref=head_out,
        dst_ref=head_in,
        send_sem=head_send,
        recv_sem=head_recv,
        device_id=at(y * 2 + 1 - core, x, z),
        device_id_type=MESH,
    )

    def both_heads(count):
        head_out[...] = attend(y * 2 + 1 - core, count)
        head_copy.start()
        out_ref[:, pl.ds(pl.multiple_of(core * HD, HD), HD)] = attend(ctx, count)

    @pl.when(y == 0)
    def _():
        for r in (0, 1):
            y_copy(r, 3).wait_recv()
            finish(r)
        both_heads(256)

    @pl.when(y == 1)
    def _():
        def arrived(i, carry):
            r = (i + 2) % 4

            @pl.when(r < 2)
            def _():
                y_copy(r, 2).wait_recv()

            @pl.when(r >= 2)
            def _():
                y_copy(r, 3).wait_recv()

            finish(r)
            return carry

        lax.fori_loop(0, 4, arrived, 0)
        both_heads(512)

    head_copy.wait_recv()
    out_ref[:, pl.ds(pl.multiple_of((1 - core) * HD, HD), HD)] = head_in[...]

    head_copy.wait_send()

    for k in range(4):
        feats_cross(k).wait_send()
        if k > 0:
            feats_copy(k).wait_send()
    for side in (0, 1):

        @pl.when(jnp.logical_not(jnp.logical_and(stays, x == side)))
        def _():
            entry_copy(side).wait_send()

    def drain(i, carry):
        c = nth(i)
        core_copy(c).wait_send()

        @pl.when(level <= 1)
        def _():
            line_copy(c, 1 - level).wait_send()

        @pl.when(jnp.logical_and(level <= 1, carried(i)))
        def _():
            line_copy(c, 3).wait_send()
            line_copy(c, 2).wait_send()

        @pl.when(jnp.logical_and(level >= 2, carried(i)))
        def _():
            cross_copy(c * 2 + 1).wait_send()
            cross_copy(c * 2).wait_send()

        return carry

    lax.fori_loop(0, 4, drain, 0)

    @pl.when(y == 0)
    def _():
        for r in range(4):
            y_copy(r, 2 if r < 2 else 3).wait_send()

    @pl.when(y == 1)
    def _():
        for r in range(2):
            y_copy(r, 3).wait_send()


def fused(
    text_embed, frame_feats, frame_count, proj_weight, norm_gain, q_weight, k_weight, v_weight
):
    cosine, sine = rope_tables(512)
    vmem = pl.BlockSpec(memory_space=pltpu.VMEM)
    hbm = pl.BlockSpec(memory_space=pltpu.MemorySpace.HBM)
    dma = pltpu.SemaphoreType.DMA
    return pl.pallas_call(
        fused_kernel,
        out_shape=jax.ShapeDtypeStruct((128, 256), BF16),
        in_specs=[hbm, hbm, pl.BlockSpec(memory_space=pltpu.SMEM)] + [hbm] * 7,
        out_specs=vmem,
        scratch_shapes=[
            pltpu.VMEM((1024, 512), BF16),
            pltpu.VMEM((1024, 768), BF16),
            pltpu.VMEM((512, HD), F32),
            pltpu.VMEM((512, HD), F32),
            pltpu.VMEM((1024,), BF16),
            pltpu.VMEM((1, 1024), F32),
            pltpu.VMEM((128, 512), BF16),
            pltpu.VMEM((8, 128, 128), BF16),
            pltpu.VMEM((128, 512), F32),
            pltpu.VMEM((128, 512), BF16),
            pltpu.VMEM((8, 128, 512), BF16),
            pltpu.VMEM((4, 128, 384), F32),
            pltpu.VMEM((4, 8, 128), F32),
            pltpu.VMEM((4, 144, 384), BF16),
            pltpu.VMEM((4, 144, 384), BF16),
            pltpu.VMEM((4, 144, 384), BF16),
            pltpu.VMEM((4, 144, 384), BF16),
            pltpu.VMEM((256, HD), BF16),
            pltpu.VMEM((512, HD), BF16),
            pltpu.VMEM((512, HD), BF16),
            pltpu.VMEM((128, HD), BF16),
            pltpu.VMEM((128, HD), BF16),
            dma((12,)),
            dma((8,)),
            dma((8,)),
            dma((2,)),
            dma((16,)),
            dma((8,)),
            dma((8,)),
            dma((4,)),
            dma((4,)),
            dma((4,)),
            dma((4,)),
            dma,
            dma,
        ],
        compiler_params=pltpu.CompilerParams(
            collective_id=0, has_side_effects=True, vmem_limit_bytes=63 * 1024 * 1024
        ),
    )(
        text_embed,
        frame_feats,
        frame_count,
        norm_gain,
        proj_weight,
        q_weight,
        k_weight,
        v_weight,
        jnp.asarray(cosine),
        jnp.asarray(sine),
    )


def solution(mesh):
    small = (mesh.shape["ctx"], mesh.shape["section"], mesh.shape["tp"]) == (4, 2, 4)
    body = fused if small else local
    in_specs = (
        P("ctx", ("section", "tp")),
        P("ctx", ("section", "tp")),
        P("ctx"),
        P(None, ("section", "tp")),
        P(),
        P("ctx", ("section", "tp")),
        P("ctx", ("section", "tp")),
        P("ctx", ("section", "tp")),
    )
    out_specs = P("ctx", ("section", "tp"))
    return jax.shard_map(body, mesh=mesh, in_specs=in_specs, out_specs=out_specs, check_vma=False)
```

```python
import math

import jax
import jax.numpy as jnp
import numpy as np
from jax import lax
from jax.experimental import pallas as pl
from jax.experimental.pallas import tpu as pltpu
from jax.sharding import PartitionSpec as P

HD = 128


ROPE_BASE = 1000000.0
NORM_EPS = 1e-05
MASKED = -1e30


def rotate(values, positions):
    half = values.shape[-1] // 2
    ladder = jnp.arange(half, dtype=jnp.float32) * 2.0 / values.shape[-1]
    freq = ROPE_BASE ** (-ladder)
    angle = positions.astype(jnp.float32)[:, None] * freq[None, :]
    cosine = jnp.cos(angle)[:, None, :]
    sine = jnp.sin(angle)[:, None, :]
    first = values[..., :half]
    second = values[..., half:]
    return jnp.concatenate(
        [first * cosine - second * sine, second * cosine + first * sine], axis=-1
    )


def attend_block(state, key_rows, value_rows, queries, query_pos, scale):
    best, total, accum = state
    rows = key_rows.shape[0]
    heads = queries.shape[1]
    width = queries.shape[2]
    keys_three = key_rows.reshape(rows, heads, width)
    values_three = value_rows.reshape(rows, heads, width)
    scores = (
        jnp.einsum("qhd,khd->hqk", queries, keys_three, preferred_element_type=jnp.float32) * scale
    )
    key_pos = jnp.arange(rows, dtype=jnp.int32)
    allowed = key_pos[None, None, :] <= query_pos[None, :, None]
    block_best = jnp.max(jnp.where(allowed, scores, MASKED), axis=-1)
    new_best = jnp.maximum(best, block_best)
    weights = jnp.where(allowed, jnp.exp(scores - new_best[..., None]), 0.0)
    total = jnp.sum(weights, axis=-1)
    product = jnp.einsum(
        "hqk,khd->hqd",
        weights.astype(jnp.bfloat16),
        values_three,
        preferred_element_type=jnp.float32,
    )
    accum = product
    return (new_best, total, accum)


def local(
    text_embed, frame_feats, frame_count, proj_weight, norm_gain, q_weight, k_weight, v_weight
):
    tok_rows = text_embed.shape[0]
    vision = jnp.dot(
        lax.all_gather(frame_feats, ("section", "tp"), axis=1, tiled=True),
        proj_weight,
        preferred_element_type=jnp.float32,
    )
    offsets = jnp.arange(tok_rows, dtype=jnp.int32)
    is_frame = offsets < frame_count[0]
    joined = jnp.where(is_frame[:, None], vision, text_embed.astype(jnp.float32)).astype(
        jnp.bfloat16
    )
    whole = lax.all_gather(joined, ("section", "tp"), axis=1, tiled=True)
    wide = whole.astype(jnp.float32)
    mean_square = jnp.mean(wide * wide, axis=-1, keepdims=True)
    normed = (wide * lax.rsqrt(mean_square + NORM_EPS) * norm_gain.astype(jnp.float32)).astype(
        jnp.bfloat16
    )
    head_cols = q_weight.shape[1]

    def add_rows(piece):
        return jnp.dot(normed, piece, preferred_element_type=jnp.float32)

    q_full = add_rows(lax.all_gather(q_weight, "ctx", axis=0, tiled=True))
    k_full = add_rows(lax.all_gather(k_weight, "ctx", axis=0, tiled=True))
    v_full = add_rows(lax.all_gather(v_weight, "ctx", axis=0, tiled=True))
    first_pos = lax.axis_index("ctx") * tok_rows
    query_pos = first_pos + offsets
    heads = head_cols // HD
    queries = rotate(q_full.reshape(tok_rows, heads, HD), query_pos).astype(jnp.bfloat16)
    keys = (
        rotate(k_full.reshape(tok_rows, heads, HD), query_pos)
        .astype(jnp.bfloat16)
        .reshape(tok_rows, head_cols)
    )
    values = v_full.astype(jnp.bfloat16)
    scale = 1.0 / math.sqrt(HD)
    initial = (
        jnp.full((heads, tok_rows), MASKED, jnp.float32),
        jnp.zeros((heads, tok_rows), jnp.float32),
        jnp.zeros((heads, tok_rows, HD), jnp.float32),
    )
    state = attend_block(
        initial,
        lax.all_gather(keys, "ctx", axis=0, tiled=True),
        lax.all_gather(values, "ctx", axis=0, tiled=True),
        queries,
        query_pos,
        scale,
    )
    best, total, accum = state
    result = accum / total[..., None]
    return result.transpose(1, 0, 2).reshape(tok_rows, head_cols).astype(jnp.bfloat16)


MESH = pl.DeviceIdType.MESH
F32 = jnp.float32
BF16 = jnp.bfloat16


def rope_tables(tokens):
    half = HD // 2
    freq = ROPE_BASE ** (-(np.arange(half, dtype=np.float64) * 2.0 / HD))
    angle = np.arange(tokens, dtype=np.float64)[:, None] * freq[None, :]
    cosine, sine = np.cos(angle), np.sin(angle)
    return (
        np.concatenate([cosine, cosine], axis=1).astype(np.float32),
        np.concatenate([-sine, sine], axis=1).astype(np.float32),
    )


def fused_kernel(
    text_hbm,
    feats_hbm,
    count_ref,
    gain_hbm,
    proj_hbm,
    q_hbm,
    k_hbm,
    v_hbm,
    cos_hbm,
    sin_hbm,
    out_ref,
    proj,
    weight,
    cos_tab,
    sin_tab,
    gain_raw,
    gain_ref,
    text_ref,
    feats,
    vision,
    joined,
    blocks,
    own,
    own_row,
    core_out,
    core_in,
    y_out,
    y_in,
    queries,
    keys,
    values,
    head_out,
    head_in,
    load_sem,
    feats_send,
    feats_recv,
    entry_send,
    line_send,
    cross_send,
    block_recv,
    core_send,
    core_recv,
    y_send,
    y_recv,
    head_send,
    head_recv,
):
    ctx = lax.axis_index("ctx")
    x = lax.axis_index("section")
    z = lax.axis_index("tp")
    y = ctx // 2
    core = ctx % 2
    g = x * 4 + z

    def at(c, s, t):
        return {"ctx": c, "section": s, "tp": t}

    feats_load = pltpu.make_async_copy(feats_hbm, feats.at[0], load_sem.at[10])
    feats_load.start()
    loads = [
        pltpu.make_async_copy(proj_hbm, proj, load_sem.at[0]),
        pltpu.make_async_copy(text_hbm, text_ref, load_sem.at[11]),
        pltpu.make_async_copy(cos_hbm, cos_tab, load_sem.at[1]),
        pltpu.make_async_copy(sin_hbm, sin_tab, load_sem.at[2]),
        pltpu.make_async_copy(
            gain_hbm.at[pl.ds(pl.multiple_of(ctx * 1024, 1024), 1024)], gain_raw, load_sem.at[9]
        ),
    ]
    for place, head in enumerate((core, 1 - core)):
        for kind, source in enumerate((q_hbm, k_hbm, v_hbm)):
            loads.append(
                pltpu.make_async_copy(
                    source.at[:, pl.ds(pl.multiple_of(head * HD, HD), HD)],
                    weight.at[:, pl.ds((place * 3 + kind) * HD, HD)],
                    load_sem.at[3 + place * 3 + kind],
                )
            )
    for load in loads:
        load.start()

    barrier = pltpu.get_barrier_semaphore()

    def greet_plane(k, carry):
        other = (ctx * 2 + x + k) % 8
        pl.semaphore_signal(
            barrier, inc=1, device_id=at(other // 2, other % 2, z), device_id_type=MESH
        )
        return carry

    lax.fori_loop(1, 8, greet_plane, 0)

    def greet_line(k, carry):
        for side in (0, 1):
            pl.semaphore_signal(
                barrier, inc=1, device_id=at(ctx, side, (z + k) % 4), device_id_type=MESH
            )
        return carry

    lax.fori_loop(1, 4, greet_line, 0)
    feats_load.wait()
    pl.semaphore_wait(barrier, 13)

    def feats_copy(k):
        return pltpu.make_async_remote_copy(
            src_ref=feats.at[0],
            dst_ref=feats.at[k * 2],
            send_sem=feats_send.at[k * 2],
            recv_sem=feats_recv.at[k * 2],
            device_id=at(ctx, x, (z + k) % 4),
            device_id_type=MESH,
        )

    def feats_cross(k):
        return pltpu.make_async_remote_copy(
            src_ref=feats.at[k * 2],
            dst_ref=feats.at[k * 2 + 1],
            send_sem=feats_send.at[k * 2 + 1],
            recv_sem=feats_recv.at[k * 2 + 1],
            device_id=at(ctx, 1 - x, z),
            device_id_type=MESH,
        )

    for k in (1, 3, 2):
        feats_copy(k).start()
    feats_cross(0).start()
    loads[0].wait()
    loads[1].wait()

    def feats_dot(k, side):
        owner = (x * (1 - side) + (1 - x) * side) * 4 + (z + 4 - k) % 4
        rows_of = pl.ds(pl.multiple_of(owner * 128, 128), 128)
        return jnp.dot(feats[k * 2 + side], proj[rows_of, :], preferred_element_type=F32)

    vision[...] = feats_dot(0, 0)
    for k in (1, 3, 2):
        feats_copy(k).wait_recv()
        feats_cross(k).start()
    vision[...] += (feats_dot(1, 0) + feats_dot(3, 0)) + feats_dot(2, 0)
    for k in (0, 1, 3, 2):
        feats_cross(k).wait_recv()
        vision[...] += feats_dot(k, 1)
    rows = lax.broadcasted_iota(jnp.int32, (128, 512), 0)
    mixed = jnp.where(rows < count_ref[0], vision[...], text_ref[...].astype(F32)).astype(BF16)
    for half in (0, 1):
        joined[half] = mixed[:, half * 256 : half * 256 + 256]

    to_core = z // 2
    to_ctx = x * 2 + to_core
    to_part = z * (1 - to_core) + (3 - z) * to_core

    def entry_copy(side, half):
        slot = (ctx * 2 + to_part) * 2 + half
        return pltpu.make_async_remote_copy(
            src_ref=joined.at[half],
            dst_ref=blocks.at[slot],
            send_sem=entry_send.at[side * 2 + half],
            recv_sem=block_recv.at[slot],
            device_id=at(to_ctx, side, z),
            device_id_type=MESH,
        )

    stays = to_ctx == ctx
    for side in (0, 1):
        here = jnp.logical_and(stays, x == side)

        @pl.when(here)
        def _():
            for half in (0, 1):
                blocks[(ctx * 2 + to_part) * 2 + half] = joined[half]

        @pl.when(jnp.logical_not(here))
        def _():
            for half in (0, 1):
                entry_copy(side, half).start()

    level = z * (1 - core) + (3 - z) * core

    parity = (x + y) % 2

    def nth(i):
        return (i + 2 * (1 - y)) % 4

    def carried(i):
        return i % 2 == parity

    def block_arrival(slot):
        pltpu.make_async_copy(blocks.at[slot], blocks.at[slot], block_recv.at[slot]).wait()

    def line_copy(c, to_level, half):
        slot = (c * 2 + level) * 2 + half
        return pltpu.make_async_remote_copy(
            src_ref=blocks.at[slot],
            dst_ref=blocks.at[slot],
            send_sem=line_send.at[(c * 4 + to_level) * 2 + half],
            recv_sem=block_recv.at[slot],
            device_id=at(ctx, x, to_level * (1 - core) + (3 - to_level) * core),
            device_id_type=MESH,
        )

    def cross_copy(slot):
        return pltpu.make_async_remote_copy(
            src_ref=blocks.at[slot],
            dst_ref=blocks.at[slot],
            send_sem=cross_send.at[slot],
            recv_sem=block_recv.at[slot],
            device_id=at(ctx, 1 - x, z),
            device_id_type=MESH,
        )

    @pl.when(level <= 1)
    def _():
        def pass_on(i, carry):
            c = nth(i)
            local_block = jnp.logical_and(c == ctx, x == y)
            for half in (0, 1):

                @pl.when(jnp.logical_not(local_block))
                def _():
                    block_arrival((c * 2 + level) * 2 + half)

                @pl.when(carried(i))
                def _():
                    line_copy(c, 3, half).start()
                    line_copy(c, 2, half).start()

                line_copy(c, 1 - level, half).start()

            return carry

        lax.fori_loop(0, 4, pass_on, 0)

    for load in loads[2:]:
        load.wait()
    gain_ref[...] = gain_raw[...].astype(F32).reshape(1, 1024)

    def product(slot, part):
        offset = (part + core) % 2 * 512
        block = jnp.concatenate([blocks[slot * 2], blocks[slot * 2 + 1]], axis=1).astype(F32)
        gain = gain_ref[:, pl.ds(pl.multiple_of(offset, 512), 512)]
        scaled = (block * gain).astype(BF16)
        square = block * block
        lanes = (square[:, :128] + square[:, 128:256]) + (square[:, 256:384] + square[:, 384:])
        rows_of = pl.ds(pl.multiple_of(offset, 512), 512)
        return jnp.dot(scaled, weight[rows_of, :], preferred_element_type=F32), lanes

    def core_copy(r):
        return pltpu.make_async_remote_copy(
            src_ref=core_out.at[r],
            dst_ref=core_in.at[r],
            send_sem=core_send.at[r],
            recv_sem=core_recv.at[r],
            device_id=at(y * 2 + 1 - core, x, z),
            device_id_type=MESH,
        )

    def y_copy(r, kinds):
        columns = pl.ds((3 - kinds) * HD, kinds * HD)
        return pltpu.make_async_remote_copy(
            src_ref=y_out.at[r, :, columns],
            dst_ref=y_in.at[r, :, columns],
            send_sem=y_send.at[r],
            recv_sem=y_recv.at[r],
            device_id=at((1 - y) * 2 + core, x, z),
            device_id_type=MESH,
        )

    def write_row(ref, r, row):
        high = row.astype(BF16)
        low = (row - high.astype(F32)).astype(BF16)
        ref[r, 128:144, 0:128] = jnp.zeros((16, 128), BF16)
        ref[r, 128:144, 128:256] = jnp.broadcast_to(high, (16, 128))
        ref[r, 128:144, 256:384] = jnp.broadcast_to(low, (16, 128))

    def read_row(ref, r):
        tail = ref[r, 128:144, 128:384].astype(F32)
        return tail[0:1, 0:128] + tail[0:1, 128:256]

    def core_sum(r):
        core_copy(r).wait_recv()
        total = own[r] + core_in[r, 0:128, :].astype(F32)
        row = own_row[r, 0:1, :] + read_row(core_in, r)
        own[r] = total
        own_row[r] = jnp.broadcast_to(row, (8, 128))
        y_out[r, 0:128, :] = total.astype(BF16)
        write_row(y_out, r, row)

        @pl.when(jnp.logical_and(y == 0, r < 2))
        def _():
            y_copy(r, 2).start()

        @pl.when(jnp.logical_or(jnp.logical_and(y == 0, r >= 2), jnp.logical_and(y == 1, r < 2)))
        def _():
            y_copy(r, 3).start()

    def row_block(i, carry):
        c = nth(i)

        @pl.when(i >= 1)
        def _():
            core_sum(nth(i + 3))

        @pl.when(jnp.logical_and(level >= 2, i % 2 == 0))
        def _():
            for piece in (2, 3, 0, 1):
                slot = nth(i + parity) * 4 + piece
                block_arrival(slot)
                cross_copy(slot).start()

        for part in (1, 0):
            by_line = jnp.logical_and(level >= 2, carried(i))

            @pl.when(jnp.logical_not(jnp.logical_or(level == part, by_line)))
            def _():
                for half in (0, 1):
                    block_arrival((c * 2 + part) * 2 + half)

        first, first_lanes = product(c * 2 + 1, 1)
        second, second_lanes = product(c * 2, 0)
        result = first + second
        own[c] = result[:, :384]
        core_out[c, 0:128, :] = result[:, 384:].astype(BF16)
        row = jnp.sum((first_lanes + second_lanes).T, axis=0, keepdims=True)
        own_row[c] = jnp.broadcast_to(row, (8, 128))
        write_row(core_out, c, row)
        core_copy(c).start()
        return carry

    lax.fori_loop(0, 4, row_block, 0)
    core_sum(nth(3))

    def turn(vector, r):
        rows_of = pl.ds(pl.multiple_of(r * 128, 128), 128)
        return vector * cos_tab[rows_of, :] + pltpu.roll(vector, HD // 2, 1) * sin_tab[rows_of, :]

    def finish(r):
        row = own_row[r, 0:1, :] + read_row(y_in, r)
        factor = lax.rsqrt(row * (1.0 / 4096.0) + NORM_EPS)
        factor = jnp.broadcast_to(factor, (128, 128)).T

        def whole(kind):
            columns = pl.ds(kind * HD, HD)
            return (own[r, :, columns] + y_in[r, 0:128, columns].astype(F32)) * factor

        rows_of = pl.ds(pl.multiple_of(r * 128, 128), 128)

        @pl.when(r // 2 == y)
        def _():
            query_rows = pl.ds(pl.multiple_of(r % 2 * 128, 128), 128)
            queries[query_rows, :] = turn(whole(0), r).astype(BF16)

        keys[rows_of, :] = turn(whole(1), r).astype(BF16)
        values[rows_of, :] = whole(2).astype(BF16)

    def attend(r, count):
        query = queries[pl.ds(pl.multiple_of(r % 2 * 128, 128), 128), :]
        scores = lax.dot_general(
            query, keys[0:count, :], (((1,), (1,)), ((), ())), preferred_element_type=F32
        ) * (1.0 / math.sqrt(HD))
        place = r * 128 + lax.broadcasted_iota(jnp.int32, (128, count), 0)
        allowed = lax.broadcasted_iota(jnp.int32, (128, count), 1) <= place
        best = jnp.max(jnp.where(allowed, scores, MASKED), axis=1, keepdims=True)
        weights = jnp.where(allowed, jnp.exp(scores - best), 0.0)
        total = jnp.sum(weights, axis=1, keepdims=True)
        out = jnp.dot(weights.astype(BF16), values[0:count, :], preferred_element_type=F32)
        return (out / total).astype(BF16)

    head_copy = pltpu.make_async_remote_copy(
        src_ref=head_out,
        dst_ref=head_in,
        send_sem=head_send,
        recv_sem=head_recv,
        device_id=at(y * 2 + 1 - core, x, z),
        device_id_type=MESH,
    )

    def both_heads(count):
        head_out[...] = attend(y * 2 + 1 - core, count)
        head_copy.start()
        out_ref[:, pl.ds(pl.multiple_of(core * HD, HD), HD)] = attend(ctx, count).astype(F32)

    @pl.when(y == 0)
    def _():
        for r in (0, 1):
            y_copy(r, 3).wait_recv()
            finish(r)
        both_heads(256)

    @pl.when(y == 1)
    def _():
        def arrived(i, carry):
            r = (i + 2) % 4

            @pl.when(r < 2)
            def _():
                y_copy(r, 2).wait_recv()

            @pl.when(r >= 2)
            def _():
                y_copy(r, 3).wait_recv()

            finish(r)
            return carry

        lax.fori_loop(0, 4, arrived, 0)
        both_heads(512)

    head_copy.wait_recv()
    out_ref[:, pl.ds(pl.multiple_of((1 - core) * HD, HD), HD)] = head_in[...].astype(F32)

    head_copy.wait_send()

    for k in range(4):
        feats_cross(k).wait_send()
        if k > 0:
            feats_copy(k).wait_send()
    for side in (0, 1):

        @pl.when(jnp.logical_not(jnp.logical_and(stays, x == side)))
        def _():
            for half in (0, 1):
                entry_copy(side, half).wait_send()

    def drain(i, carry):
        c = nth(i)
        core_copy(c).wait_send()

        @pl.when(level <= 1)
        def _():
            for half in (0, 1):
                line_copy(c, 1 - level, half).wait_send()

        @pl.when(jnp.logical_and(level <= 1, carried(i)))
        def _():
            for half in (0, 1):
                line_copy(c, 3, half).wait_send()
                line_copy(c, 2, half).wait_send()

        @pl.when(jnp.logical_and(level >= 2, carried(i)))
        def _():
            for piece in range(4):
                cross_copy(c * 4 + piece).wait_send()

        return carry

    lax.fori_loop(0, 4, drain, 0)

    @pl.when(y == 0)
    def _():
        for r in range(4):
            y_copy(r, 2 if r < 2 else 3).wait_send()

    @pl.when(y == 1)
    def _():
        for r in range(2):
            y_copy(r, 3).wait_send()


def fused(
    text_embed, frame_feats, frame_count, proj_weight, norm_gain, q_weight, k_weight, v_weight
):
    cosine, sine = rope_tables(512)
    vmem = pl.BlockSpec(memory_space=pltpu.VMEM)
    hbm = pl.BlockSpec(memory_space=pltpu.MemorySpace.HBM)
    dma = pltpu.SemaphoreType.DMA
    return pl.pallas_call(
        fused_kernel,
        out_shape=jax.ShapeDtypeStruct((128, 256), F32),
        in_specs=[hbm, hbm, pl.BlockSpec(memory_space=pltpu.SMEM)] + [hbm] * 7,
        out_specs=vmem,
        scratch_shapes=[
            pltpu.VMEM((1024, 512), BF16),
            pltpu.VMEM((1024, 768), BF16),
            pltpu.VMEM((512, HD), F32),
            pltpu.VMEM((512, HD), F32),
            pltpu.VMEM((1024,), BF16),
            pltpu.VMEM((1, 1024), F32),
            pltpu.VMEM((128, 512), BF16),
            pltpu.VMEM((8, 128, 128), BF16),
            pltpu.VMEM((128, 512), F32),
            pltpu.VMEM((2, 128, 256), BF16),
            pltpu.VMEM((16, 128, 256), BF16),
            pltpu.VMEM((4, 128, 384), F32),
            pltpu.VMEM((4, 8, 128), F32),
            pltpu.VMEM((4, 144, 384), BF16),
            pltpu.VMEM((4, 144, 384), BF16),
            pltpu.VMEM((4, 144, 384), BF16),
            pltpu.VMEM((4, 144, 384), BF16),
            pltpu.VMEM((256, HD), BF16),
            pltpu.VMEM((512, HD), BF16),
            pltpu.VMEM((512, HD), BF16),
            pltpu.VMEM((128, HD), BF16),
            pltpu.VMEM((128, HD), BF16),
            dma((12,)),
            dma((8,)),
            dma((8,)),
            dma((4,)),
            dma((32,)),
            dma((16,)),
            dma((16,)),
            dma((4,)),
            dma((4,)),
            dma((4,)),
            dma((4,)),
            dma,
            dma,
        ],
        compiler_params=pltpu.CompilerParams(
            collective_id=0, has_side_effects=True, vmem_limit_bytes=63 * 1024 * 1024
        ),
    )(
        text_embed,
        frame_feats,
        frame_count,
        norm_gain,
        proj_weight,
        q_weight,
        k_weight,
        v_weight,
        jnp.asarray(cosine),
        jnp.asarray(sine),
    ).astype(BF16)


def solution(mesh):
    small = (mesh.shape["ctx"], mesh.shape["section"], mesh.shape["tp"]) == (4, 2, 4)
    body = fused if small else local
    in_specs = (
        P("ctx", ("section", "tp")),
        P("ctx", ("section", "tp")),
        P("ctx"),
        P(None, ("section", "tp")),
        P(),
        P("ctx", ("section", "tp")),
        P("ctx", ("section", "tp")),
        P("ctx", ("section", "tp")),
    )
    out_specs = P("ctx", ("section", "tp"))
    return jax.shard_map(body, mesh=mesh, in_specs=in_specs, out_specs=out_specs, check_vma=False)
```

```python
import math

import jax
import jax.numpy as jnp
import numpy as np
from jax import lax
from jax.experimental import pallas as pl
from jax.experimental.pallas import tpu as pltpu
from jax.sharding import PartitionSpec as P

HD = 128


ROPE_BASE = 1000000.0
NORM_EPS = 1e-05
MASKED = -1e30


def rotate(values, positions):
    half = values.shape[-1] // 2
    ladder = jnp.arange(half, dtype=jnp.float32) * 2.0 / values.shape[-1]
    freq = ROPE_BASE ** (-ladder)
    angle = positions.astype(jnp.float32)[:, None] * freq[None, :]
    cosine = jnp.cos(angle)[:, None, :]
    sine = jnp.sin(angle)[:, None, :]
    first = values[..., :half]
    second = values[..., half:]
    return jnp.concatenate(
        [first * cosine - second * sine, second * cosine + first * sine], axis=-1
    )


def attend_block(state, key_rows, value_rows, queries, query_pos, scale):
    best, total, accum = state
    rows = key_rows.shape[0]
    heads = queries.shape[1]
    width = queries.shape[2]
    keys_three = key_rows.reshape(rows, heads, width)
    values_three = value_rows.reshape(rows, heads, width)
    scores = (
        jnp.einsum("qhd,khd->hqk", queries, keys_three, preferred_element_type=jnp.float32) * scale
    )
    key_pos = jnp.arange(rows, dtype=jnp.int32)
    allowed = key_pos[None, None, :] <= query_pos[None, :, None]
    block_best = jnp.max(jnp.where(allowed, scores, MASKED), axis=-1)
    new_best = jnp.maximum(best, block_best)
    weights = jnp.where(allowed, jnp.exp(scores - new_best[..., None]), 0.0)
    total = jnp.sum(weights, axis=-1)
    product = jnp.einsum(
        "hqk,khd->hqd",
        weights.astype(jnp.bfloat16),
        values_three,
        preferred_element_type=jnp.float32,
    )
    accum = product
    return (new_best, total, accum)


def local(
    text_embed, frame_feats, frame_count, proj_weight, norm_gain, q_weight, k_weight, v_weight
):
    tok_rows = text_embed.shape[0]
    vision = jnp.dot(
        lax.all_gather(frame_feats, ("section", "tp"), axis=1, tiled=True),
        proj_weight,
        preferred_element_type=jnp.float32,
    )
    offsets = jnp.arange(tok_rows, dtype=jnp.int32)
    is_frame = offsets < frame_count[0]
    joined = jnp.where(is_frame[:, None], vision, text_embed.astype(jnp.float32)).astype(
        jnp.bfloat16
    )
    whole = lax.all_gather(joined, ("section", "tp"), axis=1, tiled=True)
    wide = whole.astype(jnp.float32)
    mean_square = jnp.mean(wide * wide, axis=-1, keepdims=True)
    normed = (wide * lax.rsqrt(mean_square + NORM_EPS) * norm_gain.astype(jnp.float32)).astype(
        jnp.bfloat16
    )
    head_cols = q_weight.shape[1]

    def add_rows(piece):
        return jnp.dot(normed, piece, preferred_element_type=jnp.float32)

    q_full = add_rows(lax.all_gather(q_weight, "ctx", axis=0, tiled=True))
    k_full = add_rows(lax.all_gather(k_weight, "ctx", axis=0, tiled=True))
    v_full = add_rows(lax.all_gather(v_weight, "ctx", axis=0, tiled=True))
    first_pos = lax.axis_index("ctx") * tok_rows
    query_pos = first_pos + offsets
    heads = head_cols // HD
    queries = rotate(q_full.reshape(tok_rows, heads, HD), query_pos).astype(jnp.bfloat16)
    keys = (
        rotate(k_full.reshape(tok_rows, heads, HD), query_pos)
        .astype(jnp.bfloat16)
        .reshape(tok_rows, head_cols)
    )
    values = v_full.astype(jnp.bfloat16)
    scale = 1.0 / math.sqrt(HD)
    initial = (
        jnp.full((heads, tok_rows), MASKED, jnp.float32),
        jnp.zeros((heads, tok_rows), jnp.float32),
        jnp.zeros((heads, tok_rows, HD), jnp.float32),
    )
    state = attend_block(
        initial,
        lax.all_gather(keys, "ctx", axis=0, tiled=True),
        lax.all_gather(values, "ctx", axis=0, tiled=True),
        queries,
        query_pos,
        scale,
    )
    best, total, accum = state
    result = accum / total[..., None]
    return result.transpose(1, 0, 2).reshape(tok_rows, head_cols).astype(jnp.bfloat16)


MESH = pl.DeviceIdType.MESH
F32 = jnp.float32
BF16 = jnp.bfloat16


def rope_tables(tokens):
    half = HD // 2
    freq = ROPE_BASE ** (-(np.arange(half, dtype=np.float64) * 2.0 / HD))
    angle = np.arange(tokens, dtype=np.float64)[:, None] * freq[None, :]
    cosine, sine = np.cos(angle), np.sin(angle)
    return (
        np.concatenate([cosine, cosine], axis=1).astype(np.float32),
        np.concatenate([-sine, sine], axis=1).astype(np.float32),
    )


def fused_kernel(
    text_hbm,
    feats_hbm,
    count_ref,
    gain_hbm,
    proj_hbm,
    q_hbm,
    k_hbm,
    v_hbm,
    cos_hbm,
    sin_hbm,
    out_ref,
    proj,
    weight,
    cos_tab,
    sin_tab,
    gain_raw,
    gain_ref,
    text_ref,
    feats,
    vision,
    joined,
    blocks,
    own,
    own_row,
    core_out,
    core_in,
    y_out,
    y_in,
    queries,
    keys,
    values,
    accum,
    bests,
    totals,
    head_out,
    head_in,
    load_sem,
    feats_send,
    feats_recv,
    entry_send,
    line_send,
    cross_send,
    block_recv,
    core_send,
    core_recv,
    y_send,
    y_recv,
    head_send,
    head_recv,
):
    ctx = lax.axis_index("ctx")
    x = lax.axis_index("section")
    z = lax.axis_index("tp")
    y = ctx // 2
    core = ctx % 2
    g = x * 4 + z

    def at(c, s, t):
        return {"ctx": c, "section": s, "tp": t}

    feats_load = pltpu.make_async_copy(feats_hbm, feats.at[0], load_sem.at[10])
    feats_load.start()
    loads = [
        pltpu.make_async_copy(proj_hbm, proj, load_sem.at[0]),
        pltpu.make_async_copy(text_hbm, text_ref, load_sem.at[11]),
        pltpu.make_async_copy(cos_hbm, cos_tab, load_sem.at[1]),
        pltpu.make_async_copy(sin_hbm, sin_tab, load_sem.at[2]),
        pltpu.make_async_copy(
            gain_hbm.at[pl.ds(pl.multiple_of(ctx * 1024, 1024), 1024)], gain_raw, load_sem.at[9]
        ),
    ]
    for place, head in enumerate((core, 1 - core)):
        for kind, source in enumerate((q_hbm, k_hbm, v_hbm)):
            loads.append(
                pltpu.make_async_copy(
                    source.at[:, pl.ds(pl.multiple_of(head * HD, HD), HD)],
                    weight.at[:, pl.ds((place * 3 + kind) * HD, HD)],
                    load_sem.at[3 + place * 3 + kind],
                )
            )
    for load in loads:
        load.start()

    barrier = pltpu.get_barrier_semaphore()

    def greet_plane(k, carry):
        other = (ctx * 2 + x + k) % 8
        pl.semaphore_signal(
            barrier, inc=1, device_id=at(other // 2, other % 2, z), device_id_type=MESH
        )
        return carry

    lax.fori_loop(1, 8, greet_plane, 0)

    def greet_line(k, carry):
        for side in (0, 1):
            pl.semaphore_signal(
                barrier, inc=1, device_id=at(ctx, side, (z + k) % 4), device_id_type=MESH
            )
        return carry

    lax.fori_loop(1, 4, greet_line, 0)
    feats_load.wait()
    pl.semaphore_wait(barrier, 13)

    def feats_copy(k):
        return pltpu.make_async_remote_copy(
            src_ref=feats.at[0],
            dst_ref=feats.at[k * 2],
            send_sem=feats_send.at[k * 2],
            recv_sem=feats_recv.at[k * 2],
            device_id=at(ctx, x, (z + k) % 4),
            device_id_type=MESH,
        )

    def feats_cross(k):
        return pltpu.make_async_remote_copy(
            src_ref=feats.at[k * 2],
            dst_ref=feats.at[k * 2 + 1],
            send_sem=feats_send.at[k * 2 + 1],
            recv_sem=feats_recv.at[k * 2 + 1],
            device_id=at(ctx, 1 - x, z),
            device_id_type=MESH,
        )

    for k in (1, 3, 2):
        feats_copy(k).start()
    feats_cross(0).start()
    loads[0].wait()
    loads[1].wait()

    def feats_dot(k, side):
        owner = (x * (1 - side) + (1 - x) * side) * 4 + (z + 4 - k) % 4
        rows_of = pl.ds(pl.multiple_of(owner * 128, 128), 128)
        return jnp.dot(feats[k * 2 + side], proj[rows_of, :], preferred_element_type=F32)

    vision[...] = feats_dot(0, 0)
    for k in (1, 3, 2):
        feats_copy(k).wait_recv()
        feats_cross(k).start()
    vision[...] += (feats_dot(1, 0) + feats_dot(3, 0)) + feats_dot(2, 0)
    for k in (0, 1, 3, 2):
        feats_cross(k).wait_recv()
        vision[...] += feats_dot(k, 1)
    rows = lax.broadcasted_iota(jnp.int32, (128, 512), 0)
    mixed = jnp.where(rows < count_ref[0], vision[...], text_ref[...].astype(F32)).astype(BF16)
    for half in (0, 1):
        joined[half] = mixed[:, half * 256 : half * 256 + 256]

    to_core = z // 2
    to_ctx = x * 2 + to_core
    to_part = z * (1 - to_core) + (3 - z) * to_core

    def entry_copy(side, half):
        slot = (ctx * 2 + to_part) * 2 + half
        return pltpu.make_async_remote_copy(
            src_ref=joined.at[half],
            dst_ref=blocks.at[slot],
            send_sem=entry_send.at[side * 2 + half],
            recv_sem=block_recv.at[slot],
            device_id=at(to_ctx, side, z),
            device_id_type=MESH,
        )

    stays = to_ctx == ctx
    for side in (0, 1):
        here = jnp.logical_and(stays, x == side)

        @pl.when(here)
        def _():
            for half in (0, 1):
                blocks[(ctx * 2 + to_part) * 2 + half] = joined[half]

        @pl.when(jnp.logical_not(here))
        def _():
            for half in (0, 1):
                entry_copy(side, half).start()

    level = z * (1 - core) + (3 - z) * core

    parity = (x + y) % 2

    def nth(i):
        return (i + 2 * (1 - y)) % 4

    def carried(i):
        return i % 2 == parity

    def block_arrival(slot):
        pltpu.make_async_copy(blocks.at[slot], blocks.at[slot], block_recv.at[slot]).wait()

    def line_copy(c, to_level, half):
        slot = (c * 2 + level) * 2 + half
        return pltpu.make_async_remote_copy(
            src_ref=blocks.at[slot],
            dst_ref=blocks.at[slot],
            send_sem=line_send.at[(c * 4 + to_level) * 2 + half],
            recv_sem=block_recv.at[slot],
            device_id=at(ctx, x, to_level * (1 - core) + (3 - to_level) * core),
            device_id_type=MESH,
        )

    def cross_copy(slot):
        return pltpu.make_async_remote_copy(
            src_ref=blocks.at[slot],
            dst_ref=blocks.at[slot],
            send_sem=cross_send.at[slot],
            recv_sem=block_recv.at[slot],
            device_id=at(ctx, 1 - x, z),
            device_id_type=MESH,
        )

    @pl.when(level <= 1)
    def _():
        def pass_on(i, carry):
            c = nth(i)
            local_block = jnp.logical_and(c == ctx, x == y)
            for half in (0, 1):

                @pl.when(jnp.logical_not(local_block))
                def _():
                    block_arrival((c * 2 + level) * 2 + half)

                @pl.when(carried(i))
                def _():
                    line_copy(c, 3, half).start()
                    line_copy(c, 2, half).start()

                line_copy(c, 1 - level, half).start()

            return carry

        lax.fori_loop(0, 4, pass_on, 0)

    for load in loads[2:]:
        load.wait()
    gain_ref[...] = gain_raw[...].astype(F32).reshape(1, 1024)

    def product(slot, part):
        offset = (part + core) % 2 * 512
        block = jnp.concatenate([blocks[slot * 2], blocks[slot * 2 + 1]], axis=1).astype(F32)
        gain = gain_ref[:, pl.ds(pl.multiple_of(offset, 512), 512)]
        scaled = (block * gain).astype(BF16)
        square = block * block
        lanes = (square[:, :128] + square[:, 128:256]) + (square[:, 256:384] + square[:, 384:])
        rows_of = pl.ds(pl.multiple_of(offset, 512), 512)
        return jnp.dot(scaled, weight[rows_of, :], preferred_element_type=F32), lanes

    def core_copy(r):
        return pltpu.make_async_remote_copy(
            src_ref=core_out.at[r],
            dst_ref=core_in.at[r],
            send_sem=core_send.at[r],
            recv_sem=core_recv.at[r],
            device_id=at(y * 2 + 1 - core, x, z),
            device_id_type=MESH,
        )

    def y_copy(r, kinds):
        columns = pl.ds((3 - kinds) * HD, kinds * HD)
        return pltpu.make_async_remote_copy(
            src_ref=y_out.at[r, :, columns],
            dst_ref=y_in.at[r, :, columns],
            send_sem=y_send.at[r],
            recv_sem=y_recv.at[r],
            device_id=at((1 - y) * 2 + core, x, z),
            device_id_type=MESH,
        )

    def write_row(ref, r, row):
        high = row.astype(BF16)
        low = (row - high.astype(F32)).astype(BF16)
        ref[r, 128:144, 0:128] = jnp.zeros((16, 128), BF16)
        ref[r, 128:144, 128:256] = jnp.broadcast_to(high, (16, 128))
        ref[r, 128:144, 256:384] = jnp.broadcast_to(low, (16, 128))

    def read_row(ref, r):
        tail = ref[r, 128:144, 128:384].astype(F32)
        return tail[0:1, 0:128] + tail[0:1, 128:256]

    def core_sum(r):
        core_copy(r).wait_recv()
        total = own[r] + core_in[r, 0:128, :].astype(F32)
        row = own_row[r, 0:1, :] + read_row(core_in, r)
        own[r] = total
        own_row[r] = jnp.broadcast_to(row, (8, 128))
        y_out[r, 0:128, :] = total.astype(BF16)
        write_row(y_out, r, row)

        @pl.when(jnp.logical_and(y == 0, r < 2))
        def _():
            y_copy(r, 2).start()

        @pl.when(jnp.logical_or(jnp.logical_and(y == 0, r >= 2), jnp.logical_and(y == 1, r < 2)))
        def _():
            y_copy(r, 3).start()

    def row_block(i, carry):
        c = nth(i)

        @pl.when(i >= 1)
        def _():
            core_sum(nth(i + 3))

        @pl.when(jnp.logical_and(level >= 2, i % 2 == 0))
        def _():
            for piece in (2, 3, 0, 1):
                slot = nth(i + parity) * 4 + piece
                block_arrival(slot)
                cross_copy(slot).start()

        for part in (1, 0):
            by_line = jnp.logical_and(level >= 2, carried(i))

            @pl.when(jnp.logical_not(jnp.logical_or(level == part, by_line)))
            def _():
                for half in (0, 1):
                    block_arrival((c * 2 + part) * 2 + half)

        first, first_lanes = product(c * 2 + 1, 1)
        second, second_lanes = product(c * 2, 0)
        result = first + second
        own[c] = result[:, :384]
        core_out[c, 0:128, :] = result[:, 384:].astype(BF16)
        row = jnp.sum((first_lanes + second_lanes).T, axis=0, keepdims=True)
        own_row[c] = jnp.broadcast_to(row, (8, 128))
        write_row(core_out, c, row)
        core_copy(c).start()
        return carry

    lax.fori_loop(0, 4, row_block, 0)
    core_sum(nth(3))

    def turn(vector, r):
        rows_of = pl.ds(pl.multiple_of(r * 128, 128), 128)
        return vector * cos_tab[rows_of, :] + pltpu.roll(vector, HD // 2, 1) * sin_tab[rows_of, :]

    def finish(r):
        row = own_row[r, 0:1, :] + read_row(y_in, r)
        factor = lax.rsqrt(row * (1.0 / 4096.0) + NORM_EPS)
        factor = jnp.broadcast_to(factor, (128, 128)).T

        def whole(kind):
            columns = pl.ds(kind * HD, HD)
            return (own[r, :, columns] + y_in[r, 0:128, columns].astype(F32)) * factor

        rows_of = pl.ds(pl.multiple_of(r * 128, 128), 128)

        @pl.when(r // 2 == y)
        def _():
            query_rows = pl.ds(pl.multiple_of(r % 2 * 128, 128), 128)
            queries[query_rows, :] = turn(whole(0), r).astype(BF16)

        keys[rows_of, :] = turn(whole(1), r).astype(BF16)
        values[rows_of, :] = whole(2).astype(BF16)

    def attend(r, count):
        query = queries[pl.ds(pl.multiple_of(r % 2 * 128, 128), 128), :]
        scores = lax.dot_general(
            query, keys[0:count, :], (((1,), (1,)), ((), ())), preferred_element_type=F32
        ) * (1.0 / math.sqrt(HD))
        place = r * 128 + lax.broadcasted_iota(jnp.int32, (128, count), 0)
        allowed = lax.broadcasted_iota(jnp.int32, (128, count), 1) <= place
        best = jnp.max(jnp.where(allowed, scores, MASKED), axis=1, keepdims=True)
        weights = jnp.where(allowed, jnp.exp(scores - best), 0.0)
        total = jnp.sum(weights, axis=1, keepdims=True)
        out = jnp.dot(weights.astype(BF16), values[0:count, :], preferred_element_type=F32)
        return (out / total).astype(BF16)

    def query_scores(part, start, count):
        query = queries[pl.ds(pl.multiple_of(part * 128, 128), 128), :]
        return lax.dot_general(
            query,
            keys[start : start + count, :],
            (((1,), (1,)), ((), ())),
            preferred_element_type=F32,
        ) * (1.0 / math.sqrt(HD))

    def early(part, carry):
        far = query_scores(part, 0, 128)
        near = query_scores(part, 256, 256)
        place = part * 128 + lax.broadcasted_iota(jnp.int32, (128, 256), 0)
        allowed = lax.broadcasted_iota(jnp.int32, (128, 256), 1) <= place
        best = jnp.maximum(
            jnp.max(far, axis=1, keepdims=True),
            jnp.max(jnp.where(allowed, near, MASKED), axis=1, keepdims=True),
        )
        far = jnp.exp(far - best)
        near = jnp.where(allowed, jnp.exp(near - best), 0.0)
        total = jnp.sum(far, axis=1, keepdims=True) + jnp.sum(near, axis=1, keepdims=True)
        accum[part] = jnp.dot(
            far.astype(BF16), values[0:128, :], preferred_element_type=F32
        ) + jnp.dot(near.astype(BF16), values[256:512, :], preferred_element_type=F32)
        bests[part] = jnp.broadcast_to(best, (128, HD))
        totals[part] = jnp.broadcast_to(total, (128, HD))
        return carry

    def late(part):
        scores = query_scores(part, 128, 128)
        best = jnp.maximum(bests[part], jnp.max(scores, axis=1, keepdims=True))
        weights = jnp.exp(scores - best)
        shrink = jnp.exp(bests[part] - best)
        total = totals[part] * shrink + jnp.sum(weights, axis=1, keepdims=True)
        out = accum[part] * shrink + jnp.dot(
            weights.astype(BF16), values[128:256, :], preferred_element_type=F32
        )
        return (out / total).astype(BF16)

    head_copy = pltpu.make_async_remote_copy(
        src_ref=head_out,
        dst_ref=head_in,
        send_sem=head_send,
        recv_sem=head_recv,
        device_id=at(y * 2 + 1 - core, x, z),
        device_id_type=MESH,
    )

    def both_heads(count):
        head_out[...] = attend(y * 2 + 1 - core, count)
        head_copy.start()
        out_ref[:, pl.ds(pl.multiple_of(core * HD, HD), HD)] = attend(ctx, count)

    @pl.when(y == 0)
    def _():
        for r in (0, 1):
            y_copy(r, 3).wait_recv()
            finish(r)
        both_heads(256)

    @pl.when(y == 1)
    def _():
        def arrived(i, carry):
            r = (i + 2) % 4

            @pl.when(r < 2)
            def _():
                y_copy(r, 2).wait_recv()

            @pl.when(r >= 2)
            def _():
                y_copy(r, 3).wait_recv()

            finish(r)
            return carry

        lax.fori_loop(0, 3, arrived, 0)
        lax.fori_loop(0, 2, early, 0)
        arrived(3, 0)
        head_out[...] = late(1 - core)
        head_copy.start()
        out_ref[:, pl.ds(pl.multiple_of(core * HD, HD), HD)] = late(core)

    head_copy.wait_recv()
    out_ref[:, pl.ds(pl.multiple_of((1 - core) * HD, HD), HD)] = head_in[...]

    head_copy.wait_send()

    for k in range(4):
        feats_cross(k).wait_send()
        if k > 0:
            feats_copy(k).wait_send()
    for side in (0, 1):

        @pl.when(jnp.logical_not(jnp.logical_and(stays, x == side)))
        def _():
            for half in (0, 1):
                entry_copy(side, half).wait_send()

    def drain(i, carry):
        c = nth(i)
        core_copy(c).wait_send()

        @pl.when(level <= 1)
        def _():
            for half in (0, 1):
                line_copy(c, 1 - level, half).wait_send()

        @pl.when(jnp.logical_and(level <= 1, carried(i)))
        def _():
            for half in (0, 1):
                line_copy(c, 3, half).wait_send()
                line_copy(c, 2, half).wait_send()

        @pl.when(jnp.logical_and(level >= 2, carried(i)))
        def _():
            for piece in range(4):
                cross_copy(c * 4 + piece).wait_send()

        return carry

    lax.fori_loop(0, 4, drain, 0)

    @pl.when(y == 0)
    def _():
        for r in range(4):
            y_copy(r, 2 if r < 2 else 3).wait_send()

    @pl.when(y == 1)
    def _():
        for r in range(2):
            y_copy(r, 3).wait_send()


def fused(
    text_embed, frame_feats, frame_count, proj_weight, norm_gain, q_weight, k_weight, v_weight
):
    cosine, sine = rope_tables(512)
    vmem = pl.BlockSpec(memory_space=pltpu.VMEM)
    hbm = pl.BlockSpec(memory_space=pltpu.MemorySpace.HBM)
    dma = pltpu.SemaphoreType.DMA
    return pl.pallas_call(
        fused_kernel,
        out_shape=jax.ShapeDtypeStruct((128, 256), BF16),
        in_specs=[hbm, hbm, pl.BlockSpec(memory_space=pltpu.SMEM)] + [hbm] * 7,
        out_specs=vmem,
        scratch_shapes=[
            pltpu.VMEM((1024, 512), BF16),
            pltpu.VMEM((1024, 768), BF16),
            pltpu.VMEM((512, HD), F32),
            pltpu.VMEM((512, HD), F32),
            pltpu.VMEM((1024,), BF16),
            pltpu.VMEM((1, 1024), F32),
            pltpu.VMEM((128, 512), BF16),
            pltpu.VMEM((8, 128, 128), BF16),
            pltpu.VMEM((128, 512), F32),
            pltpu.VMEM((2, 128, 256), BF16),
            pltpu.VMEM((16, 128, 256), BF16),
            pltpu.VMEM((4, 128, 384), F32),
            pltpu.VMEM((4, 8, 128), F32),
            pltpu.VMEM((4, 144, 384), BF16),
            pltpu.VMEM((4, 144, 384), BF16),
            pltpu.VMEM((4, 144, 384), BF16),
            pltpu.VMEM((4, 144, 384), BF16),
            pltpu.VMEM((256, HD), BF16),
            pltpu.VMEM((512, HD), BF16),
            pltpu.VMEM((512, HD), BF16),
            pltpu.VMEM((2, 128, HD), F32),
            pltpu.VMEM((2, 128, HD), F32),
            pltpu.VMEM((2, 128, HD), F32),
            pltpu.VMEM((128, HD), BF16),
            pltpu.VMEM((128, HD), BF16),
            dma((12,)),
            dma((8,)),
            dma((8,)),
            dma((4,)),
            dma((32,)),
            dma((16,)),
            dma((16,)),
            dma((4,)),
            dma((4,)),
            dma((4,)),
            dma((4,)),
            dma,
            dma,
        ],
        compiler_params=pltpu.CompilerParams(
            collective_id=0, has_side_effects=True, vmem_limit_bytes=63 * 1024 * 1024
        ),
    )(
        text_embed,
        frame_feats,
        frame_count,
        norm_gain,
        proj_weight,
        q_weight,
        k_weight,
        v_weight,
        jnp.asarray(cosine),
        jnp.asarray(sine),
    )


def solution(mesh):
    small = (mesh.shape["ctx"], mesh.shape["section"], mesh.shape["tp"]) == (4, 2, 4)
    body = fused if small else local
    in_specs = (
        P("ctx", ("section", "tp")),
        P("ctx", ("section", "tp")),
        P("ctx"),
        P(None, ("section", "tp")),
        P(),
        P("ctx", ("section", "tp")),
        P("ctx", ("section", "tp")),
        P("ctx", ("section", "tp")),
    )
    out_specs = P("ctx", ("section", "tp"))
    return jax.shard_map(body, mesh=mesh, in_specs=in_specs, out_specs=out_specs, check_vma=False)
```

```python
import math

import jax
import jax.numpy as jnp
import numpy as np
from jax import lax
from jax.experimental import pallas as pl
from jax.experimental.pallas import tpu as pltpu
from jax.sharding import PartitionSpec as P

HD = 128


ROPE_BASE = 1000000.0
NORM_EPS = 1e-05
MASKED = -1e30


def rotate(values, positions):
    half = values.shape[-1] // 2
    ladder = jnp.arange(half, dtype=jnp.float32) * 2.0 / values.shape[-1]
    freq = ROPE_BASE ** (-ladder)
    angle = positions.astype(jnp.float32)[:, None] * freq[None, :]
    cosine = jnp.cos(angle)[:, None, :]
    sine = jnp.sin(angle)[:, None, :]
    first = values[..., :half]
    second = values[..., half:]
    return jnp.concatenate(
        [first * cosine - second * sine, second * cosine + first * sine], axis=-1
    )


def attend_block(state, key_rows, value_rows, queries, query_pos, scale):
    best, total, accum = state
    rows = key_rows.shape[0]
    heads = queries.shape[1]
    width = queries.shape[2]
    keys_three = key_rows.reshape(rows, heads, width)
    values_three = value_rows.reshape(rows, heads, width)
    scores = (
        jnp.einsum("qhd,khd->hqk", queries, keys_three, preferred_element_type=jnp.float32) * scale
    )
    key_pos = jnp.arange(rows, dtype=jnp.int32)
    allowed = key_pos[None, None, :] <= query_pos[None, :, None]
    block_best = jnp.max(jnp.where(allowed, scores, MASKED), axis=-1)
    new_best = jnp.maximum(best, block_best)
    weights = jnp.where(allowed, jnp.exp(scores - new_best[..., None]), 0.0)
    total = jnp.sum(weights, axis=-1)
    product = jnp.einsum(
        "hqk,khd->hqd",
        weights.astype(jnp.bfloat16),
        values_three,
        preferred_element_type=jnp.float32,
    )
    accum = product
    return (new_best, total, accum)


def local(
    text_embed, frame_feats, frame_count, proj_weight, norm_gain, q_weight, k_weight, v_weight
):
    tok_rows = text_embed.shape[0]
    vision = jnp.dot(
        lax.all_gather(frame_feats, ("section", "tp"), axis=1, tiled=True),
        proj_weight,
        preferred_element_type=jnp.float32,
    )
    offsets = jnp.arange(tok_rows, dtype=jnp.int32)
    is_frame = offsets < frame_count[0]
    joined = jnp.where(is_frame[:, None], vision, text_embed.astype(jnp.float32)).astype(
        jnp.bfloat16
    )
    whole = lax.all_gather(joined, ("section", "tp"), axis=1, tiled=True)
    wide = whole.astype(jnp.float32)
    mean_square = jnp.mean(wide * wide, axis=-1, keepdims=True)
    normed = (wide * lax.rsqrt(mean_square + NORM_EPS) * norm_gain.astype(jnp.float32)).astype(
        jnp.bfloat16
    )
    head_cols = q_weight.shape[1]

    def add_rows(piece):
        return jnp.dot(normed, piece, preferred_element_type=jnp.float32)

    q_full = add_rows(lax.all_gather(q_weight, "ctx", axis=0, tiled=True))
    k_full = add_rows(lax.all_gather(k_weight, "ctx", axis=0, tiled=True))
    v_full = add_rows(lax.all_gather(v_weight, "ctx", axis=0, tiled=True))
    first_pos = lax.axis_index("ctx") * tok_rows
    query_pos = first_pos + offsets
    heads = head_cols // HD
    queries = rotate(q_full.reshape(tok_rows, heads, HD), query_pos).astype(jnp.bfloat16)
    keys = (
        rotate(k_full.reshape(tok_rows, heads, HD), query_pos)
        .astype(jnp.bfloat16)
        .reshape(tok_rows, head_cols)
    )
    values = v_full.astype(jnp.bfloat16)
    scale = 1.0 / math.sqrt(HD)
    initial = (
        jnp.full((heads, tok_rows), MASKED, jnp.float32),
        jnp.zeros((heads, tok_rows), jnp.float32),
        jnp.zeros((heads, tok_rows, HD), jnp.float32),
    )
    state = attend_block(
        initial,
        lax.all_gather(keys, "ctx", axis=0, tiled=True),
        lax.all_gather(values, "ctx", axis=0, tiled=True),
        queries,
        query_pos,
        scale,
    )
    best, total, accum = state
    result = accum / total[..., None]
    return result.transpose(1, 0, 2).reshape(tok_rows, head_cols).astype(jnp.bfloat16)


MESH = pl.DeviceIdType.MESH
F32 = jnp.float32
BF16 = jnp.bfloat16


def rope_tables(tokens):
    half = HD // 2
    freq = ROPE_BASE ** (-(np.arange(half, dtype=np.float64) * 2.0 / HD))
    angle = np.arange(tokens, dtype=np.float64)[:, None] * freq[None, :]
    cosine, sine = np.cos(angle), np.sin(angle)
    return (
        np.concatenate([cosine, cosine], axis=1).astype(np.float32),
        np.concatenate([-sine, sine], axis=1).astype(np.float32),
    )


def fused_kernel(
    text_hbm,
    feats_hbm,
    count_ref,
    gain_hbm,
    proj_hbm,
    q_hbm,
    k_hbm,
    v_hbm,
    cos_hbm,
    sin_hbm,
    out_ref,
    proj,
    weight,
    cos_tab,
    sin_tab,
    gain_raw,
    gain_ref,
    text_ref,
    feats,
    vision,
    joined,
    blocks,
    own,
    own_row,
    core_out,
    core_in,
    y_out,
    y_in,
    queries,
    keys,
    values,
    head_out,
    head_in,
    load_sem,
    feats_send,
    feats_recv,
    entry_send,
    line_send,
    cross_send,
    block_recv,
    core_send,
    core_recv,
    y_send,
    y_recv,
    head_send,
    head_recv,
):
    ctx = lax.axis_index("ctx")
    x = lax.axis_index("section")
    z = lax.axis_index("tp")
    y = ctx // 2
    core = ctx % 2
    g = x * 4 + z

    def at(c, s, t):
        return {"ctx": c, "section": s, "tp": t}

    feats_load = pltpu.make_async_copy(feats_hbm, feats.at[0], load_sem.at[10])
    feats_load.start()
    loads = [
        pltpu.make_async_copy(proj_hbm, proj, load_sem.at[0]),
        pltpu.make_async_copy(text_hbm, text_ref, load_sem.at[11]),
        pltpu.make_async_copy(cos_hbm, cos_tab, load_sem.at[1]),
        pltpu.make_async_copy(sin_hbm, sin_tab, load_sem.at[2]),
        pltpu.make_async_copy(
            gain_hbm.at[pl.ds(pl.multiple_of(ctx * 1024, 1024), 1024)], gain_raw, load_sem.at[9]
        ),
    ]
    for place, head in enumerate((core, 1 - core)):
        for kind, source in enumerate((q_hbm, k_hbm, v_hbm)):
            loads.append(
                pltpu.make_async_copy(
                    source.at[:, pl.ds(pl.multiple_of(head * HD, HD), HD)],
                    weight.at[:, pl.ds((place * 3 + kind) * HD, HD)],
                    load_sem.at[3 + place * 3 + kind],
                )
            )
    for load in loads:
        load.start()

    barrier = pltpu.get_barrier_semaphore()

    def greet_plane(k, carry):
        other = (ctx * 2 + x + k) % 8
        pl.semaphore_signal(
            barrier, inc=1, device_id=at(other // 2, other % 2, z), device_id_type=MESH
        )
        return carry

    lax.fori_loop(1, 8, greet_plane, 0)

    def greet_line(k, carry):
        for side in (0, 1):
            pl.semaphore_signal(
                barrier, inc=1, device_id=at(ctx, side, (z + k) % 4), device_id_type=MESH
            )
        return carry

    lax.fori_loop(1, 4, greet_line, 0)
    feats_load.wait()
    pl.semaphore_wait(barrier, 13)

    def feats_copy(k):
        return pltpu.make_async_remote_copy(
            src_ref=feats.at[0],
            dst_ref=feats.at[k * 2],
            send_sem=feats_send.at[k * 2],
            recv_sem=feats_recv.at[k * 2],
            device_id=at(ctx, x, (z + k) % 4),
            device_id_type=MESH,
        )

    def feats_cross(k):
        return pltpu.make_async_remote_copy(
            src_ref=feats.at[k * 2],
            dst_ref=feats.at[k * 2 + 1],
            send_sem=feats_send.at[k * 2 + 1],
            recv_sem=feats_recv.at[k * 2 + 1],
            device_id=at(ctx, 1 - x, z),
            device_id_type=MESH,
        )

    for k in (1, 3, 2):
        feats_copy(k).start()
    feats_cross(0).start()
    loads[0].wait()
    loads[1].wait()

    def feats_dot(k, side):
        owner = (x * (1 - side) + (1 - x) * side) * 4 + (z + 4 - k) % 4
        rows_of = pl.ds(pl.multiple_of(owner * 128, 128), 128)
        return jnp.dot(feats[k * 2 + side], proj[rows_of, :], preferred_element_type=F32)

    vision[...] = feats_dot(0, 0)
    for k in (1, 3, 2):
        feats_copy(k).wait_recv()
        feats_cross(k).start()
    vision[...] += (feats_dot(1, 0) + feats_dot(3, 0)) + feats_dot(2, 0)
    for k in (0, 1, 3, 2):
        feats_cross(k).wait_recv()
        vision[...] += feats_dot(k, 1)
    rows = lax.broadcasted_iota(jnp.int32, (128, 512), 0)
    mixed = jnp.where(rows < count_ref[0], vision[...], text_ref[...].astype(F32)).astype(BF16)
    for half in (0, 1):
        joined[half] = mixed[:, half * 256 : half * 256 + 256]

    to_core = z // 2
    to_ctx = x * 2 + to_core
    to_part = z * (1 - to_core) + (3 - z) * to_core

    def entry_copy(side, half):
        slot = (ctx * 2 + to_part) * 2 + half
        return pltpu.make_async_remote_copy(
            src_ref=joined.at[half],
            dst_ref=blocks.at[slot],
            send_sem=entry_send.at[side * 2 + half],
            recv_sem=block_recv.at[slot],
            device_id=at(to_ctx, side, z),
            device_id_type=MESH,
        )

    stays = to_ctx == ctx
    for side in (0, 1):
        here = jnp.logical_and(stays, x == side)

        @pl.when(here)
        def _():
            for half in (0, 1):
                blocks[(ctx * 2 + to_part) * 2 + half] = joined[half]

        @pl.when(jnp.logical_not(here))
        def _():
            for half in (0, 1):
                entry_copy(side, half).start()

    level = z * (1 - core) + (3 - z) * core

    parity = (x + y) % 2

    def nth(i):
        return (i + 2 * (1 - y)) % 4

    def carried(i):
        return i % 2 == parity

    def block_arrival(slot):
        pltpu.make_async_copy(blocks.at[slot], blocks.at[slot], block_recv.at[slot]).wait()

    def line_copy(c, to_level, half):
        slot = (c * 2 + level) * 2 + half
        return pltpu.make_async_remote_copy(
            src_ref=blocks.at[slot],
            dst_ref=blocks.at[slot],
            send_sem=line_send.at[(c * 4 + to_level) * 2 + half],
            recv_sem=block_recv.at[slot],
            device_id=at(ctx, x, to_level * (1 - core) + (3 - to_level) * core),
            device_id_type=MESH,
        )

    def cross_copy(slot):
        return pltpu.make_async_remote_copy(
            src_ref=blocks.at[slot],
            dst_ref=blocks.at[slot],
            send_sem=cross_send.at[slot],
            recv_sem=block_recv.at[slot],
            device_id=at(ctx, 1 - x, z),
            device_id_type=MESH,
        )

    @pl.when(level <= 1)
    def _():
        def entered(c, half):
            local_block = jnp.logical_and(c == ctx, x == y)

            @pl.when(jnp.logical_not(local_block))
            def _():
                block_arrival((c * 2 + level) * 2 + half)

        def pass_on(i, carry):
            c = nth(i * 2 + parity)
            for half in (0, 1):
                entered(c, half)
                line_copy(c, 3, half).start()
                line_copy(c, 2, half).start()
            return carry

        lax.fori_loop(0, 2, pass_on, 0)

        def pass_back(i, carry):
            c = nth(i)
            for half in (0, 1):

                @pl.when(jnp.logical_not(carried(i)))
                def _():
                    entered(c, half)

                line_copy(c, 1 - level, half).start()
            return carry

        lax.fori_loop(0, 4, pass_back, 0)

    for load in loads[2:]:
        load.wait()
    gain_ref[...] = gain_raw[...].astype(F32).reshape(1, 1024)

    def product(slot, part):
        offset = (part + core) % 2 * 512
        block = jnp.concatenate([blocks[slot * 2], blocks[slot * 2 + 1]], axis=1).astype(F32)
        gain = gain_ref[:, pl.ds(pl.multiple_of(offset, 512), 512)]
        scaled = (block * gain).astype(BF16)
        square = block * block
        lanes = (square[:, :128] + square[:, 128:256]) + (square[:, 256:384] + square[:, 384:])
        rows_of = pl.ds(pl.multiple_of(offset, 512), 512)
        return jnp.dot(scaled, weight[rows_of, :], preferred_element_type=F32), lanes

    def core_copy(r):
        return pltpu.make_async_remote_copy(
            src_ref=core_out.at[r],
            dst_ref=core_in.at[r],
            send_sem=core_send.at[r],
            recv_sem=core_recv.at[r],
            device_id=at(y * 2 + 1 - core, x, z),
            device_id_type=MESH,
        )

    def y_copy(r, kinds):
        columns = pl.ds((3 - kinds) * HD, kinds * HD)
        return pltpu.make_async_remote_copy(
            src_ref=y_out.at[r, :, columns],
            dst_ref=y_in.at[r, :, columns],
            send_sem=y_send.at[r],
            recv_sem=y_recv.at[r],
            device_id=at((1 - y) * 2 + core, x, z),
            device_id_type=MESH,
        )

    def write_row(ref, r, row):
        high = row.astype(BF16)
        low = (row - high.astype(F32)).astype(BF16)
        ref[r, 128:144, 0:128] = jnp.zeros((16, 128), BF16)
        ref[r, 128:144, 128:256] = jnp.broadcast_to(high, (16, 128))
        ref[r, 128:144, 256:384] = jnp.broadcast_to(low, (16, 128))

    def read_row(ref, r):
        tail = ref[r, 128:144, 128:384].astype(F32)
        return tail[0:1, 0:128] + tail[0:1, 128:256]

    def core_sum(r):
        core_copy(r).wait_recv()
        total = own[r] + core_in[r, 0:128, :].astype(F32)
        row = own_row[r, 0:1, :] + read_row(core_in, r)
        own[r] = total
        own_row[r] = jnp.broadcast_to(row, (8, 128))
        y_out[r, 0:128, :] = total.astype(BF16)
        write_row(y_out, r, row)

        @pl.when(jnp.logical_and(y == 0, r < 2))
        def _():
            y_copy(r, 2).start()

        @pl.when(jnp.logical_or(jnp.logical_and(y == 0, r >= 2), jnp.logical_and(y == 1, r < 2)))
        def _():
            y_copy(r, 3).start()

    def row_block(i, carry):
        c = nth(i)

        @pl.when(i >= 1)
        def _():
            core_sum(nth(i + 3))

        @pl.when(jnp.logical_and(level >= 2, i % 2 == 0))
        def _():
            for piece in (2, 3, 0, 1):
                slot = nth(i + parity) * 4 + piece
                block_arrival(slot)
                cross_copy(slot).start()

        for part in (1, 0):
            by_line = jnp.logical_and(level >= 2, carried(i))

            @pl.when(jnp.logical_not(jnp.logical_or(level == part, by_line)))
            def _():
                for half in (0, 1):
                    block_arrival((c * 2 + part) * 2 + half)

        first, first_lanes = product(c * 2 + 1, 1)
        second, second_lanes = product(c * 2, 0)
        result = first + second
        own[c] = result[:, :384]
        core_out[c, 0:128, :] = result[:, 384:].astype(BF16)
        row = jnp.sum((first_lanes + second_lanes).T, axis=0, keepdims=True)
        own_row[c] = jnp.broadcast_to(row, (8, 128))
        write_row(core_out, c, row)
        core_copy(c).start()
        return carry

    lax.fori_loop(0, 4, row_block, 0)
    core_sum(nth(3))

    def turn(vector, r):
        rows_of = pl.ds(pl.multiple_of(r * 128, 128), 128)
        return vector * cos_tab[rows_of, :] + pltpu.roll(vector, HD // 2, 1) * sin_tab[rows_of, :]

    def finish(r):
        row = own_row[r, 0:1, :] + read_row(y_in, r)
        factor = lax.rsqrt(row * (1.0 / 4096.0) + NORM_EPS)
        factor = jnp.broadcast_to(factor, (128, 128)).T

        def whole(kind):
            columns = pl.ds(kind * HD, HD)
            return (own[r, :, columns] + y_in[r, 0:128, columns].astype(F32)) * factor

        rows_of = pl.ds(pl.multiple_of(r * 128, 128), 128)

        @pl.when(r // 2 == y)
        def _():
            query_rows = pl.ds(pl.multiple_of(r % 2 * 128, 128), 128)
            queries[query_rows, :] = turn(whole(0), r).astype(BF16)

        keys[rows_of, :] = turn(whole(1), r).astype(BF16)
        values[rows_of, :] = whole(2).astype(BF16)

    def attend(r, count):
        query = queries[pl.ds(pl.multiple_of(r % 2 * 128, 128), 128), :]
        scores = lax.dot_general(
            query, keys[0:count, :], (((1,), (1,)), ((), ())), preferred_element_type=F32
        ) * (1.0 / math.sqrt(HD))
        place = r * 128 + lax.broadcasted_iota(jnp.int32, (128, count), 0)
        allowed = lax.broadcasted_iota(jnp.int32, (128, count), 1) <= place
        best = jnp.max(jnp.where(allowed, scores, MASKED), axis=1, keepdims=True)
        weights = jnp.where(allowed, jnp.exp(scores - best), 0.0)
        total = jnp.sum(weights, axis=1, keepdims=True)
        out = jnp.dot(weights.astype(BF16), values[0:count, :], preferred_element_type=F32)
        return (out / total).astype(BF16)

    head_copy = pltpu.make_async_remote_copy(
        src_ref=head_out,
        dst_ref=head_in,
        send_sem=head_send,
        recv_sem=head_recv,
        device_id=at(y * 2 + 1 - core, x, z),
        device_id_type=MESH,
    )

    def both_heads(count):
        head_out[...] = attend(y * 2 + 1 - core, count)
        head_copy.start()
        out_ref[:, pl.ds(pl.multiple_of(core * HD, HD), HD)] = attend(ctx, count).astype(F32)

    @pl.when(y == 0)
    def _():
        for r in (0, 1):
            y_copy(r, 3).wait_recv()
            finish(r)
        both_heads(256)

    @pl.when(y == 1)
    def _():
        def arrived(i, carry):
            r = (i + 2) % 4

            @pl.when(r < 2)
            def _():
                y_copy(r, 2).wait_recv()

            @pl.when(r >= 2)
            def _():
                y_copy(r, 3).wait_recv()

            finish(r)
            return carry

        lax.fori_loop(0, 4, arrived, 0)
        both_heads(512)

    head_copy.wait_recv()
    out_ref[:, pl.ds(pl.multiple_of((1 - core) * HD, HD), HD)] = head_in[...].astype(F32)

    head_copy.wait_send()

    for k in range(4):
        feats_cross(k).wait_send()
        if k > 0:
            feats_copy(k).wait_send()
    for side in (0, 1):

        @pl.when(jnp.logical_not(jnp.logical_and(stays, x == side)))
        def _():
            for half in (0, 1):
                entry_copy(side, half).wait_send()

    def drain(i, carry):
        c = nth(i)
        core_copy(c).wait_send()

        @pl.when(level <= 1)
        def _():
            for half in (0, 1):
                line_copy(c, 1 - level, half).wait_send()

        @pl.when(jnp.logical_and(level <= 1, carried(i)))
        def _():
            for half in (0, 1):
                line_copy(c, 3, half).wait_send()
                line_copy(c, 2, half).wait_send()

        @pl.when(jnp.logical_and(level >= 2, carried(i)))
        def _():
            for piece in range(4):
                cross_copy(c * 4 + piece).wait_send()

        return carry

    lax.fori_loop(0, 4, drain, 0)

    @pl.when(y == 0)
    def _():
        for r in range(4):
            y_copy(r, 2 if r < 2 else 3).wait_send()

    @pl.when(y == 1)
    def _():
        for r in range(2):
            y_copy(r, 3).wait_send()


def fused(
    text_embed, frame_feats, frame_count, proj_weight, norm_gain, q_weight, k_weight, v_weight
):
    cosine, sine = rope_tables(512)
    vmem = pl.BlockSpec(memory_space=pltpu.VMEM)
    hbm = pl.BlockSpec(memory_space=pltpu.MemorySpace.HBM)
    dma = pltpu.SemaphoreType.DMA
    return pl.pallas_call(
        fused_kernel,
        out_shape=jax.ShapeDtypeStruct((128, 256), F32),
        in_specs=[hbm, hbm, pl.BlockSpec(memory_space=pltpu.SMEM)] + [hbm] * 7,
        out_specs=vmem,
        scratch_shapes=[
            pltpu.VMEM((1024, 512), BF16),
            pltpu.VMEM((1024, 768), BF16),
            pltpu.VMEM((512, HD), F32),
            pltpu.VMEM((512, HD), F32),
            pltpu.VMEM((1024,), BF16),
            pltpu.VMEM((1, 1024), F32),
            pltpu.VMEM((128, 512), BF16),
            pltpu.VMEM((8, 128, 128), BF16),
            pltpu.VMEM((128, 512), F32),
            pltpu.VMEM((2, 128, 256), BF16),
            pltpu.VMEM((16, 128, 256), BF16),
            pltpu.VMEM((4, 128, 384), F32),
            pltpu.VMEM((4, 8, 128), F32),
            pltpu.VMEM((4, 144, 384), BF16),
            pltpu.VMEM((4, 144, 384), BF16),
            pltpu.VMEM((4, 144, 384), BF16),
            pltpu.VMEM((4, 144, 384), BF16),
            pltpu.VMEM((256, HD), BF16),
            pltpu.VMEM((512, HD), BF16),
            pltpu.VMEM((512, HD), BF16),
            pltpu.VMEM((128, HD), BF16),
            pltpu.VMEM((128, HD), BF16),
            dma((12,)),
            dma((8,)),
            dma((8,)),
            dma((4,)),
            dma((32,)),
            dma((16,)),
            dma((16,)),
            dma((4,)),
            dma((4,)),
            dma((4,)),
            dma((4,)),
            dma,
            dma,
        ],
        compiler_params=pltpu.CompilerParams(
            collective_id=0, has_side_effects=True, vmem_limit_bytes=63 * 1024 * 1024
        ),
    )(
        text_embed,
        frame_feats,
        frame_count,
        norm_gain,
        proj_weight,
        q_weight,
        k_weight,
        v_weight,
        jnp.asarray(cosine),
        jnp.asarray(sine),
    ).astype(BF16)


def solution(mesh):
    small = (mesh.shape["ctx"], mesh.shape["section"], mesh.shape["tp"]) == (4, 2, 4)
    body = fused if small else local
    in_specs = (
        P("ctx", ("section", "tp")),
        P("ctx", ("section", "tp")),
        P("ctx"),
        P(None, ("section", "tp")),
        P(),
        P("ctx", ("section", "tp")),
        P("ctx", ("section", "tp")),
        P("ctx", ("section", "tp")),
    )
    out_specs = P("ctx", ("section", "tp"))
    return jax.shard_map(body, mesh=mesh, in_specs=in_specs, out_specs=out_specs, check_vma=False)
```

```python
import math

import jax
import jax.numpy as jnp
import numpy as np
from jax import lax
from jax.experimental import pallas as pl
from jax.experimental.pallas import tpu as pltpu
from jax.sharding import PartitionSpec as P

HD = 128


ROPE_BASE = 1000000.0
NORM_EPS = 1e-05
MASKED = -1e30


def rotate(values, positions):
    half = values.shape[-1] // 2
    ladder = jnp.arange(half, dtype=jnp.float32) * 2.0 / values.shape[-1]
    freq = ROPE_BASE ** (-ladder)
    angle = positions.astype(jnp.float32)[:, None] * freq[None, :]
    cosine = jnp.cos(angle)[:, None, :]
    sine = jnp.sin(angle)[:, None, :]
    first = values[..., :half]
    second = values[..., half:]
    return jnp.concatenate(
        [first * cosine - second * sine, second * cosine + first * sine], axis=-1
    )


def attend_block(state, key_rows, value_rows, queries, query_pos, scale):
    best, total, accum = state
    rows = key_rows.shape[0]
    heads = queries.shape[1]
    width = queries.shape[2]
    keys_three = key_rows.reshape(rows, heads, width)
    values_three = value_rows.reshape(rows, heads, width)
    scores = (
        jnp.einsum("qhd,khd->hqk", queries, keys_three, preferred_element_type=jnp.float32) * scale
    )
    key_pos = jnp.arange(rows, dtype=jnp.int32)
    allowed = key_pos[None, None, :] <= query_pos[None, :, None]
    block_best = jnp.max(jnp.where(allowed, scores, MASKED), axis=-1)
    new_best = jnp.maximum(best, block_best)
    weights = jnp.where(allowed, jnp.exp(scores - new_best[..., None]), 0.0)
    total = jnp.sum(weights, axis=-1)
    product = jnp.einsum(
        "hqk,khd->hqd",
        weights.astype(jnp.bfloat16),
        values_three,
        preferred_element_type=jnp.float32,
    )
    accum = product
    return (new_best, total, accum)


def local(
    text_embed, frame_feats, frame_count, proj_weight, norm_gain, q_weight, k_weight, v_weight
):
    tok_rows = text_embed.shape[0]
    vision = jnp.dot(
        lax.all_gather(frame_feats, ("section", "tp"), axis=1, tiled=True),
        proj_weight,
        preferred_element_type=jnp.float32,
    )
    offsets = jnp.arange(tok_rows, dtype=jnp.int32)
    is_frame = offsets < frame_count[0]
    joined = jnp.where(is_frame[:, None], vision, text_embed.astype(jnp.float32)).astype(
        jnp.bfloat16
    )
    whole = lax.all_gather(joined, ("section", "tp"), axis=1, tiled=True)
    wide = whole.astype(jnp.float32)
    mean_square = jnp.mean(wide * wide, axis=-1, keepdims=True)
    normed = (wide * lax.rsqrt(mean_square + NORM_EPS) * norm_gain.astype(jnp.float32)).astype(
        jnp.bfloat16
    )
    head_cols = q_weight.shape[1]

    def add_rows(piece):
        return jnp.dot(normed, piece, preferred_element_type=jnp.float32)

    q_full = add_rows(lax.all_gather(q_weight, "ctx", axis=0, tiled=True))
    k_full = add_rows(lax.all_gather(k_weight, "ctx", axis=0, tiled=True))
    v_full = add_rows(lax.all_gather(v_weight, "ctx", axis=0, tiled=True))
    first_pos = lax.axis_index("ctx") * tok_rows
    query_pos = first_pos + offsets
    heads = head_cols // HD
    queries = rotate(q_full.reshape(tok_rows, heads, HD), query_pos).astype(jnp.bfloat16)
    keys = (
        rotate(k_full.reshape(tok_rows, heads, HD), query_pos)
        .astype(jnp.bfloat16)
        .reshape(tok_rows, head_cols)
    )
    values = v_full.astype(jnp.bfloat16)
    scale = 1.0 / math.sqrt(HD)
    initial = (
        jnp.full((heads, tok_rows), MASKED, jnp.float32),
        jnp.zeros((heads, tok_rows), jnp.float32),
        jnp.zeros((heads, tok_rows, HD), jnp.float32),
    )
    state = attend_block(
        initial,
        lax.all_gather(keys, "ctx", axis=0, tiled=True),
        lax.all_gather(values, "ctx", axis=0, tiled=True),
        queries,
        query_pos,
        scale,
    )
    best, total, accum = state
    result = accum / total[..., None]
    return result.transpose(1, 0, 2).reshape(tok_rows, head_cols).astype(jnp.bfloat16)


MESH = pl.DeviceIdType.MESH
F32 = jnp.float32
BF16 = jnp.bfloat16


def rope_tables(tokens):
    half = HD // 2
    freq = ROPE_BASE ** (-(np.arange(half, dtype=np.float64) * 2.0 / HD))
    angle = np.arange(tokens, dtype=np.float64)[:, None] * freq[None, :]
    cosine, sine = np.cos(angle), np.sin(angle)
    return (
        np.concatenate([cosine, cosine], axis=1).astype(np.float32),
        np.concatenate([-sine, sine], axis=1).astype(np.float32),
    )


def fused_kernel(
    text_hbm,
    feats_hbm,
    count_ref,
    gain_hbm,
    proj_hbm,
    q_hbm,
    k_hbm,
    v_hbm,
    cos_hbm,
    sin_hbm,
    out_ref,
    proj,
    weight,
    cos_tab,
    sin_tab,
    gain_raw,
    gain_ref,
    text_ref,
    feats,
    vision,
    joined,
    blocks,
    own,
    own_row,
    core_out,
    core_in,
    y_out,
    y_in,
    queries,
    keys,
    values,
    head_out,
    head_in,
    load_sem,
    feats_send,
    feats_recv,
    entry_send,
    line_send,
    cross_send,
    block_recv,
    core_send,
    core_recv,
    y_send,
    y_recv,
    head_send,
    head_recv,
):
    ctx = lax.axis_index("ctx")
    x = lax.axis_index("section")
    z = lax.axis_index("tp")
    y = ctx // 2
    core = ctx % 2
    g = x * 4 + z

    def at(c, s, t):
        return {"ctx": c, "section": s, "tp": t}

    feats_load = pltpu.make_async_copy(feats_hbm, feats.at[0], load_sem.at[10])
    feats_load.start()
    loads = [
        pltpu.make_async_copy(proj_hbm, proj, load_sem.at[0]),
        pltpu.make_async_copy(text_hbm, text_ref, load_sem.at[11]),
        pltpu.make_async_copy(cos_hbm, cos_tab, load_sem.at[1]),
        pltpu.make_async_copy(sin_hbm, sin_tab, load_sem.at[2]),
        pltpu.make_async_copy(
            gain_hbm.at[pl.ds(pl.multiple_of(ctx * 1024, 1024), 1024)], gain_raw, load_sem.at[9]
        ),
    ]
    for place, head in enumerate((core, 1 - core)):
        for kind, source in enumerate((q_hbm, k_hbm, v_hbm)):
            loads.append(
                pltpu.make_async_copy(
                    source.at[:, pl.ds(pl.multiple_of(head * HD, HD), HD)],
                    weight.at[:, pl.ds((place * 3 + kind) * HD, HD)],
                    load_sem.at[3 + place * 3 + kind],
                )
            )
    for load in loads:
        load.start()

    barrier = pltpu.get_barrier_semaphore()

    def greet_plane(k, carry):
        other = (ctx * 2 + x + k) % 8
        pl.semaphore_signal(
            barrier, inc=1, device_id=at(other // 2, other % 2, z), device_id_type=MESH
        )
        return carry

    lax.fori_loop(1, 8, greet_plane, 0)

    def greet_line(k, carry):
        for side in (0, 1):
            pl.semaphore_signal(
                barrier, inc=1, device_id=at(ctx, side, (z + k) % 4), device_id_type=MESH
            )
        return carry

    lax.fori_loop(1, 4, greet_line, 0)
    feats_load.wait()
    pl.semaphore_wait(barrier, 13)

    def feats_copy(k):
        return pltpu.make_async_remote_copy(
            src_ref=feats.at[0],
            dst_ref=feats.at[k * 2],
            send_sem=feats_send.at[k * 2],
            recv_sem=feats_recv.at[k * 2],
            device_id=at(ctx, x, (z + k) % 4),
            device_id_type=MESH,
        )

    def feats_cross(k):
        return pltpu.make_async_remote_copy(
            src_ref=feats.at[k * 2],
            dst_ref=feats.at[k * 2 + 1],
            send_sem=feats_send.at[k * 2 + 1],
            recv_sem=feats_recv.at[k * 2 + 1],
            device_id=at(ctx, 1 - x, z),
            device_id_type=MESH,
        )

    for k in (1, 3, 2):
        feats_copy(k).start()
    feats_cross(0).start()
    loads[0].wait()
    loads[1].wait()

    def feats_dot(k, side):
        owner = (x * (1 - side) + (1 - x) * side) * 4 + (z + 4 - k) % 4
        rows_of = pl.ds(pl.multiple_of(owner * 128, 128), 128)
        return jnp.dot(feats[k * 2 + side], proj[rows_of, :], preferred_element_type=F32)

    vision[...] = feats_dot(0, 0)
    for k in (1, 3, 2):
        feats_copy(k).wait_recv()
        feats_cross(k).start()
    vision[...] += (feats_dot(1, 0) + feats_dot(3, 0)) + feats_dot(2, 0)
    for k in (0, 1, 3, 2):
        feats_cross(k).wait_recv()
        vision[...] += feats_dot(k, 1)
    rows = lax.broadcasted_iota(jnp.int32, (128, 512), 0)
    mixed = jnp.where(rows < count_ref[0], vision[...], text_ref[...].astype(F32)).astype(BF16)
    for half in (0, 1):
        joined[half] = mixed[:, half * 256 : half * 256 + 256]

    to_core = z // 2
    to_ctx = x * 2 + to_core
    to_part = z * (1 - to_core) + (3 - z) * to_core

    def entry_copy(side, half):
        slot = (ctx * 2 + to_part) * 2 + half
        return pltpu.make_async_remote_copy(
            src_ref=joined.at[half],
            dst_ref=blocks.at[slot],
            send_sem=entry_send.at[side * 2 + half],
            recv_sem=block_recv.at[slot],
            device_id=at(to_ctx, side, z),
            device_id_type=MESH,
        )

    stays = to_ctx == ctx
    for side in (0, 1):
        here = jnp.logical_and(stays, x == side)

        @pl.when(here)
        def _():
            for half in (0, 1):
                blocks[(ctx * 2 + to_part) * 2 + half] = joined[half]

        @pl.when(jnp.logical_not(here))
        def _():
            for half in (0, 1):
                entry_copy(side, half).start()

    level = z * (1 - core) + (3 - z) * core

    parity = (x + y) % 2

    def nth(i):
        return (i + 2 * (1 - y)) % 4

    def carried(i):
        return i % 2 == parity

    def block_arrival(slot):
        pltpu.make_async_copy(blocks.at[slot], blocks.at[slot], block_recv.at[slot]).wait()

    def line_copy(c, to_level, half):
        slot = (c * 2 + level) * 2 + half
        return pltpu.make_async_remote_copy(
            src_ref=blocks.at[slot],
            dst_ref=blocks.at[slot],
            send_sem=line_send.at[(c * 4 + to_level) * 2 + half],
            recv_sem=block_recv.at[slot],
            device_id=at(ctx, x, to_level * (1 - core) + (3 - to_level) * core),
            device_id_type=MESH,
        )

    def cross_copy(slot):
        return pltpu.make_async_remote_copy(
            src_ref=blocks.at[slot],
            dst_ref=blocks.at[slot],
            send_sem=cross_send.at[slot],
            recv_sem=block_recv.at[slot],
            device_id=at(ctx, 1 - x, z),
            device_id_type=MESH,
        )

    @pl.when(level <= 1)
    def _():
        def pass_on(i, carry):
            c = nth(i)
            local_block = jnp.logical_and(c == ctx, x == y)
            for half in (0, 1):

                @pl.when(jnp.logical_not(local_block))
                def _():
                    block_arrival((c * 2 + level) * 2 + half)

                line_copy(c, 1 - level, half).start()

                @pl.when(carried(i))
                def _():
                    line_copy(c, 2, half).start()
                    line_copy(c, 3, half).start()

            return carry

        lax.fori_loop(0, 4, pass_on, 0)

    for load in loads[2:]:
        load.wait()
    gain_ref[...] = gain_raw[...].astype(F32).reshape(1, 1024)

    def product(slot, part):
        offset = (part + core) % 2 * 512
        block = jnp.concatenate([blocks[slot * 2], blocks[slot * 2 + 1]], axis=1).astype(F32)
        gain = gain_ref[:, pl.ds(pl.multiple_of(offset, 512), 512)]
        scaled = (block * gain).astype(BF16)
        square = block * block
        lanes = (square[:, :128] + square[:, 128:256]) + (square[:, 256:384] + square[:, 384:])
        rows_of = pl.ds(pl.multiple_of(offset, 512), 512)
        return jnp.dot(scaled, weight[rows_of, :], preferred_element_type=F32), lanes

    def core_copy(r):
        return pltpu.make_async_remote_copy(
            src_ref=core_out.at[r],
            dst_ref=core_in.at[r],
            send_sem=core_send.at[r],
            recv_sem=core_recv.at[r],
            device_id=at(y * 2 + 1 - core, x, z),
            device_id_type=MESH,
        )

    def y_copy(r, kinds):
        columns = pl.ds((3 - kinds) * HD, kinds * HD)
        return pltpu.make_async_remote_copy(
            src_ref=y_out.at[r, :, columns],
            dst_ref=y_in.at[r, :, columns],
            send_sem=y_send.at[r],
            recv_sem=y_recv.at[r],
            device_id=at((1 - y) * 2 + core, x, z),
            device_id_type=MESH,
        )

    def write_row(ref, r, row):
        high = row.astype(BF16)
        low = (row - high.astype(F32)).astype(BF16)
        ref[r, 128:144, 0:128] = jnp.zeros((16, 128), BF16)
        ref[r, 128:144, 128:256] = jnp.broadcast_to(high, (16, 128))
        ref[r, 128:144, 256:384] = jnp.broadcast_to(low, (16, 128))

    def read_row(ref, r):
        tail = ref[r, 128:144, 128:384].astype(F32)
        return tail[0:1, 0:128] + tail[0:1, 128:256]

    def core_sum(r):
        core_copy(r).wait_recv()
        total = own[r] + core_in[r, 0:128, :].astype(F32)
        row = own_row[r, 0:1, :] + read_row(core_in, r)
        own[r] = total
        own_row[r] = jnp.broadcast_to(row, (8, 128))
        y_out[r, 0:128, :] = total.astype(BF16)
        write_row(y_out, r, row)

        @pl.when(jnp.logical_and(y == 0, r < 2))
        def _():
            y_copy(r, 2).start()

        @pl.when(jnp.logical_or(jnp.logical_and(y == 0, r >= 2), jnp.logical_and(y == 1, r < 2)))
        def _():
            y_copy(r, 3).start()

    def row_block(i, carry):
        c = nth(i)

        @pl.when(i >= 1)
        def _():
            core_sum(nth(i + 3))

        @pl.when(jnp.logical_and(level >= 2, i % 2 == 0))
        def _():
            for piece in (2, 3, 0, 1):
                slot = nth(i + parity) * 4 + piece
                block_arrival(slot)
                cross_copy(slot).start()

        for part in (1, 0):
            by_line = jnp.logical_and(level >= 2, carried(i))

            @pl.when(jnp.logical_not(jnp.logical_or(level == part, by_line)))
            def _():
                for half in (0, 1):
                    block_arrival((c * 2 + part) * 2 + half)

        first, first_lanes = product(c * 2 + 1, 1)
        second, second_lanes = product(c * 2, 0)
        result = first + second
        own[c] = result[:, :384]
        core_out[c, 0:128, :] = result[:, 384:].astype(BF16)
        row = jnp.sum((first_lanes + second_lanes).T, axis=0, keepdims=True)
        own_row[c] = jnp.broadcast_to(row, (8, 128))
        write_row(core_out, c, row)
        core_copy(c).start()
        return carry

    lax.fori_loop(0, 4, row_block, 0)
    core_sum(nth(3))

    def turn(vector, r):
        rows_of = pl.ds(pl.multiple_of(r * 128, 128), 128)
        return vector * cos_tab[rows_of, :] + pltpu.roll(vector, HD // 2, 1) * sin_tab[rows_of, :]

    def finish(r):
        row = own_row[r, 0:1, :] + read_row(y_in, r)
        factor = lax.rsqrt(row * (1.0 / 4096.0) + NORM_EPS)
        factor = jnp.broadcast_to(factor, (128, 128)).T

        def whole(kind):
            columns = pl.ds(kind * HD, HD)
            return (own[r, :, columns] + y_in[r, 0:128, columns].astype(F32)) * factor

        rows_of = pl.ds(pl.multiple_of(r * 128, 128), 128)

        @pl.when(r // 2 == y)
        def _():
            query_rows = pl.ds(pl.multiple_of(r % 2 * 128, 128), 128)
            queries[query_rows, :] = turn(whole(0), r).astype(BF16)

        keys[rows_of, :] = turn(whole(1), r).astype(BF16)
        values[rows_of, :] = whole(2).astype(BF16)

    def attend(r, count):
        query = queries[pl.ds(pl.multiple_of(r % 2 * 128, 128), 128), :]
        scores = lax.dot_general(
            query, keys[0:count, :], (((1,), (1,)), ((), ())), preferred_element_type=F32
        ) * (1.0 / math.sqrt(HD))
        place = r * 128 + lax.broadcasted_iota(jnp.int32, (128, count), 0)
        allowed = lax.broadcasted_iota(jnp.int32, (128, count), 1) <= place
        best = jnp.max(jnp.where(allowed, scores, MASKED), axis=1, keepdims=True)
        weights = jnp.where(allowed, jnp.exp(scores - best), 0.0)
        total = jnp.sum(weights, axis=1, keepdims=True)
        out = jnp.dot(weights.astype(BF16), values[0:count, :], preferred_element_type=F32)
        return (out / total).astype(BF16)

    head_copy = pltpu.make_async_remote_copy(
        src_ref=head_out,
        dst_ref=head_in,
        send_sem=head_send,
        recv_sem=head_recv,
        device_id=at(y * 2 + 1 - core, x, z),
        device_id_type=MESH,
    )

    def both_heads(count):
        head_out[...] = attend(y * 2 + 1 - core, count)
        head_copy.start()
        out_ref[:, pl.ds(pl.multiple_of(core * HD, HD), HD)] = attend(ctx, count).astype(F32)

    @pl.when(y == 0)
    def _():
        for r in (0, 1):
            y_copy(r, 3).wait_recv()
            finish(r)
        both_heads(256)

    @pl.when(y == 1)
    def _():
        def arrived(i, carry):
            r = (i + 2) % 4

            @pl.when(r < 2)
            def _():
                y_copy(r, 2).wait_recv()

            @pl.when(r >= 2)
            def _():
                y_copy(r, 3).wait_recv()

            finish(r)
            return carry

        lax.fori_loop(0, 4, arrived, 0)
        both_heads(512)

    head_copy.wait_recv()
    out_ref[:, pl.ds(pl.multiple_of((1 - core) * HD, HD), HD)] = head_in[...].astype(F32)

    head_copy.wait_send()

    for k in range(4):
        feats_cross(k).wait_send()
        if k > 0:
            feats_copy(k).wait_send()
    for side in (0, 1):

        @pl.when(jnp.logical_not(jnp.logical_and(stays, x == side)))
        def _():
            for half in (0, 1):
                entry_copy(side, half).wait_send()

    def drain(i, carry):
        c = nth(i)
        core_copy(c).wait_send()

        @pl.when(level <= 1)
        def _():
            for half in (0, 1):
                line_copy(c, 1 - level, half).wait_send()

        @pl.when(jnp.logical_and(level <= 1, carried(i)))
        def _():
            for half in (0, 1):
                line_copy(c, 3, half).wait_send()
                line_copy(c, 2, half).wait_send()

        @pl.when(jnp.logical_and(level >= 2, carried(i)))
        def _():
            for piece in range(4):
                cross_copy(c * 4 + piece).wait_send()

        return carry

    lax.fori_loop(0, 4, drain, 0)

    @pl.when(y == 0)
    def _():
        for r in range(4):
            y_copy(r, 2 if r < 2 else 3).wait_send()

    @pl.when(y == 1)
    def _():
        for r in range(2):
            y_copy(r, 3).wait_send()


def fused(
    text_embed, frame_feats, frame_count, proj_weight, norm_gain, q_weight, k_weight, v_weight
):
    cosine, sine = rope_tables(512)
    vmem = pl.BlockSpec(memory_space=pltpu.VMEM)
    hbm = pl.BlockSpec(memory_space=pltpu.MemorySpace.HBM)
    dma = pltpu.SemaphoreType.DMA
    return pl.pallas_call(
        fused_kernel,
        out_shape=jax.ShapeDtypeStruct((128, 256), F32),
        in_specs=[hbm, hbm, pl.BlockSpec(memory_space=pltpu.SMEM)] + [hbm] * 7,
        out_specs=vmem,
        scratch_shapes=[
            pltpu.VMEM((1024, 512), BF16),
            pltpu.VMEM((1024, 768), BF16),
            pltpu.VMEM((512, HD), F32),
            pltpu.VMEM((512, HD), F32),
            pltpu.VMEM((1024,), BF16),
            pltpu.VMEM((1, 1024), F32),
            pltpu.VMEM((128, 512), BF16),
            pltpu.VMEM((8, 128, 128), BF16),
            pltpu.VMEM((128, 512), F32),
            pltpu.VMEM((2, 128, 256), BF16),
            pltpu.VMEM((16, 128, 256), BF16),
            pltpu.VMEM((4, 128, 384), F32),
            pltpu.VMEM((4, 8, 128), F32),
            pltpu.VMEM((4, 144, 384), BF16),
            pltpu.VMEM((4, 144, 384), BF16),
            pltpu.VMEM((4, 144, 384), BF16),
            pltpu.VMEM((4, 144, 384), BF16),
            pltpu.VMEM((256, HD), BF16),
            pltpu.VMEM((512, HD), BF16),
            pltpu.VMEM((512, HD), BF16),
            pltpu.VMEM((128, HD), BF16),
            pltpu.VMEM((128, HD), BF16),
            dma((12,)),
            dma((8,)),
            dma((8,)),
            dma((4,)),
            dma((32,)),
            dma((16,)),
            dma((16,)),
            dma((4,)),
            dma((4,)),
            dma((4,)),
            dma((4,)),
            dma,
            dma,
        ],
        compiler_params=pltpu.CompilerParams(
            collective_id=0, has_side_effects=True, vmem_limit_bytes=63 * 1024 * 1024
        ),
    )(
        text_embed,
        frame_feats,
        frame_count,
        norm_gain,
        proj_weight,
        q_weight,
        k_weight,
        v_weight,
        jnp.asarray(cosine),
        jnp.asarray(sine),
    ).astype(BF16)


def solution(mesh):
    small = (mesh.shape["ctx"], mesh.shape["section"], mesh.shape["tp"]) == (4, 2, 4)
    body = fused if small else local
    in_specs = (
        P("ctx", ("section", "tp")),
        P("ctx", ("section", "tp")),
        P("ctx"),
        P(None, ("section", "tp")),
        P(),
        P("ctx", ("section", "tp")),
        P("ctx", ("section", "tp")),
        P("ctx", ("section", "tp")),
    )
    out_specs = P("ctx", ("section", "tp"))
    return jax.shard_map(body, mesh=mesh, in_specs=in_specs, out_specs=out_specs, check_vma=False)
```
